32 devices in a mesh: region: 8 (over z, y), sub: 4 (over x, core).
Axes of the slice: x: 2, y: 2, z: 4, core: 2. Of those that a mesh axis runs over, the one named last changes fastest.
Arguments:
- modal_state: float32 [9, 56, 4096], P(None, None, ('region', 'sub')), may hold values from -6 to 6
- deriv_stiff: float32 [3, 56, 56], replicated, may hold values from -0.75 to 0.75
- volume_stiff: float32 [3, 56, 56], replicated, may hold values from -0.5 to 0.5
- local_flux: float32 [4, 56, 56], replicated, may hold values from -0.375 to 0.375
- neighbour_flux: float32 [4, 12, 56, 56], replicated, may hold values from -0.375 to 0.375
- star_matrices: float32 [3, 9, 9, 4096], P(None, None, None, ('region', 'sub')), may hold values from -2 to 2
- plus_flux: float32 [4, 9, 9, 4096], P(None, None, None, ('region', 'sub')), may hold values from -2 to 2
- minus_flux: float32 [4, 9, 9, 4096], P(None, None, None, ('region', 'sub')), may hold values from -2 to 2
- cluster_ids: int32 [4096], P(('region', 'sub')), may hold values from 0 to 2
- face_neighbours: int32 [4, 4096], P(None, ('region', 'sub')), may hold values from 0 to 287
- face_orient: int32 [4, 4096], P(None, ('region', 'sub')), may hold values from 0 to 11
- send_lists: int32 [32, 4, 3, 32], P(('region', 'sub')), may hold values from 0 to 127
- sub_lists: int32 [32, 3, 8], P(('region', 'sub')), may hold values from 0 to 127
Outputs:
- new_state: float32 [9, 56, 4096], P(None, None, ('region', 'sub'))
The draws below stay inside these ranges and needn't reach their ends.
Inputs may be any that keep to these rules, and one draw needn't show every extreme that they name: `face_neighbours`: values below 128 name elements of the same partition, the next 128 name slots received from neighbouring regions, the last 32 slots received from the region's subpartitions. `send_lists`: every slot of every list is used. `sub_lists`: every slot of every list is used.
All inputs are finite; a program needn't handle non-finite values.
Results may differ from the reference program's by a relative error of at most 0.0003.
Values sent between devices are 32-bit elements; how exact they have to be, the bound alone decides.
No kernel may reach another device: no remote copies, remote signals or barrier semaphores. Data moves between devices by JAX's collectives and lax.ppermute only.
A program may use at most 128 MiB of HBM per device.

```python
import jax
import jax.numpy as jnp
from jax import lax

M = 56
NQ = 9
NDER = 6
NCLUS = 3
ORIENT = 12
E_DEV = 128
SLOT = 32
SLOT_SUB = 8
DEVICES_ALL = 32
ELEMS = 4096
N_REGION = 8
N_SUB = 4


def with_ends(drawn, rng, least, high):
    extent = drawn.shape
    index_at = [jax.random.randint(jax.random.fold_in(rng, axis), (), 0, extent[axis]) for axis in range(len(extent))]
    drawn = drawn.at[tuple(index_at)].set(least)
    longest = extent.index(max(extent))
    index_at[longest] = (index_at[longest] + 1) % extent[longest]
    return drawn.at[tuple(index_at)].set(high)


def block_levels(rng, dims, shards, smallest, high):
    def one(dim, shards_of):
        draws = jax.random.uniform(jax.random.fold_in(jax.random.fold_in(rng, 6), dim), (shards_of,), jnp.float32, smallest / len(shards), high / len(shards))
        return jnp.repeat(jnp.exp(draws), dims[dim] // shards_of).reshape((-1,) + (1,) * (len(dims) - dim - 1))

    loudness = one(*shards[0])
    for cut in shards[1:]:
        loudness = loudness * one(*cut)
    return loudness


def noise(rng, dims, scale, bound, shards=(), kind=jnp.bfloat16):
    entries = jax.random.normal(rng, dims, jnp.float32) * scale
    if len(shards) > 0:
        entries = block_levels(rng, dims, shards, -0.22, 0.18) * entries
    return jnp.clip(entries, min=-bound, max=bound).astype(kind)


def setup_inputs(seed: int = 0) -> dict:
    key_list = jax.random.split(jax.random.key(seed), 14)
    return {
        "modal_state": noise(key_list[0], (NQ, M, ELEMS), 1.0, 6.0, ((2, 32),), jnp.float32),
        "deriv_stiff": noise(key_list[1], (3, M, M), M ** -0.5, 0.75, (), jnp.float32),
        "volume_stiff": noise(key_list[2], (3, M, M), (3 * M) ** -0.5, 0.5, (), jnp.float32),
        "local_flux": noise(key_list[3], (4, M, M), (4 * M) ** -0.5, 0.375, (), jnp.float32),
        "neighbour_flux": noise(key_list[4], (4, ORIENT, M, M), (4 * M) ** -0.5, 0.375, (), jnp.float32),
        "star_matrices": noise(key_list[5], (3, NQ, NQ, ELEMS), NQ ** -0.5, 2.0, ((3, 32),), jnp.float32),
        "plus_flux": noise(key_list[6], (4, NQ, NQ, ELEMS), NQ ** -0.5, 2.0, ((3, 32),), jnp.float32),
        "minus_flux": noise(key_list[7], (4, NQ, NQ, ELEMS), NQ ** -0.5, 2.0, ((3, 32),), jnp.float32),
        "cluster_ids": with_ends(jax.random.randint(key_list[8], (ELEMS,), 0, NCLUS), jax.random.fold_in(key_list[8], 1), 0, NCLUS - 1).astype(jnp.int32),
        "face_neighbours": with_ends(jax.random.randint(key_list[9], (4, ELEMS), 0, E_DEV + 4 * SLOT + N_SUB * SLOT_SUB), jax.random.fold_in(key_list[9], 1), 0, (E_DEV + 4 * SLOT + N_SUB * SLOT_SUB) - 1).astype(jnp.int32),
        "face_orient": with_ends(jax.random.randint(key_list[10], (4, ELEMS), 0, ORIENT), jax.random.fold_in(key_list[10], 1), 0, ORIENT - 1).astype(jnp.int32),
        "send_lists": with_ends(jax.random.randint(key_list[11], (DEVICES_ALL, 4, NCLUS, SLOT), 0, E_DEV), jax.random.fold_in(key_list[11], 1), 0, E_DEV - 1).astype(jnp.int32),
        "sub_lists": with_ends(jax.random.randint(key_list[12], (DEVICES_ALL, NCLUS, SLOT_SUB), 0, E_DEV), jax.random.fold_in(key_list[12], 1), 0, E_DEV - 1).astype(jnp.int32),
    }


base_step = 0.25


def apply_small(matrix, values):
    running = matrix[:, 0, :][:, None, :] * values[0][None, :, :]
    for column in range(1, values.shape[0]):
        running = running + matrix[:, column, :][:, None, :] * values[column][None, :, :]
    return running


def apply_modes(matrix, values):
    return jnp.einsum("mn,qne->qme", matrix, values, precision=lax.Precision.HIGHEST, preferred_element_type=jnp.float32)


def predict(start_state, stars, deriv_stiff):
    series = [start_state]
    current = start_state
    for deriv_order in range(NDER - 1):
        running = jnp.zeros_like(current)
        for direction in range(3):
            running = running + apply_small(stars[direction], apply_modes(deriv_stiff[direction], current))
        current = -running
        series.append(current)
    results = []
    for cluster in range(NCLUS):
        step_width = base_step * 2.0 ** cluster
        running = jnp.zeros_like(start_state)
        factor = 1.0
        for deriv_order in range(NDER):
            factor = factor * step_width / (deriv_order + 1)
            running = running + factor * series[deriv_order]
        results.append(running)
    return jnp.stack(results)


def reference(modal_state, deriv_stiff, volume_stiff, local_flux, neighbour_flux, star_matrices, plus_flux, minus_flux, cluster_ids, face_neighbours, face_orient, send_lists, sub_lists):
    local_count = E_DEV
    partitions = N_REGION * N_SUB
    region_slots = 4 * SLOT

    def predict_device(device):
        start = device * local_count
        start_state = lax.dynamic_slice_in_dim(modal_state, start, local_count, 2)
        stars = lax.dynamic_slice_in_dim(star_matrices, start, local_count, 3)
        return predict(start_state, stars, deriv_stiff)

    integrals = lax.map(predict_device, jnp.arange(partitions, dtype=jnp.int32))
    offsets = jnp.array([-2, -1, 1, 2], dtype=jnp.int32)

    def update_device(device):
        start = device * local_count
        region = device // N_SUB
        sub_index = device % N_SUB
        start_state = lax.dynamic_slice_in_dim(modal_state, start, local_count, 2)
        stars = lax.dynamic_slice_in_dim(star_matrices, start, local_count, 3)
        plus_side = lax.dynamic_slice_in_dim(plus_flux, start, local_count, 3)
        minus_side = lax.dynamic_slice_in_dim(minus_flux, start, local_count, 3)
        clusters = lax.dynamic_slice_in_dim(cluster_ids, start, local_count, 0)
        neighbours = lax.dynamic_slice_in_dim(face_neighbours, start, local_count, 1)
        orients = lax.dynamic_slice_in_dim(face_orient, start, local_count, 1)
        local_all = integrals[device]
        own_integral = jnp.zeros_like(start_state)
        for cluster in range(NCLUS):
            own_integral = jnp.where(clusters[None, None, :] == cluster, local_all[cluster], own_integral)
        result = start_state
        for direction in range(3):
            result = result + apply_small(stars[direction], apply_modes(volume_stiff[direction], own_integral))
        for face_index in range(4):
            result = result - apply_small(plus_side[face_index], apply_modes(local_flux[face_index], own_integral))
            neighbour_entry = neighbours[face_index]
            is_local = neighbour_entry < local_count
            is_region = (neighbour_entry >= local_count) & (neighbour_entry < local_count + region_slots)
            region_pos = jnp.clip(neighbour_entry - local_count, 0, region_slots - 1)
            block_index = region_pos // SLOT
            slot_index = region_pos % SLOT
            source_region = (region + offsets[block_index]) % N_REGION
            region_device = source_region * N_SUB + sub_index
            region_element = send_lists[region_device, 3 - block_index, clusters, slot_index]
            sub_pos = jnp.clip(neighbour_entry - local_count - region_slots, 0, N_SUB * SLOT_SUB - 1)
            sub_device = region * N_SUB + sub_pos // SLOT_SUB
            sub_element = sub_lists[sub_device, clusters, sub_pos % SLOT_SUB]
            source_device = jnp.where(is_local, device, jnp.where(is_region, region_device, sub_device)).astype(jnp.int32)
            source_element = jnp.where(is_local, jnp.clip(neighbour_entry, 0, local_count - 1), jnp.where(is_region, region_element, sub_element)).astype(jnp.int32)
            gathered = integrals[source_device, clusters, :, :, source_element]
            partner = jnp.transpose(gathered, (1, 2, 0))
            mixed = apply_small(minus_side[face_index], partner)
            selected = jnp.zeros_like(mixed)
            for orient_id in range(ORIENT):
                selected = jnp.where(orients[face_index][None, None, :] == orient_id, apply_modes(neighbour_flux[face_index, orient_id], mixed), selected)
            result = result - selected
        return result

    updated = lax.map(update_device, jnp.arange(partitions, dtype=jnp.int32))
    return jnp.transpose(updated, (1, 2, 0, 3)).reshape(NQ, M, partitions * local_count)
```

```python
import jax
import jax.numpy as jnp
from jax import lax
from jax.experimental import pallas as pl
from jax.experimental.pallas import tpu as pltpu
from jax.sharding import PartitionSpec as P

NDER = 6
BASE_STEP = 0.25
OFFSETS = (-2, -1, 1, 2)
BLOCKS = 4
LANES = 128
QUARTER = 32
F32 = jnp.float32
BF16 = jnp.bfloat16


def split_rows(values):
    high = values.astype(BF16).astype(F32)
    low = values - high
    blank = jnp.zeros((8, values.shape[1]), F32)
    return jnp.concatenate([high, high, low, blank], axis=0).astype(BF16)


def split_columns(matrix):
    high = matrix.astype(BF16).astype(F32)
    low = matrix - high
    blank = jnp.zeros((matrix.shape[0], 8), F32)
    return jnp.concatenate([high, low, high, blank], axis=1).astype(BF16)


def odd_and_high(shape):
    quarter = lax.broadcasted_iota(jnp.int32, shape, 1) // QUARTER
    return quarter % 2 == 1, quarter >= 2


def turned(odd, high, rows):
    pairs = [jnp.where(odd, rows[(k + 1) % BLOCKS], rows[k]) for k in range(BLOCKS)]
    return [
        jnp.where(high, pairs[(2 - i) % BLOCKS], pairs[(-i) % BLOCKS]) for i in range(BLOCKS)
    ]


def lane_gather(values, index):
    return jnp.take_along_axis(values, index, axis=1)


def groups(count):
    return (count + BLOCKS - 1) // BLOCKS


def taylor_factors(clusters):
    factors = []
    for cluster in range(clusters):
        width = BASE_STEP * 2.0**cluster
        factor = 1.0
        row = []
        for order in range(NDER):
            factor = factor * width / (order + 1)
            row.append(factor)
        factors.append(row)
    return factors


def pairing_blocks(region):
    second = region // 2 % 2
    odd = region % 2
    return [3 * second, 1 + odd, 3 - 3 * second, 2 - odd]


def predict_kernel(
    state_hbm,
    stiff_hbm,
    star_hbm,
    send_hbm,
    sub_hbm,
    cluster_hbm,
    face_hbm,
    orient_hbm,
    region_index_ref,
    sub_index_ref,
    integral_hbm,
    table_hbm,
    region_hbm0,
    region_hbm1,
    region_hbm2,
    region_hbm3,
    within_hbm0,
    within_hbm1,
    within_hbm2,
    stiff_ref,
    star_ref,
    send_ref,
    sub_ref,
    cluster_ref,
    face_ref,
    orient_ref,
    series_ref,
    product_ref,
    integral_ref,
    table_ref,
    region_ref,
    within_ref,
    arrived,
    sent,
):
    region_hbms = (region_hbm0, region_hbm1, region_hbm2, region_hbm3)
    quants, modes, lanes = state_hbm.shape
    clusters = integral_hbm.shape[0]
    dims = stiff_hbm.shape[0]
    copies = [
        pltpu.make_async_copy(source, target, arrived.at[place])
        for place, (source, target) in enumerate(
            [
                (stiff_hbm, stiff_ref),
                (state_hbm, series_ref.at[0]),
                (star_hbm, star_ref),
                (send_hbm, send_ref),
                (sub_hbm, sub_ref),
                (cluster_hbm, cluster_ref),
                (face_hbm, face_ref),
                (orient_hbm, orient_ref),
            ]
        )
    ]
    for copy in copies:
        copy.start()
    copies[0].wait()
    stacked = jnp.concatenate([stiff_ref[d] for d in range(dims)], axis=0)
    lhs = split_columns(-stacked)
    copies[1].wait()
    block = 3
    blocks = [range(first, min(first + block, quants)) for first in range(0, quants, block)]

    def multiply(slot, rows, values):
        product = jnp.dot(
            lhs, split_rows(jnp.concatenate(values, axis=1)), preferred_element_type=F32
        )
        for place, row in enumerate(rows):
            product_ref[slot, row] = product[:, place * lanes : (place + 1) * lanes]

    for rows in blocks:
        multiply(0, rows, [series_ref[0, row] for row in rows])
    for copy in copies[2:]:
        copy.wait()
    for order in range(1, NDER):
        slot = (order - 1) % 2
        for rows in blocks:
            sums = [None for _ in rows]
            for column in range(quants):
                for d in range(dims):
                    value = product_ref[slot, column, pl.ds(d * modes, modes), :]
                    for place, row in enumerate(rows):
                        term = star_ref[row, column, pl.ds(d, 1), :] * value
                        sums[place] = term if sums[place] is None else sums[place] + term
            for place, row in enumerate(rows):
                series_ref[order, row] = sums[place]
            if order < NDER - 1:
                multiply(1 - slot, rows, sums)

    factors = taylor_factors(clusters)
    per_quant = modes // 8
    count = quants * per_quant
    odd, high = odd_and_high((8, lanes))
    lists = pairing_blocks(region_index_ref[0])
    index = []
    for cluster in range(clusters):
        base = jnp.concatenate(
            [send_ref[0, cluster, pl.ds(lists[s], 1), :] for s in range(BLOCKS)], axis=1
        )
        base = jnp.broadcast_to(base, (8, lanes))
        index.append([base] + [pltpu.roll(base, QUARTER * i, 1) for i in range(1, BLOCKS)])
    sub_slots = sub_ref.shape[2]
    blank = jnp.zeros((1, QUARTER - clusters * sub_slots), jnp.int32)
    row = jnp.concatenate([sub_ref[c] for c in range(clusters)] + [blank], axis=1)
    sub_index = jnp.broadcast_to(jnp.concatenate([row] * BLOCKS, axis=1), (8, lanes))
    owner = lax.broadcasted_iota(jnp.int32, (8, lanes), 1) % QUARTER // sub_slots
    chunk = 4
    leaving = []
    here = sub_index_ref[0]
    brought = pairing_blocks(region_index_ref[0])
    cluster_row = cluster_ref[...]
    for face in range(face_ref.shape[0]):
        entry = face_ref[pl.ds(face, 1), :]
        place = entry - lanes
        sub_place = place - BLOCKS * QUARTER
        block = place // QUARTER
        slot = sum(jnp.where(block == brought[p], p, 0) for p in range(BLOCKS))
        source = (sub_place // sub_slots) ^ here
        for i in range(BLOCKS):
            region = ((slot + i) & (BLOCKS - 1)) * QUARTER + (place & (QUARTER - 1))
            within = ((source + i) & (BLOCKS - 1)) * QUARTER + cluster_row * sub_slots
            within = within + (sub_place & (sub_slots - 1))
            table_ref[face, pl.ds(i, 1), :] = region & (lanes - 1)
            table_ref[face, pl.ds(BLOCKS + i, 1), :] = within & (lanes - 1)
        table_ref[face, pl.ds(2 * BLOCKS + 2, 1), :] = entry & (lanes - 1)
        table_ref[face, pl.ds(2 * BLOCKS + 3, 1), :] = cluster_row
        kind = jnp.where(place < 0, -1, jnp.where(sub_place < 0, cluster_row, clusters))
        table_ref[face, pl.ds(2 * BLOCKS, 1), :] = kind
        table_ref[face, pl.ds(2 * BLOCKS + 1, 1), :] = orient_ref[pl.ds(face, 1), :]

    for group in range(groups(count)):
        picked = [[] for _ in range(clusters)]
        shared = []
        for member in range(BLOCKS):
            at = group * BLOCKS + member
            if at >= count:
                for cluster in range(clusters):
                    picked[cluster].append(picked[cluster][-1])
                shared.append(shared[-1])
                continue
            quant, rows = at // per_quant, pl.ds(at % per_quant * 8, 8)
            series = [series_ref[order, quant, rows, :] for order in range(NDER)]
            for cluster in range(clusters):
                total = factors[cluster][0] * series[0]
                for order in range(1, NDER):
                    total = total + factors[cluster][order] * series[order]
                integral_ref[cluster, at] = total
                picked[cluster].append(lane_gather(total, index[cluster][member]))
                other = lane_gather(total, sub_index)
                within = other if cluster == 0 else jnp.where(owner == cluster, other, within)
            shared.append(within)
        for cluster in range(clusters):
            for b, packed in enumerate(turned(odd, high, picked[cluster])):
                region_ref[b, cluster, group] = packed
        for k, packed in enumerate(turned(odd, high, shared)):
            within_ref[(0, 2, 1, 3)[k], group] = packed
        if (group + 1) % chunk == 0:
            part = pl.ds(group + 1 - chunk, chunk)
            leaving += [
                pltpu.make_async_copy(
                    region_ref.at[b, :, part],
                    region_hbms[b].at[:, part],
                    sent.at[len(leaving) + b],
                )
                for b in range(BLOCKS)
            ]
            for copy in leaving[-BLOCKS:]:
                copy.start()
    for source, target in (
        (within_ref.at[pl.ds(2, 2)], within_hbm1),
        (within_ref.at[0], within_hbm0),
        (within_ref.at[pl.ds(1, 1)], within_hbm2),
        (integral_ref, integral_hbm),
        (table_ref, table_hbm),
    ):
        leaving.append(pltpu.make_async_copy(source, target, sent.at[len(leaving)]))
        leaving[-1].start()
    for copy in leaving:
        copy.wait()


def near_kernel(table_ref, integral_ref, partner_ref):
    clusters, quants, modes, lanes = integral_ref.shape

    def one_face(face, _):
        index = jnp.broadcast_to(table_ref[face, pl.ds(2 * BLOCKS + 2, 1), :], (modes, lanes))
        cluster_row = table_ref[face, pl.ds(2 * BLOCKS + 3, 1), :]
        for quant in range(quants):
            total = lane_gather(integral_ref[0, quant], index)
            for cluster in range(1, clusters):
                other = lane_gather(integral_ref[cluster, quant], index)
                total = jnp.where(cluster_row == cluster, other, total)
            partner_ref[face, quant] = total
        return 0

    lax.fori_loop(0, table_ref.shape[0], one_face, 0)


def own_kernel(
    table_ref,
    volume_ref,
    local_ref,
    integral_ref,
    state_ref,
    star_ref,
    plus_ref,
    neighbour_ref,
    result_ref,
    flux_ref,
    lhs_ref,
    product_ref,
):
    quants, modes, lanes = state_ref.shape
    clusters = integral_ref.shape[0]
    dims = volume_ref.shape[0]
    faces, orients = neighbour_ref.shape[:2]
    cluster_row = table_ref[0, pl.ds(2 * BLOCKS + 3, 1), :]

    stacked = jnp.concatenate(
        [volume_ref[d] for d in range(dims)] + [-local_ref[f] for f in range(faces)], axis=0
    )
    lhs_ref[...] = split_columns(stacked)
    for quant in range(quants):
        own = integral_ref[0, quant]
        for cluster in range(1, clusters):
            own = jnp.where(cluster_row == cluster, integral_ref[cluster, quant], own)
        product_ref[quant] = jnp.dot(lhs_ref[...], split_rows(own), preferred_element_type=F32)

    def own_row(row, _):
        total = state_ref[row]
        for column in range(quants):
            for part in range(dims + faces):
                value = product_ref[column, pl.ds(part * modes, modes), :]
                if part < dims:
                    matrix = star_ref[row, column, pl.ds(part, 1), :]
                else:
                    matrix = plus_ref[row, column, pl.ds(part - dims, 1), :]
                total = total + matrix * value
        result_ref[row] = total
        return 0

    lax.fori_loop(0, quants, own_row, 0)

    def one_face(face, _):
        stack = jnp.concatenate([-neighbour_ref[face, o] for o in range(orients)], axis=0)
        flux_ref[face] = split_columns(stack)
        return 0

    lax.fori_loop(0, faces, one_face, 0)


def neighbour_kernel(
    region_refs,
    first_ref,
    beside_ref,
    across_ref,
    table_ref,
    near_ref,
    minus_ref,
    flux_ref,
    own_ref,
    result_ref,
    pool_ref,
    sub_pool_ref,
    partner_ref,
):
    quants, modes, lanes = own_ref.shape
    faces = flux_ref.shape[0]
    clusters = region_refs[0].shape[0]
    orients = flux_ref.shape[1] // modes
    per_quant = modes // 8
    count = quants * per_quant
    odd, high = odd_and_high((8, lanes))

    def spread(face, row):
        return jnp.broadcast_to(table_ref[face, pl.ds(row, 1), :], (8, lanes))

    def unpack(group):
        for cluster in range(clusters):
            pools = turned(odd, high, [region_refs[b][cluster, group] for b in range(BLOCKS)])
            for member, pool in enumerate(pools):
                if group * BLOCKS + member < count:
                    pool_ref[cluster, group * BLOCKS + member] = pool
        within = [first_ref[group], beside_ref[0, group], across_ref[0, group], across_ref[1, group]]
        pools = turned(odd, high, within)
        for member, pool in enumerate(pools):
            if group * BLOCKS + member < count:
                sub_pool_ref[group * BLOCKS + member] = pool

    def gather(face, ats):
        kind = spread(face, 2 * BLOCKS)
        hits = [kind == cluster for cluster in range(clusters + 1)]
        for at in ats:
            rows = pl.ds(at % per_quant * 8, 8)
            region_index = spread(face, at % BLOCKS)
            sub_index = spread(face, BLOCKS + at % BLOCKS)
            total = near_ref[face, at // per_quant, rows, :]
            for cluster in range(clusters):
                other = lane_gather(pool_ref[cluster, at], region_index)
                total = jnp.where(hits[cluster], other, total)
            other = lane_gather(sub_pool_ref[at], sub_index)
            partner_ref[face, at // per_quant, rows, :] = jnp.where(hits[clusters], other, total)

    block = 2
    blocks = [range(first, min(first + block, quants)) for first in range(0, quants, block)]

    def flux(face, rows):
        orient = table_ref[face, pl.ds(2 * BLOCKS + 1, 1), :]
        mixed = [None for _ in rows]
        for column in range(quants):
            value = partner_ref[face, column]
            for place, row in enumerate(rows):
                term = minus_ref[row, column, pl.ds(face, 1), :] * value
                mixed[place] = term if mixed[place] is None else mixed[place] + term
        every = jnp.dot(
            flux_ref[face], split_rows(jnp.concatenate(mixed, axis=1)), preferred_element_type=F32
        )
        for place, row in enumerate(rows):
            part = every[:, place * lanes : (place + 1) * lanes]
            selected = part[0:modes]
            for o in range(1, orients):
                selected = jnp.where(orient == o, part[o * modes : (o + 1) * modes], selected)
            if face == 0:
                result_ref[row] = own_ref[row] + selected
            else:
                result_ref[row] += selected

    for group in range(groups(count)):
        unpack(group)
    gather(0, range(count))
    for face in range(faces):
        step = (count + len(blocks) - 1) // len(blocks)
        for place, rows in enumerate(blocks):
            flux(face, rows)
            if face + 1 < faces:
                gather(face + 1, range(place * step, min((place + 1) * step, count)))


def whole(count):
    return [pl.BlockSpec(memory_space=pltpu.VMEM) for _ in range(count)]


def far(count):
    return [pl.BlockSpec(memory_space=pltpu.HBM) for _ in range(count)]


def paired(value, axis, pairing):
    count = lax.axis_size(axis)
    pairs = []
    for source in range(count):
        offset = OFFSETS[pairing_blocks(source)[pairing]]
        pairs.append((source, (source + offset) % count))
    return lax.ppermute(value, axis, pairs)


def swapped(value, axis, bit):
    return lax.ppermute(value, axis, [(s, s ^ bit) for s in range(lax.axis_size(axis))])


def local(
    modal_state,
    deriv_stiff,
    volume_stiff,
    local_flux,
    neighbour_flux,
    star_matrices,
    plus_flux,
    minus_flux,
    cluster_ids,
    face_neighbours,
    face_orient,
    send_lists,
    sub_lists,
):
    quants, modes, lanes = modal_state.shape
    clusters = send_lists.shape[2]
    faces, orients = neighbour_flux.shape[:2]
    dims = deriv_stiff.shape[0]
    depth = 3 * modes + 8
    count = quants * modes // 8
    fours = groups(count)
    near_params = pltpu.CompilerParams(vmem_limit_bytes=40 * 1024 * 1024)
    params = pltpu.CompilerParams(vmem_limit_bytes=60 * 1024 * 1024)
    shape = jax.ShapeDtypeStruct
    stars, plus, minus = (
        jnp.transpose(matrix, (1, 2, 0, 3)) for matrix in (star_matrices, plus_flux, minus_flux)
    )
    sends = jnp.transpose(send_lists, (0, 2, 1, 3))
    subs = jnp.transpose(sub_lists, (1, 0, 2))

    here = lax.axis_index("sub").astype(jnp.int32).reshape(1)
    region = lax.axis_index("region").astype(jnp.int32).reshape(1)

    integrals, table, *packed = pl.pallas_call(
        predict_kernel,
        out_shape=(
            shape((clusters, count, 8, lanes), F32),
            shape((faces, 2 * BLOCKS + 8, lanes), jnp.int32),
            *[shape((clusters, fours, 8, lanes), F32)] * BLOCKS,
            shape((fours, 8, lanes), F32),
            shape((2, fours, 8, lanes), F32),
            shape((1, fours, 8, lanes), F32),
        ),
        in_specs=far(8) + [pl.BlockSpec(memory_space=pltpu.SMEM)] * 2,
        out_specs=tuple(far(5 + BLOCKS)),
        scratch_shapes=[
            pltpu.VMEM(deriv_stiff.shape, F32),
            pltpu.VMEM(stars.shape, F32),
            pltpu.VMEM(sends.shape, jnp.int32),
            pltpu.VMEM(subs.shape, jnp.int32),
            pltpu.VMEM((1, lanes), jnp.int32),
            pltpu.VMEM(face_neighbours.shape, jnp.int32),
            pltpu.VMEM(face_orient.shape, jnp.int32),
            pltpu.VMEM((NDER, quants, modes, lanes), F32),
            pltpu.VMEM((2, quants, dims * modes, lanes), F32),
            pltpu.VMEM((clusters, count, 8, lanes), F32),
            pltpu.VMEM((faces, 2 * BLOCKS + 8, lanes), jnp.int32),
            pltpu.VMEM((BLOCKS, clusters, fours, 8, lanes), F32),
            pltpu.VMEM((BLOCKS, fours, 8, lanes), F32),
            pltpu.SemaphoreType.DMA((8,)),
            pltpu.SemaphoreType.DMA((fours + 5,)),
        ],
        compiler_params=params,
        name="predict",
    )(
        modal_state,
        deriv_stiff,
        stars,
        sends,
        subs,
        cluster_ids.reshape(1, lanes),
        face_neighbours,
        face_orient,
        region,
        here,
    )

    arrived = [paired(packed[p], "region", p) for p in range(BLOCKS)]
    first, beside, across = packed[BLOCKS:]
    beside = swapped(beside, "sub", 1)
    across = swapped(jnp.concatenate([across, beside[1:]], axis=0), "sub", 2)
    integrals = integrals.reshape(clusters, quants, modes, lanes)
    near_partner = pl.pallas_call(
        near_kernel,
        out_shape=shape((faces, quants, modes, lanes), F32),
        in_specs=whole(2),
        out_specs=whole(1)[0],
        compiler_params=near_params,
        cost_estimate=pl.CostEstimate(
            flops=4_000_000_000, bytes_accessed=8_000_000, transcendentals=0
        ),
        name="near",
    )(table, integrals)

    own, flux = pl.pallas_call(
        own_kernel,
        out_shape=(
            shape((quants, modes, lanes), F32),
            shape((faces, orients * modes, depth), BF16),
        ),
        in_specs=whole(8),
        out_specs=tuple(whole(2)),
        scratch_shapes=[
            pltpu.VMEM(((dims + faces) * modes, depth), BF16),
            pltpu.VMEM((quants, (dims + faces) * modes, lanes), F32),
        ],
        compiler_params=near_params,
        cost_estimate=pl.CostEstimate(
            flops=4_000_000_000, bytes_accessed=8_000_000, transcendentals=0
        ),
        name="own",
    )(
        table,
        volume_stiff,
        local_flux,
        integrals,
        modal_state,
        stars,
        plus,
        neighbour_flux,
    )

    return pl.pallas_call(
        neighbour_kernel,
        out_shape=shape((quants, modes, lanes), F32),
        in_specs=[whole(BLOCKS), *whole(8)],
        out_specs=whole(1)[0],
        scratch_shapes=[
            pltpu.VMEM((clusters, count, 8, lanes), F32),
            pltpu.VMEM((count, 8, lanes), F32),
            pltpu.VMEM((faces, quants, modes, lanes), F32),
        ],
        compiler_params=near_params,
        name="neighbour",
    )(arrived, first, beside, across, table, near_partner, minus, flux, own)


def solution(mesh):
    return jax.shard_map(
        local,
        mesh=mesh,
        in_specs=(
            P(None, None, ("region", "sub")),
            P(),
            P(),
            P(),
            P(),
            P(None, None, None, ("region", "sub")),
            P(None, None, None, ("region", "sub")),
            P(None, None, None, ("region", "sub")),
            P(("region", "sub")),
            P(None, ("region", "sub")),
            P(None, ("region", "sub")),
            P(("region", "sub"), None, None, None),
            P(("region", "sub"), None, None),
        ),
        out_specs=P(None, None, ("region", "sub")),
        check_vma=False,
    )
```

```python
import jax
import jax.numpy as jnp
from jax import lax
from jax.experimental import pallas as pl
from jax.experimental.pallas import tpu as pltpu
from jax.sharding import PartitionSpec as P

NDER = 6
BASE_STEP = 0.25
OFFSETS = (-2, -1, 1, 2)
BLOCKS = 4
LANES = 128
QUARTER = 32
F32 = jnp.float32
BF16 = jnp.bfloat16


def split_rows(values):
    high = values.astype(BF16).astype(F32)
    low = values - high
    blank = jnp.zeros((8, values.shape[1]), F32)
    return jnp.concatenate([high, high, low, blank], axis=0).astype(BF16)


def split_columns(matrix):
    high = matrix.astype(BF16).astype(F32)
    low = matrix - high
    blank = jnp.zeros((matrix.shape[0], 8), F32)
    return jnp.concatenate([high, low, high, blank], axis=1).astype(BF16)


def odd_and_high(shape):
    quarter = lax.broadcasted_iota(jnp.int32, shape, 1) // QUARTER
    return quarter % 2 == 1, quarter >= 2


def turned(odd, high, rows):
    pairs = [jnp.where(odd, rows[(k + 1) % BLOCKS], rows[k]) for k in range(BLOCKS)]
    return [
        jnp.where(high, pairs[(2 - i) % BLOCKS], pairs[(-i) % BLOCKS]) for i in range(BLOCKS)
    ]


def lane_gather(values, index):
    numbers = lax.GatherDimensionNumbers(
        offset_dims=(),
        collapsed_slice_dims=(1,),
        start_index_map=(1,),
        operand_batching_dims=(0,),
        start_indices_batching_dims=(0,),
    )
    return lax.gather(
        values,
        index[:, :, None],
        dimension_numbers=numbers,
        slice_sizes=(1, 1),
        mode=lax.GatherScatterMode.PROMISE_IN_BOUNDS,
    )


def groups(count):
    return (count + BLOCKS - 1) // BLOCKS


def taylor_factors(clusters):
    factors = []
    for cluster in range(clusters):
        width = BASE_STEP * 2.0**cluster
        factor = 1.0
        row = []
        for order in range(NDER):
            factor = factor * width / (order + 1)
            row.append(factor)
        factors.append(row)
    return factors


def brought_blocks(sub):
    odd = sub % 2
    return [0, BLOCKS - 1, 1 + odd, 2 - odd]


def predict_kernel(
    state_hbm,
    stiff_hbm,
    star_hbm,
    send_hbm,
    sub_hbm,
    cluster_hbm,
    face_hbm,
    orient_hbm,
    sub_index_ref,
    integral_hbm,
    table_hbm,
    region_hbm0,
    region_hbm1,
    region_hbm2,
    region_hbm3,
    within_hbm0,
    within_hbm1,
    within_hbm2,
    stiff_ref,
    star_ref,
    send_ref,
    sub_ref,
    cluster_ref,
    face_ref,
    orient_ref,
    series_ref,
    product_ref,
    integral_ref,
    table_ref,
    region_ref,
    within_ref,
    arrived,
    sent,
):
    region_hbms = (region_hbm0, region_hbm1, region_hbm2, region_hbm3)
    quants, modes, lanes = state_hbm.shape
    clusters = integral_hbm.shape[0]
    dims = stiff_hbm.shape[0]
    copies = [
        pltpu.make_async_copy(source, target, arrived.at[place])
        for place, (source, target) in enumerate(
            [
                (stiff_hbm, stiff_ref),
                (state_hbm, series_ref.at[0]),
                (star_hbm, star_ref),
                (send_hbm, send_ref),
                (sub_hbm, sub_ref),
                (cluster_hbm, cluster_ref),
                (face_hbm, face_ref),
                (orient_hbm, orient_ref),
            ]
        )
    ]
    for copy in copies:
        copy.start()
    copies[0].wait()
    stacked = jnp.concatenate([stiff_ref[d] for d in range(dims)], axis=0)
    lhs = split_columns(-stacked)
    copies[1].wait()
    block = 3
    blocks = [range(first, min(first + block, quants)) for first in range(0, quants, block)]

    def multiply(slot, rows, values):
        product = jnp.dot(
            lhs, split_rows(jnp.concatenate(values, axis=1)), preferred_element_type=F32
        )
        for place, row in enumerate(rows):
            product_ref[slot, row] = product[:, place * lanes : (place + 1) * lanes]

    for rows in blocks:
        multiply(0, rows, [series_ref[0, row] for row in rows])
    for copy in copies[2:]:
        copy.wait()
    for order in range(1, NDER):
        slot = (order - 1) % 2
        for rows in blocks:
            sums = [None for _ in rows]
            for column in range(quants):
                for d in range(dims):
                    value = product_ref[slot, column, pl.ds(d * modes, modes), :]
                    for place, row in enumerate(rows):
                        term = star_ref[row, column, pl.ds(d, 1), :] * value
                        sums[place] = term if sums[place] is None else sums[place] + term
            for place, row in enumerate(rows):
                series_ref[order, row] = sums[place]
            if order < NDER - 1:
                multiply(1 - slot, rows, sums)

    factors = taylor_factors(clusters)
    per_quant = modes // 8
    count = quants * per_quant
    odd, high = odd_and_high((8, lanes))
    lists = [BLOCKS - 1 - block for block in brought_blocks(sub_index_ref[0])]
    index = []
    for cluster in range(clusters):
        base = jnp.concatenate(
            [send_ref[0, cluster, pl.ds(lists[s], 1), :] for s in range(BLOCKS)], axis=1
        )
        base = jnp.broadcast_to(base, (8, lanes))
        index.append([base] + [pltpu.roll(base, QUARTER * i, 1) for i in range(1, BLOCKS)])
    sub_slots = sub_ref.shape[2]
    blank = jnp.zeros((1, QUARTER - clusters * sub_slots), jnp.int32)
    row = jnp.concatenate([sub_ref[c] for c in range(clusters)] + [blank], axis=1)
    sub_index = jnp.broadcast_to(jnp.concatenate([row] * BLOCKS, axis=1), (8, lanes))
    owner = lax.broadcasted_iota(jnp.int32, (8, lanes), 1) % QUARTER // sub_slots
    chunk = 4
    leaving = []
    here = sub_index_ref[0]
    brought = brought_blocks(sub_index_ref[0])
    cluster_row = cluster_ref[...]
    for face in range(face_ref.shape[0]):
        entry = face_ref[pl.ds(face, 1), :]
        place = entry - lanes
        sub_place = place - BLOCKS * QUARTER
        block = place // QUARTER
        slot = sum(jnp.where(block == brought[p], p, 0) for p in range(BLOCKS))
        source = (sub_place // sub_slots) ^ here
        for i in range(BLOCKS):
            region = ((slot + i) & (BLOCKS - 1)) * QUARTER + (place & (QUARTER - 1))
            within = ((source + i) & (BLOCKS - 1)) * QUARTER + cluster_row * sub_slots
            within = within + (sub_place & (sub_slots - 1))
            table_ref[face, pl.ds(i, 1), :] = region & (lanes - 1)
            table_ref[face, pl.ds(BLOCKS + i, 1), :] = within & (lanes - 1)
        table_ref[face, pl.ds(2 * BLOCKS + 2, 1), :] = entry & (lanes - 1)
        table_ref[face, pl.ds(2 * BLOCKS + 3, 1), :] = cluster_row
        kind = jnp.where(place < 0, -1, jnp.where(sub_place < 0, cluster_row, clusters))
        table_ref[face, pl.ds(2 * BLOCKS, 1), :] = kind
        table_ref[face, pl.ds(2 * BLOCKS + 1, 1), :] = orient_ref[pl.ds(face, 1), :]

    for group in range(groups(count)):
        picked = [[] for _ in range(clusters)]
        shared = []
        for member in range(BLOCKS):
            at = group * BLOCKS + member
            if at >= count:
                for cluster in range(clusters):
                    picked[cluster].append(picked[cluster][-1])
                shared.append(shared[-1])
                continue
            quant, rows = at // per_quant, pl.ds(at % per_quant * 8, 8)
            series = [series_ref[order, quant, rows, :] for order in range(NDER)]
            for cluster in range(clusters):
                total = factors[cluster][0] * series[0]
                for order in range(1, NDER):
                    total = total + factors[cluster][order] * series[order]
                integral_ref[cluster, at] = total
                picked[cluster].append(lane_gather(total, index[cluster][member]))
                other = lane_gather(total, sub_index)
                within = other if cluster == 0 else jnp.where(owner == cluster, other, within)
            shared.append(within)
        for cluster in range(clusters):
            for b, packed in enumerate(turned(odd, high, picked[cluster])):
                region_ref[b, cluster, group] = packed
        for k, packed in enumerate(turned(odd, high, shared)):
            within_ref[(0, 2, 1, 3)[k], group] = packed
        if (group + 1) % chunk == 0:
            part = pl.ds(group + 1 - chunk, chunk)
            leaving += [
                pltpu.make_async_copy(
                    region_ref.at[b, :, part],
                    region_hbms[b].at[:, part],
                    sent.at[len(leaving) + b],
                )
                for b in range(BLOCKS)
            ]
            for copy in leaving[-BLOCKS:]:
                copy.start()
    for source, target in (
        (within_ref.at[pl.ds(2, 2)], within_hbm1),
        (within_ref.at[0], within_hbm0),
        (within_ref.at[pl.ds(1, 1)], within_hbm2),
        (integral_ref, integral_hbm),
        (table_ref, table_hbm),
    ):
        leaving.append(pltpu.make_async_copy(source, target, sent.at[len(leaving)]))
        leaving[-1].start()
    for copy in leaving:
        copy.wait()


def near_kernel(table_ref, integral_ref, partner_ref):
    clusters, quants, modes, lanes = integral_ref.shape
    chosen = jnp.broadcast_to(table_ref[0, pl.ds(2 * BLOCKS + 3, 1), :], (8, lanes))
    masks = [chosen == cluster for cluster in range(clusters)]

    def one_face(face, _):
        index = jnp.broadcast_to(table_ref[face, pl.ds(2 * BLOCKS + 2, 1), :], (8, lanes))
        for quant in range(quants):
            for first in range(0, modes, 8):
                rows = pl.ds(first, 8)
                total = lane_gather(integral_ref[0, quant, rows, :], index)
                for cluster in range(1, clusters):
                    other = lane_gather(integral_ref[cluster, quant, rows, :], index)
                    total = jnp.where(masks[cluster], other, total)
                partner_ref[face, quant, rows, :] = total
        return 0

    lax.fori_loop(0, table_ref.shape[0], one_face, 0)


def own_kernel(
    table_ref,
    volume_ref,
    local_ref,
    integral_ref,
    state_ref,
    star_ref,
    plus_ref,
    neighbour_ref,
    result_ref,
    flux_ref,
    lhs_ref,
    product_ref,
):
    quants, modes, lanes = state_ref.shape
    clusters = integral_ref.shape[0]
    dims = volume_ref.shape[0]
    faces, orients = neighbour_ref.shape[:2]
    chosen = jnp.broadcast_to(table_ref[0, pl.ds(2 * BLOCKS + 3, 1), :], (8, lanes))
    masks = [chosen == cluster for cluster in range(clusters)]

    stacked = jnp.concatenate(
        [volume_ref[d] for d in range(dims)] + [-local_ref[f] for f in range(faces)], axis=0
    )
    lhs_ref[...] = split_columns(stacked)
    for quant in range(quants):
        parts = []
        for first in range(0, modes, 8):
            rows = pl.ds(first, 8)
            own = integral_ref[0, quant, rows, :]
            for cluster in range(1, clusters):
                own = jnp.where(masks[cluster], integral_ref[cluster, quant, rows, :], own)
            parts.append(own)
        product_ref[quant] = jnp.dot(
            lhs_ref[...], split_rows(jnp.concatenate(parts, axis=0)), preferred_element_type=F32
        )

    def own_row(row, _):
        total = state_ref[row]
        for column in range(quants):
            for part in range(dims + faces):
                value = product_ref[column, pl.ds(part * modes, modes), :]
                if part < dims:
                    matrix = star_ref[row, column, pl.ds(part, 1), :]
                else:
                    matrix = plus_ref[row, column, pl.ds(part - dims, 1), :]
                total = total + matrix * value
        result_ref[row] = total
        return 0

    lax.fori_loop(0, quants, own_row, 0)

    def one_face(face, _):
        stack = jnp.concatenate([-neighbour_ref[face, o] for o in range(orients)], axis=0)
        flux_ref[face] = split_columns(stack)
        return 0

    lax.fori_loop(0, faces, one_face, 0)


def neighbour_kernel(
    region_refs,
    first_ref,
    beside_ref,
    across_ref,
    table_ref,
    near_ref,
    minus_ref,
    flux_ref,
    own_ref,
    result_ref,
    pool_ref,
    sub_pool_ref,
    partner_ref,
):
    quants, modes, lanes = own_ref.shape
    faces = flux_ref.shape[0]
    clusters = region_refs[0].shape[0]
    orients = flux_ref.shape[1] // modes
    per_quant = modes // 8
    count = quants * per_quant
    odd, high = odd_and_high((8, lanes))

    def spread(face, row):
        return jnp.broadcast_to(table_ref[face, pl.ds(row, 1), :], (8, lanes))

    def unpack(group):
        for cluster in range(clusters):
            pools = turned(odd, high, [region_refs[b][cluster, group] for b in range(BLOCKS)])
            for member, pool in enumerate(pools):
                if group * BLOCKS + member < count:
                    pool_ref[cluster, group * BLOCKS + member] = pool
        within = [first_ref[group], beside_ref[0, group], across_ref[0, group], across_ref[1, group]]
        pools = turned(odd, high, within)
        for member, pool in enumerate(pools):
            if group * BLOCKS + member < count:
                sub_pool_ref[group * BLOCKS + member] = pool

    def gather(face, ats):
        kind = spread(face, 2 * BLOCKS)
        hits = [kind == cluster for cluster in range(clusters + 1)]
        region_index = [spread(face, i) for i in range(BLOCKS)]
        sub_index = [spread(face, BLOCKS + i) for i in range(BLOCKS)]
        for at in ats:
            rows = pl.ds(at % per_quant * 8, 8)
            total = near_ref[face, at // per_quant, rows, :]
            for cluster in range(clusters):
                other = lane_gather(pool_ref[cluster, at], region_index[at % BLOCKS])
                total = jnp.where(hits[cluster], other, total)
            other = lane_gather(sub_pool_ref[at], sub_index[at % BLOCKS])
            partner_ref[face, at // per_quant, rows, :] = jnp.where(hits[clusters], other, total)

    block = 2
    blocks = [range(first, min(first + block, quants)) for first in range(0, quants, block)]

    def flux(face, rows):
        orient = spread(face, 2 * BLOCKS + 1)
        masks = [orient == o for o in range(orients)]
        mixed = [None for _ in rows]
        for column in range(quants):
            value = partner_ref[face, column]
            for place, row in enumerate(rows):
                term = minus_ref[row, column, pl.ds(face, 1), :] * value
                mixed[place] = term if mixed[place] is None else mixed[place] + term
        every = jnp.dot(
            flux_ref[face], split_rows(jnp.concatenate(mixed, axis=1)), preferred_element_type=F32
        )
        for place, row in enumerate(rows):
            for first in range(0, modes, 8):
                columns = slice(place * lanes, (place + 1) * lanes)
                total = every[first : first + 8, columns]
                for o in range(1, orients):
                    at = o * modes + first
                    total = jnp.where(masks[o], every[at : at + 8, columns], total)
                where = pl.ds(first, 8)
                if face == 0:
                    total = total + own_ref[row, where, :]
                else:
                    total = total + result_ref[row, where, :]
                result_ref[row, where, :] = total

    for group in range(groups(count)):
        unpack(group)
    gather(0, range(count))
    for face in range(faces):
        step = (count + len(blocks) - 1) // len(blocks)
        for place, rows in enumerate(blocks):
            flux(face, rows)
            if face + 1 < faces:
                gather(face + 1, range(place * step, min((place + 1) * step, count)))


def whole(count):
    return [pl.BlockSpec(memory_space=pltpu.VMEM) for _ in range(count)]


def far(count):
    return [pl.BlockSpec(memory_space=pltpu.HBM) for _ in range(count)]


def exchanged(value, place):
    regions, subs = lax.axis_size("region"), lax.axis_size("sub")
    pairs = []
    for region in range(regions):
        for sub in range(subs):
            target = (region - OFFSETS[brought_blocks(sub)[place]]) % regions
            pairs.append((region * subs + sub, target * subs + sub))
    return lax.ppermute(value, ("region", "sub"), pairs)


def swapped(value, axis, bit):
    return lax.ppermute(value, axis, [(s, s ^ bit) for s in range(lax.axis_size(axis))])


def local(
    modal_state,
    deriv_stiff,
    volume_stiff,
    local_flux,
    neighbour_flux,
    star_matrices,
    plus_flux,
    minus_flux,
    cluster_ids,
    face_neighbours,
    face_orient,
    send_lists,
    sub_lists,
):
    quants, modes, lanes = modal_state.shape
    clusters = send_lists.shape[2]
    faces, orients = neighbour_flux.shape[:2]
    dims = deriv_stiff.shape[0]
    depth = 3 * modes + 8
    count = quants * modes // 8
    fours = groups(count)
    near_params = pltpu.CompilerParams(vmem_limit_bytes=40 * 1024 * 1024)
    params = pltpu.CompilerParams(vmem_limit_bytes=60 * 1024 * 1024)
    shape = jax.ShapeDtypeStruct
    stars, plus, minus = (
        jnp.transpose(matrix, (1, 2, 0, 3)) for matrix in (star_matrices, plus_flux, minus_flux)
    )
    sends = jnp.transpose(send_lists, (0, 2, 1, 3))
    subs = jnp.transpose(sub_lists, (1, 0, 2))

    here = lax.axis_index("sub").astype(jnp.int32).reshape(1)

    integrals, table, *packed = pl.pallas_call(
        predict_kernel,
        out_shape=(
            shape((clusters, count, 8, lanes), F32),
            shape((faces, 2 * BLOCKS + 8, lanes), jnp.int32),
            *[shape((clusters, fours, 8, lanes), F32)] * BLOCKS,
            shape((fours, 8, lanes), F32),
            shape((2, fours, 8, lanes), F32),
            shape((1, fours, 8, lanes), F32),
        ),
        in_specs=far(8) + [pl.BlockSpec(memory_space=pltpu.SMEM)],
        out_specs=tuple(far(5 + BLOCKS)),
        scratch_shapes=[
            pltpu.VMEM(deriv_stiff.shape, F32),
            pltpu.VMEM(stars.shape, F32),
            pltpu.VMEM(sends.shape, jnp.int32),
            pltpu.VMEM(subs.shape, jnp.int32),
            pltpu.VMEM((1, lanes), jnp.int32),
            pltpu.VMEM(face_neighbours.shape, jnp.int32),
            pltpu.VMEM(face_orient.shape, jnp.int32),
            pltpu.VMEM((NDER, quants, modes, lanes), F32),
            pltpu.VMEM((2, quants, dims * modes, lanes), F32),
            pltpu.VMEM((clusters, count, 8, lanes), F32),
            pltpu.VMEM((faces, 2 * BLOCKS + 8, lanes), jnp.int32),
            pltpu.VMEM((BLOCKS, clusters, fours, 8, lanes), F32),
            pltpu.VMEM((BLOCKS, fours, 8, lanes), F32),
            pltpu.SemaphoreType.DMA((8,)),
            pltpu.SemaphoreType.DMA((fours + 5,)),
        ],
        compiler_params=params,
        name="predict",
    )(
        modal_state,
        deriv_stiff,
        stars,
        sends,
        subs,
        cluster_ids.reshape(1, lanes),
        face_neighbours,
        face_orient,
        here,
    )

    arrived = [exchanged(packed[p], p) for p in range(BLOCKS)]
    first, beside, across = packed[BLOCKS:]
    beside = swapped(beside, "sub", 1)
    across = swapped(jnp.concatenate([across, beside[1:]], axis=0), "sub", 2)
    integrals = integrals.reshape(clusters, quants, modes, lanes)
    near_partner = pl.pallas_call(
        near_kernel,
        out_shape=shape((faces, quants, modes, lanes), F32),
        in_specs=whole(2),
        out_specs=whole(1)[0],
        compiler_params=near_params,
        cost_estimate=pl.CostEstimate(
            flops=4_000_000_000, bytes_accessed=8_000_000, transcendentals=0
        ),
        name="near",
    )(table, integrals)

    own, flux = pl.pallas_call(
        own_kernel,
        out_shape=(
            shape((quants, modes, lanes), F32),
            shape((faces, orients * modes, depth), BF16),
        ),
        in_specs=whole(8),
        out_specs=tuple(whole(2)),
        scratch_shapes=[
            pltpu.VMEM(((dims + faces) * modes, depth), BF16),
            pltpu.VMEM((quants, (dims + faces) * modes, lanes), F32),
        ],
        compiler_params=near_params,
        cost_estimate=pl.CostEstimate(
            flops=4_000_000_000, bytes_accessed=8_000_000, transcendentals=0
        ),
        name="own",
    )(
        table,
        volume_stiff,
        local_flux,
        integrals,
        modal_state,
        stars,
        plus,
        neighbour_flux,
    )

    return pl.pallas_call(
        neighbour_kernel,
        out_shape=shape((quants, modes, lanes), F32),
        in_specs=[whole(BLOCKS), *whole(8)],
        out_specs=whole(1)[0],
        scratch_shapes=[
            pltpu.VMEM((clusters, count, 8, lanes), F32),
            pltpu.VMEM((count, 8, lanes), F32),
            pltpu.VMEM((faces, quants, modes, lanes), F32),
        ],
        compiler_params=near_params,
        name="neighbour",
    )(arrived, first, beside, across, table, near_partner, minus, flux, own)


def solution(mesh):
    return jax.shard_map(
        local,
        mesh=mesh,
        in_specs=(
            P(None, None, ("region", "sub")),
            P(),
            P(),
            P(),
            P(),
            P(None, None, None, ("region", "sub")),
            P(None, None, None, ("region", "sub")),
            P(None, None, None, ("region", "sub")),
            P(("region", "sub")),
            P(None, ("region", "sub")),
            P(None, ("region", "sub")),
            P(("region", "sub"), None, None, None),
            P(("region", "sub"), None, None),
        ),
        out_specs=P(None, None, ("region", "sub")),
        check_vma=False,
    )
```

```python
import jax
import jax.numpy as jnp
from jax import lax
from jax.experimental import pallas as pl
from jax.experimental.pallas import tpu as pltpu
from jax.sharding import PartitionSpec as P

NDER = 6
BASE_STEP = 0.25
OFFSETS = (-2, -1, 1, 2)
BLOCKS = 4
LANES = 128
QUARTER = 32
F32 = jnp.float32
BF16 = jnp.bfloat16


def split_rows(values):
    high = values.astype(BF16).astype(F32)
    low = values - high
    blank = jnp.zeros((8, values.shape[1]), F32)
    return jnp.concatenate([high, high, low, blank], axis=0).astype(BF16)


def split_columns(matrix):
    high = matrix.astype(BF16).astype(F32)
    low = matrix - high
    blank = jnp.zeros((matrix.shape[0], 8), F32)
    return jnp.concatenate([high, low, high, blank], axis=1).astype(BF16)


def odd_and_high(shape):
    quarter = lax.broadcasted_iota(jnp.int32, shape, 1) // QUARTER
    return quarter % 2 == 1, quarter >= 2


def turned(odd, high, rows):
    pairs = [jnp.where(odd, rows[(k + 1) % BLOCKS], rows[k]) for k in range(BLOCKS)]
    return [
        jnp.where(high, pairs[(2 - i) % BLOCKS], pairs[(-i) % BLOCKS]) for i in range(BLOCKS)
    ]


def lane_gather(values, index):
    numbers = lax.GatherDimensionNumbers(
        offset_dims=(),
        collapsed_slice_dims=(1,),
        start_index_map=(1,),
        operand_batching_dims=(0,),
        start_indices_batching_dims=(0,),
    )
    return lax.gather(
        values,
        index[:, :, None],
        dimension_numbers=numbers,
        slice_sizes=(1, 1),
        mode=lax.GatherScatterMode.PROMISE_IN_BOUNDS,
    )


def groups(count):
    return (count + BLOCKS - 1) // BLOCKS


def taylor_factors(clusters):
    factors = []
    for cluster in range(clusters):
        width = BASE_STEP * 2.0**cluster
        factor = 1.0
        row = []
        for order in range(NDER):
            factor = factor * width / (order + 1)
            row.append(factor)
        factors.append(row)
    return factors


def pairing_blocks(region):
    second = region // 2 % 2
    odd = region % 2
    return [3 * second, 1 + odd, 3 - 3 * second, 2 - odd]


def predict_kernel(
    state_hbm,
    stiff_hbm,
    star_hbm,
    send_hbm,
    sub_hbm,
    cluster_hbm,
    face_hbm,
    orient_hbm,
    region_index_ref,
    sub_index_ref,
    integral_hbm,
    table_hbm,
    region_hbm0,
    region_hbm1,
    region_hbm2,
    region_hbm3,
    within_hbm0,
    within_hbm1,
    within_hbm2,
    stiff_ref,
    star_ref,
    send_ref,
    sub_ref,
    cluster_ref,
    face_ref,
    orient_ref,
    series_ref,
    product_ref,
    integral_ref,
    table_ref,
    region_ref,
    within_ref,
    arrived,
    sent,
):
    region_hbms = (region_hbm0, region_hbm1, region_hbm2, region_hbm3)
    quants, modes, lanes = state_hbm.shape
    clusters = integral_hbm.shape[0]
    dims = stiff_hbm.shape[0]
    copies = [
        pltpu.make_async_copy(source, target, arrived.at[place])
        for place, (source, target) in enumerate(
            [
                (stiff_hbm, stiff_ref),
                (state_hbm, series_ref.at[0]),
                (star_hbm, star_ref),
                (send_hbm, send_ref),
                (sub_hbm, sub_ref),
                (cluster_hbm, cluster_ref),
                (face_hbm, face_ref),
                (orient_hbm, orient_ref),
            ]
        )
    ]
    for copy in copies:
        copy.start()
    copies[0].wait()
    stacked = jnp.concatenate([stiff_ref[d] for d in range(dims)], axis=0)
    lhs = split_columns(-stacked)
    copies[1].wait()
    block = 5
    blocks = [range(first, min(first + block, quants)) for first in range(0, quants, block)]

    def multiply(slot, rows, values):
        product = jnp.dot(
            lhs, split_rows(jnp.concatenate(values, axis=1)), preferred_element_type=F32
        )
        for place, row in enumerate(rows):
            product_ref[slot, row] = product[:, place * lanes : (place + 1) * lanes]

    for rows in blocks:
        multiply(0, rows, [series_ref[0, row] for row in rows])
    for copy in copies[2:]:
        copy.wait()
    for order in range(1, NDER):
        slot = (order - 1) % 2
        for rows in blocks:
            sums = [None for _ in rows]
            for column in range(quants):
                for d in range(dims):
                    value = product_ref[slot, column, pl.ds(d * modes, modes), :]
                    for place, row in enumerate(rows):
                        term = star_ref[row, column, pl.ds(d, 1), :] * value
                        sums[place] = term if sums[place] is None else sums[place] + term
            for place, row in enumerate(rows):
                series_ref[order, row] = sums[place]
            if order < NDER - 1:
                multiply(1 - slot, rows, sums)

    factors = taylor_factors(clusters)
    per_quant = modes // 8
    count = quants * per_quant
    odd, high = odd_and_high((8, lanes))
    lists = pairing_blocks(region_index_ref[0])
    index = []
    for cluster in range(clusters):
        base = jnp.concatenate(
            [send_ref[0, cluster, pl.ds(lists[s], 1), :] for s in range(BLOCKS)], axis=1
        )
        base = jnp.broadcast_to(base, (8, lanes))
        index.append([base] + [pltpu.roll(base, QUARTER * i, 1) for i in range(1, BLOCKS)])
    sub_slots = sub_ref.shape[2]
    blank = jnp.zeros((1, QUARTER - clusters * sub_slots), jnp.int32)
    row = jnp.concatenate([sub_ref[c] for c in range(clusters)] + [blank], axis=1)
    sub_index = jnp.broadcast_to(jnp.concatenate([row] * BLOCKS, axis=1), (8, lanes))
    owner = lax.broadcasted_iota(jnp.int32, (8, lanes), 1) % QUARTER // sub_slots
    chunk = 4
    leaving = []

    def leave(source, target):
        leaving.append(pltpu.make_async_copy(source, target, sent.at[len(leaving)]))
        leaving[-1].start()

    here = sub_index_ref[0]
    brought = pairing_blocks(region_index_ref[0])
    cluster_row = cluster_ref[...]
    for face in range(face_ref.shape[0]):
        entry = face_ref[pl.ds(face, 1), :]
        place = entry - lanes
        sub_place = place - BLOCKS * QUARTER
        block = place // QUARTER
        slot = sum(jnp.where(block == brought[p], p, 0) for p in range(BLOCKS))
        source = (sub_place // sub_slots) ^ here
        for i in range(BLOCKS):
            region = ((slot + i) & (BLOCKS - 1)) * QUARTER + (place & (QUARTER - 1))
            within = ((source + i) & (BLOCKS - 1)) * QUARTER + cluster_row * sub_slots
            within = within + (sub_place & (sub_slots - 1))
            table_ref[face, pl.ds(i, 1), :] = region & (lanes - 1)
            table_ref[face, pl.ds(BLOCKS + i, 1), :] = within & (lanes - 1)
        table_ref[face, pl.ds(2 * BLOCKS + 2, 1), :] = entry & (lanes - 1)
        table_ref[face, pl.ds(2 * BLOCKS + 3, 1), :] = cluster_row
        kind = jnp.where(place < 0, -1, jnp.where(sub_place < 0, cluster_row, clusters))
        table_ref[face, pl.ds(2 * BLOCKS, 1), :] = kind
        table_ref[face, pl.ds(2 * BLOCKS + 1, 1), :] = orient_ref[pl.ds(face, 1), :]
    leave(table_ref, table_hbm)

    for group in range(groups(count)):
        picked = [[] for _ in range(clusters)]
        shared = []
        for member in range(BLOCKS):
            at = group * BLOCKS + member
            if at >= count:
                for cluster in range(clusters):
                    picked[cluster].append(picked[cluster][-1])
                shared.append(shared[-1])
                continue
            quant, rows = at // per_quant, pl.ds(at % per_quant * 8, 8)
            series = [series_ref[order, quant, rows, :] for order in range(NDER)]
            for cluster in range(clusters):
                total = factors[cluster][0] * series[0]
                for order in range(1, NDER):
                    total = total + factors[cluster][order] * series[order]
                integral_ref[cluster, at] = total
                picked[cluster].append(lane_gather(total, index[cluster][member]))
                other = lane_gather(total, sub_index)
                within = other if cluster == 0 else jnp.where(owner == cluster, other, within)
            shared.append(within)
        for cluster in range(clusters):
            for b, packed in enumerate(turned(odd, high, picked[cluster])):
                region_ref[b, cluster, group] = packed
        for k, packed in enumerate(turned(odd, high, shared)):
            within_ref[(0, 2, 1, 3)[k], group] = packed
        if (group + 1) % chunk == 0:
            part = pl.ds(group + 1 - chunk, chunk)
            for b in range(BLOCKS):
                leave(region_ref.at[b, :, part], region_hbms[b].at[:, part])
            first = (group + 1 - chunk) * BLOCKS
            done = pl.ds(first, min(chunk * BLOCKS, count - first))
            leave(integral_ref.at[:, done], integral_hbm.at[:, done])
    leave(within_ref.at[pl.ds(2, 2)], within_hbm1)
    leave(within_ref.at[0], within_hbm0)
    leave(within_ref.at[pl.ds(1, 1)], within_hbm2)
    for copy in leaving:
        copy.wait()


def near_kernel(table_ref, integral_ref, partner_ref):
    clusters, quants, modes, lanes = integral_ref.shape
    chosen = jnp.broadcast_to(table_ref[0, pl.ds(2 * BLOCKS + 3, 1), :], (8, lanes))
    masks = [chosen == cluster for cluster in range(clusters)]

    def one_face(face, _):
        index = jnp.broadcast_to(table_ref[face, pl.ds(2 * BLOCKS + 2, 1), :], (8, lanes))
        for quant in range(quants):
            for first in range(0, modes, 8):
                rows = pl.ds(first, 8)
                total = lane_gather(integral_ref[0, quant, rows, :], index)
                for cluster in range(1, clusters):
                    other = lane_gather(integral_ref[cluster, quant, rows, :], index)
                    total = jnp.where(masks[cluster], other, total)
                partner_ref[face, quant, rows, :] = total
        return 0

    lax.fori_loop(0, table_ref.shape[0], one_face, 0)


def own_kernel(
    table_ref,
    volume_ref,
    local_ref,
    integral_ref,
    state_ref,
    star_ref,
    plus_ref,
    neighbour_ref,
    result_ref,
    flux_ref,
    lhs_ref,
    product_ref,
):
    quants, modes, lanes = state_ref.shape
    clusters = integral_ref.shape[0]
    dims = volume_ref.shape[0]
    faces, orients = neighbour_ref.shape[:2]
    chosen = jnp.broadcast_to(table_ref[0, pl.ds(2 * BLOCKS + 3, 1), :], (8, lanes))
    masks = [chosen == cluster for cluster in range(clusters)]

    stacked = jnp.concatenate(
        [volume_ref[d] for d in range(dims)] + [-local_ref[f] for f in range(faces)], axis=0
    )
    lhs_ref[...] = split_columns(stacked)
    for quant in range(quants):
        parts = []
        for first in range(0, modes, 8):
            rows = pl.ds(first, 8)
            own = integral_ref[0, quant, rows, :]
            for cluster in range(1, clusters):
                own = jnp.where(masks[cluster], integral_ref[cluster, quant, rows, :], own)
            parts.append(own)
        product_ref[quant] = jnp.dot(
            lhs_ref[...], split_rows(jnp.concatenate(parts, axis=0)), preferred_element_type=F32
        )

    def own_row(row, _):
        total = state_ref[row]
        for column in range(quants):
            for part in range(dims + faces):
                value = product_ref[column, pl.ds(part * modes, modes), :]
                if part < dims:
                    matrix = star_ref[row, column, pl.ds(part, 1), :]
                else:
                    matrix = plus_ref[row, column, pl.ds(part - dims, 1), :]
                total = total + matrix * value
        result_ref[row] = total
        return 0

    lax.fori_loop(0, quants, own_row, 0)

    def one_face(face, _):
        stack = jnp.concatenate([-neighbour_ref[face, o] for o in range(orients)], axis=0)
        flux_ref[face] = split_columns(stack)
        return 0

    lax.fori_loop(0, faces, one_face, 0)


def neighbour_kernel(
    region_refs,
    first_ref,
    beside_ref,
    across_ref,
    table_ref,
    near_ref,
    minus_ref,
    flux_ref,
    own_ref,
    result_ref,
    pool_ref,
    sub_pool_ref,
    partner_ref,
):
    quants, modes, lanes = own_ref.shape
    faces = flux_ref.shape[0]
    clusters = region_refs[0].shape[0]
    orients = flux_ref.shape[1] // modes
    per_quant = modes // 8
    count = quants * per_quant
    odd, high = odd_and_high((8, lanes))

    def spread(face, row):
        return jnp.broadcast_to(table_ref[face, pl.ds(row, 1), :], (8, lanes))

    def unpack(group):
        for cluster in range(clusters):
            pools = turned(odd, high, [region_refs[b][cluster, group] for b in range(BLOCKS)])
            for member, pool in enumerate(pools):
                if group * BLOCKS + member < count:
                    pool_ref[cluster, group * BLOCKS + member] = pool
        within = [first_ref[group], beside_ref[0, group], across_ref[0, group], across_ref[1, group]]
        pools = turned(odd, high, within)
        for member, pool in enumerate(pools):
            if group * BLOCKS + member < count:
                sub_pool_ref[group * BLOCKS + member] = pool

    def gather(face, ats):
        kind = spread(face, 2 * BLOCKS)
        hits = [kind == cluster for cluster in range(clusters + 1)]
        region_index = [spread(face, i) for i in range(BLOCKS)]
        sub_index = [spread(face, BLOCKS + i) for i in range(BLOCKS)]
        for at in ats:
            rows = pl.ds(at % per_quant * 8, 8)
            total = near_ref[face, at // per_quant, rows, :]
            for cluster in range(clusters):
                other = lane_gather(pool_ref[cluster, at], region_index[at % BLOCKS])
                total = jnp.where(hits[cluster], other, total)
            other = lane_gather(sub_pool_ref[at], sub_index[at % BLOCKS])
            partner_ref[face, at // per_quant, rows, :] = jnp.where(hits[clusters], other, total)

    block = 2
    blocks = [range(first, min(first + block, quants)) for first in range(0, quants, block)]

    def flux(face, rows):
        orient = spread(face, 2 * BLOCKS + 1)
        masks = [orient == o for o in range(orients)]
        mixed = [None for _ in rows]
        for column in range(quants):
            value = partner_ref[face, column]
            for place, row in enumerate(rows):
                term = minus_ref[row, column, pl.ds(face, 1), :] * value
                mixed[place] = term if mixed[place] is None else mixed[place] + term
        every = jnp.dot(
            flux_ref[face], split_rows(jnp.concatenate(mixed, axis=1)), preferred_element_type=F32
        )
        for place, row in enumerate(rows):
            for first in range(0, modes, 8):
                columns = slice(place * lanes, (place + 1) * lanes)
                total = every[first : first + 8, columns]
                for o in range(1, orients):
                    at = o * modes + first
                    total = jnp.where(masks[o], every[at : at + 8, columns], total)
                where = pl.ds(first, 8)
                if face == 0:
                    total = total + own_ref[row, where, :]
                else:
                    total = total + result_ref[row, where, :]
                result_ref[row, where, :] = total

    for group in range(groups(count)):
        unpack(group)
    gather(0, range(count))
    for face in range(faces):
        step = (count + len(blocks) - 1) // len(blocks)
        for place, rows in enumerate(blocks):
            flux(face, rows)
            if face + 1 < faces:
                gather(face + 1, range(place * step, min((place + 1) * step, count)))


def whole(count):
    return [pl.BlockSpec(memory_space=pltpu.VMEM) for _ in range(count)]


def far(count):
    return [pl.BlockSpec(memory_space=pltpu.HBM) for _ in range(count)]


def paired(value, axis, pairing):
    count = lax.axis_size(axis)
    pairs = []
    for source in range(count):
        offset = OFFSETS[pairing_blocks(source)[pairing]]
        pairs.append((source, (source + offset) % count))
    return lax.ppermute(value, axis, pairs)


def swapped(value, axis, bit):
    return lax.ppermute(value, axis, [(s, s ^ bit) for s in range(lax.axis_size(axis))])


def local(
    modal_state,
    deriv_stiff,
    volume_stiff,
    local_flux,
    neighbour_flux,
    star_matrices,
    plus_flux,
    minus_flux,
    cluster_ids,
    face_neighbours,
    face_orient,
    send_lists,
    sub_lists,
):
    quants, modes, lanes = modal_state.shape
    clusters = send_lists.shape[2]
    faces, orients = neighbour_flux.shape[:2]
    dims = deriv_stiff.shape[0]
    depth = 3 * modes + 8
    count = quants * modes // 8
    fours = groups(count)
    near_params = pltpu.CompilerParams(vmem_limit_bytes=40 * 1024 * 1024)
    params = pltpu.CompilerParams(vmem_limit_bytes=60 * 1024 * 1024)
    shape = jax.ShapeDtypeStruct
    stars, plus, minus = (
        jnp.transpose(matrix, (1, 2, 0, 3)) for matrix in (star_matrices, plus_flux, minus_flux)
    )
    sends = jnp.transpose(send_lists, (0, 2, 1, 3))
    subs = jnp.transpose(sub_lists, (1, 0, 2))

    here = lax.axis_index("sub").astype(jnp.int32).reshape(1)
    region = lax.axis_index("region").astype(jnp.int32).reshape(1)

    integrals, table, *packed = pl.pallas_call(
        predict_kernel,
        out_shape=(
            shape((clusters, count, 8, lanes), F32),
            shape((faces, 2 * BLOCKS + 8, lanes), jnp.int32),
            *[shape((clusters, fours, 8, lanes), F32)] * BLOCKS,
            shape((fours, 8, lanes), F32),
            shape((2, fours, 8, lanes), F32),
            shape((1, fours, 8, lanes), F32),
        ),
        in_specs=far(8) + [pl.BlockSpec(memory_space=pltpu.SMEM)] * 2,
        out_specs=tuple(far(5 + BLOCKS)),
        scratch_shapes=[
            pltpu.VMEM(deriv_stiff.shape, F32),
            pltpu.VMEM(stars.shape, F32),
            pltpu.VMEM(sends.shape, jnp.int32),
            pltpu.VMEM(subs.shape, jnp.int32),
            pltpu.VMEM((1, lanes), jnp.int32),
            pltpu.VMEM(face_neighbours.shape, jnp.int32),
            pltpu.VMEM(face_orient.shape, jnp.int32),
            pltpu.VMEM((NDER, quants, modes, lanes), F32),
            pltpu.VMEM((2, quants, dims * modes, lanes), F32),
            pltpu.VMEM((clusters, count, 8, lanes), F32),
            pltpu.VMEM((faces, 2 * BLOCKS + 8, lanes), jnp.int32),
            pltpu.VMEM((BLOCKS, clusters, fours, 8, lanes), F32),
            pltpu.VMEM((BLOCKS, fours, 8, lanes), F32),
            pltpu.SemaphoreType.DMA((8,)),
            pltpu.SemaphoreType.DMA((fours + 8,)),
        ],
        compiler_params=params,
        name="predict",
    )(
        modal_state,
        deriv_stiff,
        stars,
        sends,
        subs,
        cluster_ids.reshape(1, lanes),
        face_neighbours,
        face_orient,
        region,
        here,
    )

    arrived = [paired(packed[p], "region", p) for p in range(BLOCKS)]
    first, beside, across = packed[BLOCKS:]
    beside = swapped(beside, "sub", 1)
    across = swapped(jnp.concatenate([across, beside[1:]], axis=0), "sub", 2)
    integrals = integrals.reshape(clusters, quants, modes, lanes)
    near_partner = pl.pallas_call(
        near_kernel,
        out_shape=shape((faces, quants, modes, lanes), F32),
        in_specs=whole(2),
        out_specs=whole(1)[0],
        compiler_params=near_params,
        cost_estimate=pl.CostEstimate(
            flops=4_000_000_000, bytes_accessed=8_000_000, transcendentals=0
        ),
        name="near",
    )(table, integrals)

    own, flux = pl.pallas_call(
        own_kernel,
        out_shape=(
            shape((quants, modes, lanes), F32),
            shape((faces, orients * modes, depth), BF16),
        ),
        in_specs=whole(8),
        out_specs=tuple(whole(2)),
        scratch_shapes=[
            pltpu.VMEM(((dims + faces) * modes, depth), BF16),
            pltpu.VMEM((quants, (dims + faces) * modes, lanes), F32),
        ],
        compiler_params=near_params,
        cost_estimate=pl.CostEstimate(
            flops=4_000_000_000, bytes_accessed=8_000_000, transcendentals=0
        ),
        name="own",
    )(
        table,
        volume_stiff,
        local_flux,
        integrals,
        modal_state,
        stars,
        plus,
        neighbour_flux,
    )

    return pl.pallas_call(
        neighbour_kernel,
        out_shape=shape((quants, modes, lanes), F32),
        in_specs=[whole(BLOCKS), *whole(8)],
        out_specs=whole(1)[0],
        scratch_shapes=[
            pltpu.VMEM((clusters, count, 8, lanes), F32),
            pltpu.VMEM((count, 8, lanes), F32),
            pltpu.VMEM((faces, quants, modes, lanes), F32),
        ],
        compiler_params=near_params,
        name="neighbour",
    )(arrived, first, beside, across, table, near_partner, minus, flux, own)


def solution(mesh):
    return jax.shard_map(
        local,
        mesh=mesh,
        in_specs=(
            P(None, None, ("region", "sub")),
            P(),
            P(),
            P(),
            P(),
            P(None, None, None, ("region", "sub")),
            P(None, None, None, ("region", "sub")),
            P(None, None, None, ("region", "sub")),
            P(("region", "sub")),
            P(None, ("region", "sub")),
            P(None, ("region", "sub")),
            P(("region", "sub"), None, None, None),
            P(("region", "sub"), None, None),
        ),
        out_specs=P(None, None, ("region", "sub")),
        check_vma=False,
    )
```

```python
import jax
import jax.numpy as jnp
from jax import lax
from jax.experimental import pallas as pl
from jax.experimental.pallas import tpu as pltpu
from jax.sharding import PartitionSpec as P

NDER = 6
BASE_STEP = 0.25
OFFSETS = (-2, -1, 1, 2)
BLOCKS = 4
LANES = 128
QUARTER = 32
F32 = jnp.float32
BF16 = jnp.bfloat16


def split_rows(values):
    high = values.astype(BF16).astype(F32)
    low = values - high
    blank = jnp.zeros((8, values.shape[1]), F32)
    return jnp.concatenate([high, high, low, blank], axis=0).astype(BF16)


def split_columns(matrix):
    high = matrix.astype(BF16).astype(F32)
    low = matrix - high
    blank = jnp.zeros((matrix.shape[0], 8), F32)
    return jnp.concatenate([high, low, high, blank], axis=1).astype(BF16)


def odd_and_high(shape):
    quarter = lax.broadcasted_iota(jnp.int32, shape, 1) // QUARTER
    return quarter % 2 == 1, quarter >= 2


def turned(odd, high, rows):
    pairs = [jnp.where(odd, rows[(k + 1) % BLOCKS], rows[k]) for k in range(BLOCKS)]
    return [
        jnp.where(high, pairs[(2 - i) % BLOCKS], pairs[(-i) % BLOCKS]) for i in range(BLOCKS)
    ]


def lane_gather(values, index):
    numbers = lax.GatherDimensionNumbers(
        offset_dims=(),
        collapsed_slice_dims=(1,),
        start_index_map=(1,),
        operand_batching_dims=(0,),
        start_indices_batching_dims=(0,),
    )
    return lax.gather(
        values,
        index[:, :, None],
        dimension_numbers=numbers,
        slice_sizes=(1, 1),
        mode=lax.GatherScatterMode.PROMISE_IN_BOUNDS,
    )


def groups(count):
    return (count + BLOCKS - 1) // BLOCKS


def taylor_factors(clusters):
    factors = []
    for cluster in range(clusters):
        width = BASE_STEP * 2.0**cluster
        factor = 1.0
        row = []
        for order in range(NDER):
            factor = factor * width / (order + 1)
            row.append(factor)
        factors.append(row)
    return factors


def pairing_blocks(region):
    second = region // 2 % 2
    odd = region % 2
    return [3 * second, 1 + odd, 3 - 3 * second, 2 - odd]


def predict_kernel(
    state_hbm,
    stiff_hbm,
    star_hbm,
    send_hbm,
    sub_hbm,
    cluster_hbm,
    face_hbm,
    orient_hbm,
    region_index_ref,
    sub_index_ref,
    integral_hbm,
    table_hbm,
    region_hbm0,
    region_hbm1,
    region_hbm2,
    region_hbm3,
    within_hbm0,
    within_hbm1,
    within_hbm2,
    stiff_ref,
    star_ref,
    send_ref,
    sub_ref,
    cluster_ref,
    face_ref,
    orient_ref,
    series_ref,
    spread_ref,
    product_ref,
    integral_ref,
    table_ref,
    region_ref,
    within_ref,
    arrived,
    sent,
):
    region_hbms = (region_hbm0, region_hbm1, region_hbm2, region_hbm3)
    quants, modes, lanes = state_hbm.shape
    clusters = integral_hbm.shape[0]
    dims = stiff_hbm.shape[0]
    copies = [
        pltpu.make_async_copy(source, target, arrived.at[place])
        for place, (source, target) in enumerate(
            [
                (stiff_hbm, stiff_ref),
                (state_hbm, series_ref.at[0]),
                (star_hbm, star_ref),
                (send_hbm, send_ref),
                (sub_hbm, sub_ref),
                (cluster_hbm, cluster_ref),
                (face_hbm, face_ref),
                (orient_hbm, orient_ref),
            ]
        )
    ]
    for copy in copies:
        copy.start()
    copies[0].wait()
    stacked = jnp.concatenate([stiff_ref[d] for d in range(dims)], axis=0)
    lhs = split_columns(-stacked)
    copies[1].wait()
    factors = taylor_factors(clusters)
    per_quant = modes // 8
    count = quants * per_quant
    block = 5
    blocks = [range(first, min(first + block, quants)) for first in range(0, quants, block)]

    def multiply(slot, rows, values):
        product = jnp.dot(
            lhs, split_rows(jnp.concatenate(values, axis=1)), preferred_element_type=F32
        )
        for place, row in enumerate(rows):
            part = product[:, place * lanes : (place + 1) * lanes]
            product_ref[slot, row] = part.reshape(dims, per_quant, 8, lanes)

    for rows in blocks:
        multiply(0, rows, [series_ref[0, row] for row in rows])
    for copy in copies[2:]:
        copy.wait()
    for row in range(quants):
        for column in range(quants):
            for d in range(dims):
                spread_ref[row, column, d] = jnp.broadcast_to(
                    star_ref[row, column, pl.ds(d, 1), :], (8, lanes)
                )
    for order in range(1, NDER):
        slot = (order - 1) % 2
        for rows in blocks:
            sums = [None for _ in rows]
            for column in range(quants):
                for d in range(dims):
                    value = product_ref[slot, column, d]
                    for place, row in enumerate(rows):
                        term = spread_ref[row, column, d][None] * value
                        sums[place] = term if sums[place] is None else sums[place] + term
            if order < NDER - 1:
                multiply(1 - slot, rows, [total.reshape(modes, lanes) for total in sums])
            for place, row in enumerate(rows):
                for cluster in range(clusters):
                    term = factors[cluster][order] * sums[place]
                    if order == 1:
                        start = series_ref[0, row].reshape(per_quant, 8, lanes)
                        term = term + factors[cluster][0] * start
                    else:
                        term = term + integral_ref[cluster, pl.ds(row * per_quant, per_quant)]
                    integral_ref[cluster, pl.ds(row * per_quant, per_quant)] = term

    odd, high = odd_and_high((8, lanes))
    lists = pairing_blocks(region_index_ref[0])
    index = []
    for cluster in range(clusters):
        base = jnp.concatenate(
            [send_ref[0, cluster, pl.ds(lists[s], 1), :] for s in range(BLOCKS)], axis=1
        )
        base = jnp.broadcast_to(base, (8, lanes))
        index.append([base] + [pltpu.roll(base, QUARTER * i, 1) for i in range(1, BLOCKS)])
    sub_slots = sub_ref.shape[2]
    blank = jnp.zeros((1, QUARTER - clusters * sub_slots), jnp.int32)
    row = jnp.concatenate([sub_ref[c] for c in range(clusters)] + [blank], axis=1)
    sub_index = jnp.broadcast_to(jnp.concatenate([row] * BLOCKS, axis=1), (8, lanes))
    owner = lax.broadcasted_iota(jnp.int32, (8, lanes), 1) % QUARTER // sub_slots
    chunk = 4
    leaving = []

    def leave(source, target):
        leaving.append(pltpu.make_async_copy(source, target, sent.at[len(leaving)]))
        leaving[-1].start()

    here = sub_index_ref[0]
    brought = pairing_blocks(region_index_ref[0])
    cluster_row = cluster_ref[...]
    for face in range(face_ref.shape[0]):
        entry = face_ref[pl.ds(face, 1), :]
        place = entry - lanes
        sub_place = place - BLOCKS * QUARTER
        block = place // QUARTER
        slot = sum(jnp.where(block == brought[p], p, 0) for p in range(BLOCKS))
        source = (sub_place // sub_slots) ^ here
        for i in range(BLOCKS):
            region = ((slot + i) & (BLOCKS - 1)) * QUARTER + (place & (QUARTER - 1))
            within = ((source + i) & (BLOCKS - 1)) * QUARTER + cluster_row * sub_slots
            within = within + (sub_place & (sub_slots - 1))
            table_ref[face, pl.ds(i, 1), :] = region & (lanes - 1)
            table_ref[face, pl.ds(BLOCKS + i, 1), :] = within & (lanes - 1)
        table_ref[face, pl.ds(2 * BLOCKS + 2, 1), :] = entry & (lanes - 1)
        table_ref[face, pl.ds(2 * BLOCKS + 3, 1), :] = cluster_row
        kind = jnp.where(place < 0, -1, jnp.where(sub_place < 0, cluster_row, clusters))
        table_ref[face, pl.ds(2 * BLOCKS, 1), :] = kind
        table_ref[face, pl.ds(2 * BLOCKS + 1, 1), :] = orient_ref[pl.ds(face, 1), :]
    leave(table_ref, table_hbm)

    for group in range(groups(count)):
        picked = [[] for _ in range(clusters)]
        shared = []
        for member in range(BLOCKS):
            at = group * BLOCKS + member
            if at >= count:
                for cluster in range(clusters):
                    picked[cluster].append(picked[cluster][-1])
                shared.append(shared[-1])
                continue
            for cluster in range(clusters):
                total = integral_ref[cluster, at]
                picked[cluster].append(lane_gather(total, index[cluster][member]))
                other = lane_gather(total, sub_index)
                within = other if cluster == 0 else jnp.where(owner == cluster, other, within)
            shared.append(within)
        for cluster in range(clusters):
            for b, packed in enumerate(turned(odd, high, picked[cluster])):
                region_ref[b, cluster, group] = packed
        for k, packed in enumerate(turned(odd, high, shared)):
            within_ref[(0, 2, 1, 3)[k], group] = packed
        if (group + 1) % chunk == 0:
            part = pl.ds(group + 1 - chunk, chunk)
            for b in range(BLOCKS):
                leave(region_ref.at[b, :, part], region_hbms[b].at[:, part])
            first = (group + 1 - chunk) * BLOCKS
            done = pl.ds(first, min(chunk * BLOCKS, count - first))
            leave(integral_ref.at[:, done], integral_hbm.at[:, done])
    leave(within_ref.at[pl.ds(2, 2)], within_hbm1)
    leave(within_ref.at[0], within_hbm0)
    leave(within_ref.at[pl.ds(1, 1)], within_hbm2)
    for copy in leaving:
        copy.wait()


def near_kernel(table_ref, integral_ref, partner_ref):
    clusters, quants, modes, lanes = integral_ref.shape
    chosen = jnp.broadcast_to(table_ref[0, pl.ds(2 * BLOCKS + 3, 1), :], (8, lanes))
    masks = [chosen == cluster for cluster in range(clusters)]

    def one_face(face, _):
        index = jnp.broadcast_to(table_ref[face, pl.ds(2 * BLOCKS + 2, 1), :], (8, lanes))
        for quant in range(quants):
            for first in range(0, modes, 8):
                rows = pl.ds(first, 8)
                total = lane_gather(integral_ref[0, quant, rows, :], index)
                for cluster in range(1, clusters):
                    other = lane_gather(integral_ref[cluster, quant, rows, :], index)
                    total = jnp.where(masks[cluster], other, total)
                partner_ref[face, quant, rows, :] = total
        return 0

    lax.fori_loop(0, table_ref.shape[0], one_face, 0)


def own_kernel(
    table_ref,
    volume_ref,
    local_ref,
    integral_ref,
    state_ref,
    star_ref,
    plus_ref,
    minus_ref,
    neighbour_ref,
    result_ref,
    flux_ref,
    spread_ref,
    lhs_ref,
    product_ref,
):
    quants, modes, lanes = state_ref.shape
    clusters = integral_ref.shape[0]
    dims = volume_ref.shape[0]
    faces, orients = neighbour_ref.shape[:2]
    chosen = jnp.broadcast_to(table_ref[0, pl.ds(2 * BLOCKS + 3, 1), :], (8, lanes))
    masks = [chosen == cluster for cluster in range(clusters)]

    stacked = jnp.concatenate(
        [volume_ref[d] for d in range(dims)] + [-local_ref[f] for f in range(faces)], axis=0
    )
    lhs_ref[...] = split_columns(stacked)
    for quant in range(quants):
        parts = []
        for first in range(0, modes, 8):
            rows = pl.ds(first, 8)
            own = integral_ref[0, quant, rows, :]
            for cluster in range(1, clusters):
                own = jnp.where(masks[cluster], integral_ref[cluster, quant, rows, :], own)
            parts.append(own)
        product_ref[quant] = jnp.dot(
            lhs_ref[...], split_rows(jnp.concatenate(parts, axis=0)), preferred_element_type=F32
        )

    def own_row(row, _):
        total = state_ref[row]
        for column in range(quants):
            for part in range(dims + faces):
                value = product_ref[column, pl.ds(part * modes, modes), :]
                if part < dims:
                    matrix = star_ref[row, column, pl.ds(part, 1), :]
                else:
                    matrix = plus_ref[row, column, pl.ds(part - dims, 1), :]
                total = total + matrix * value
        result_ref[row] = total
        return 0

    lax.fori_loop(0, quants, own_row, 0)

    def one_face(face, _):
        for row in range(quants):
            for column in range(quants):
                spread_ref[face, row, column] = jnp.broadcast_to(
                    minus_ref[row, column, pl.ds(face, 1), :], (8, lanes)
                )
        stack = jnp.concatenate([-neighbour_ref[face, o] for o in range(orients)], axis=0)
        flux_ref[face] = split_columns(stack)
        return 0

    lax.fori_loop(0, faces, one_face, 0)


def neighbour_kernel(
    region_refs,
    first_ref,
    beside_ref,
    across_ref,
    table_ref,
    near_ref,
    minus_ref,
    flux_ref,
    own_ref,
    result_ref,
    pool_ref,
    sub_pool_ref,
    partner_ref,
):
    quants, modes, lanes = own_ref.shape
    faces = flux_ref.shape[0]
    clusters = region_refs[0].shape[0]
    orients = flux_ref.shape[1] // modes
    per_quant = modes // 8
    count = quants * per_quant
    odd, high = odd_and_high((8, lanes))

    def spread(face, row):
        return jnp.broadcast_to(table_ref[face, pl.ds(row, 1), :], (8, lanes))

    def unpack(group):
        for cluster in range(clusters):
            pools = turned(odd, high, [region_refs[b][cluster, group] for b in range(BLOCKS)])
            for member, pool in enumerate(pools):
                if group * BLOCKS + member < count:
                    pool_ref[cluster, group * BLOCKS + member] = pool
        within = [first_ref[group], beside_ref[0, group], across_ref[0, group], across_ref[1, group]]
        pools = turned(odd, high, within)
        for member, pool in enumerate(pools):
            if group * BLOCKS + member < count:
                sub_pool_ref[group * BLOCKS + member] = pool

    def gather(face, ats):
        kind = spread(face, 2 * BLOCKS)
        hits = [kind == cluster for cluster in range(clusters + 1)]
        region_index = [spread(face, i) for i in range(BLOCKS)]
        sub_index = [spread(face, BLOCKS + i) for i in range(BLOCKS)]
        for at in ats:
            rows = pl.ds(at % per_quant * 8, 8)
            total = near_ref[face, at // per_quant, rows, :]
            for cluster in range(clusters):
                other = lane_gather(pool_ref[cluster, at], region_index[at % BLOCKS])
                total = jnp.where(hits[cluster], other, total)
            other = lane_gather(sub_pool_ref[at], sub_index[at % BLOCKS])
            partner_ref[face, at // per_quant, rows, :] = jnp.where(hits[clusters], other, total)

    block = 2
    blocks = [range(first, min(first + block, quants)) for first in range(0, quants, block)]

    def flux(face, rows):
        orient = spread(face, 2 * BLOCKS + 1)
        masks = [orient == o for o in range(orients)]
        mixed = [None for _ in rows]
        for column in range(quants):
            value = partner_ref[face, column].reshape(per_quant, 8, lanes)
            for place, row in enumerate(rows):
                term = minus_ref[face, row, column][None] * value
                mixed[place] = term if mixed[place] is None else mixed[place] + term
        mixed = [total.reshape(modes, lanes) for total in mixed]
        every = jnp.dot(
            flux_ref[face], split_rows(jnp.concatenate(mixed, axis=1)), preferred_element_type=F32
        )
        for place, row in enumerate(rows):
            for first in range(0, modes, 8):
                columns = slice(place * lanes, (place + 1) * lanes)
                total = every[first : first + 8, columns]
                for o in range(1, orients):
                    at = o * modes + first
                    total = jnp.where(masks[o], every[at : at + 8, columns], total)
                where = pl.ds(first, 8)
                if face == 0:
                    total = total + own_ref[row, where, :]
                else:
                    total = total + result_ref[row, where, :]
                result_ref[row, where, :] = total

    for group in range(groups(count)):
        unpack(group)
    gather(0, range(count))
    for face in range(faces):
        step = (count + len(blocks) - 1) // len(blocks)
        for place, rows in enumerate(blocks):
            flux(face, rows)
            if face + 1 < faces:
                gather(face + 1, range(place * step, min((place + 1) * step, count)))


def whole(count):
    return [pl.BlockSpec(memory_space=pltpu.VMEM) for _ in range(count)]


def far(count):
    return [pl.BlockSpec(memory_space=pltpu.HBM) for _ in range(count)]


def paired(value, axis, pairing):
    count = lax.axis_size(axis)
    pairs = []
    for source in range(count):
        offset = OFFSETS[pairing_blocks(source)[pairing]]
        pairs.append((source, (source + offset) % count))
    return lax.ppermute(value, axis, pairs)


def swapped(value, axis, bit):
    return lax.ppermute(value, axis, [(s, s ^ bit) for s in range(lax.axis_size(axis))])


def local(
    modal_state,
    deriv_stiff,
    volume_stiff,
    local_flux,
    neighbour_flux,
    star_matrices,
    plus_flux,
    minus_flux,
    cluster_ids,
    face_neighbours,
    face_orient,
    send_lists,
    sub_lists,
):
    quants, modes, lanes = modal_state.shape
    clusters = send_lists.shape[2]
    faces, orients = neighbour_flux.shape[:2]
    dims = deriv_stiff.shape[0]
    depth = 3 * modes + 8
    count = quants * modes // 8
    fours = groups(count)
    near_params = pltpu.CompilerParams(vmem_limit_bytes=40 * 1024 * 1024)
    params = pltpu.CompilerParams(vmem_limit_bytes=60 * 1024 * 1024)
    shape = jax.ShapeDtypeStruct
    stars, plus, minus = (
        jnp.transpose(matrix, (1, 2, 0, 3)) for matrix in (star_matrices, plus_flux, minus_flux)
    )
    sends = jnp.transpose(send_lists, (0, 2, 1, 3))
    subs = jnp.transpose(sub_lists, (1, 0, 2))

    here = lax.axis_index("sub").astype(jnp.int32).reshape(1)
    region = lax.axis_index("region").astype(jnp.int32).reshape(1)

    integrals, table, *packed = pl.pallas_call(
        predict_kernel,
        out_shape=(
            shape((clusters, count, 8, lanes), F32),
            shape((faces, 2 * BLOCKS + 8, lanes), jnp.int32),
            *[shape((clusters, fours, 8, lanes), F32)] * BLOCKS,
            shape((fours, 8, lanes), F32),
            shape((2, fours, 8, lanes), F32),
            shape((1, fours, 8, lanes), F32),
        ),
        in_specs=far(8) + [pl.BlockSpec(memory_space=pltpu.SMEM)] * 2,
        out_specs=tuple(far(5 + BLOCKS)),
        scratch_shapes=[
            pltpu.VMEM(deriv_stiff.shape, F32),
            pltpu.VMEM(stars.shape, F32),
            pltpu.VMEM(sends.shape, jnp.int32),
            pltpu.VMEM(subs.shape, jnp.int32),
            pltpu.VMEM((1, lanes), jnp.int32),
            pltpu.VMEM(face_neighbours.shape, jnp.int32),
            pltpu.VMEM(face_orient.shape, jnp.int32),
            pltpu.VMEM((1, quants, modes, lanes), F32),
            pltpu.VMEM((quants, quants, dims, 8, lanes), F32),
            pltpu.VMEM((2, quants, dims, modes // 8, 8, lanes), F32),
            pltpu.VMEM((clusters, count, 8, lanes), F32),
            pltpu.VMEM((faces, 2 * BLOCKS + 8, lanes), jnp.int32),
            pltpu.VMEM((BLOCKS, clusters, fours, 8, lanes), F32),
            pltpu.VMEM((BLOCKS, fours, 8, lanes), F32),
            pltpu.SemaphoreType.DMA((8,)),
            pltpu.SemaphoreType.DMA((fours + 8,)),
        ],
        compiler_params=params,
        name="predict",
    )(
        modal_state,
        deriv_stiff,
        stars,
        sends,
        subs,
        cluster_ids.reshape(1, lanes),
        face_neighbours,
        face_orient,
        region,
        here,
    )

    arrived = [paired(packed[p], "region", p) for p in range(BLOCKS)]
    first, beside, across = packed[BLOCKS:]
    beside = swapped(beside, "sub", 1)
    across = swapped(jnp.concatenate([across, beside[1:]], axis=0), "sub", 2)
    integrals = integrals.reshape(clusters, quants, modes, lanes)
    near_partner = pl.pallas_call(
        near_kernel,
        out_shape=shape((faces, quants, modes, lanes), F32),
        in_specs=whole(2),
        out_specs=whole(1)[0],
        compiler_params=near_params,
        cost_estimate=pl.CostEstimate(
            flops=4_000_000_000, bytes_accessed=8_000_000, transcendentals=0
        ),
        name="near",
    )(table, integrals)

    own, flux, minus_spread = pl.pallas_call(
        own_kernel,
        out_shape=(
            shape((quants, modes, lanes), F32),
            shape((faces, orients * modes, depth), BF16),
            shape((faces, quants, quants, 8, lanes), F32),
        ),
        in_specs=whole(9),
        out_specs=tuple(whole(3)),
        scratch_shapes=[
            pltpu.VMEM(((dims + faces) * modes, depth), BF16),
            pltpu.VMEM((quants, (dims + faces) * modes, lanes), F32),
        ],
        compiler_params=near_params,
        cost_estimate=pl.CostEstimate(
            flops=4_000_000_000, bytes_accessed=8_000_000, transcendentals=0
        ),
        name="own",
    )(
        table,
        volume_stiff,
        local_flux,
        integrals,
        modal_state,
        stars,
        plus,
        minus,
        neighbour_flux,
    )

    return pl.pallas_call(
        neighbour_kernel,
        out_shape=shape((quants, modes, lanes), F32),
        in_specs=[whole(BLOCKS), *whole(8)],
        out_specs=whole(1)[0],
        scratch_shapes=[
            pltpu.VMEM((clusters, count, 8, lanes), F32),
            pltpu.VMEM((count, 8, lanes), F32),
            pltpu.VMEM((faces, quants, modes, lanes), F32),
        ],
        compiler_params=near_params,
        name="neighbour",
    )(arrived, first, beside, across, table, near_partner, minus_spread, flux, own)


def solution(mesh):
    return jax.shard_map(
        local,
        mesh=mesh,
        in_specs=(
            P(None, None, ("region", "sub")),
            P(),
            P(),
            P(),
            P(),
            P(None, None, None, ("region", "sub")),
            P(None, None, None, ("region", "sub")),
            P(None, None, None, ("region", "sub")),
            P(("region", "sub")),
            P(None, ("region", "sub")),
            P(None, ("region", "sub")),
            P(("region", "sub"), None, None, None),
            P(("region", "sub"), None, None),
        ),
        out_specs=P(None, None, ("region", "sub")),
        check_vma=False,
    )
```

```python
import jax
import jax.numpy as jnp
from jax import lax
from jax.experimental import pallas as pl
from jax.experimental.pallas import tpu as pltpu
from jax.sharding import PartitionSpec as P

NDER = 6
BASE_STEP = 0.25
OFFSETS = (-2, -1, 1, 2)
BLOCKS = 4
LANES = 128
QUARTER = 32
F32 = jnp.float32
BF16 = jnp.bfloat16


def split_rows(values):
    high = values.astype(BF16).astype(F32)
    low = values - high
    blank = jnp.zeros((8, values.shape[1]), F32)
    return jnp.concatenate([high, high, low, blank], axis=0).astype(BF16)


def split_columns(matrix):
    high = matrix.astype(BF16).astype(F32)
    low = matrix - high
    blank = jnp.zeros((matrix.shape[0], 8), F32)
    return jnp.concatenate([high, low, high, blank], axis=1).astype(BF16)


def odd_and_high(shape):
    quarter = lax.broadcasted_iota(jnp.int32, shape, 1) // QUARTER
    return quarter % 2 == 1, quarter >= 2


def turned(odd, high, rows):
    pairs = [jnp.where(odd, rows[(k + 1) % BLOCKS], rows[k]) for k in range(BLOCKS)]
    return [
        jnp.where(high, pairs[(2 - i) % BLOCKS], pairs[(-i) % BLOCKS]) for i in range(BLOCKS)
    ]


def lane_gather(values, index):
    numbers = lax.GatherDimensionNumbers(
        offset_dims=(),
        collapsed_slice_dims=(1,),
        start_index_map=(1,),
        operand_batching_dims=(0,),
        start_indices_batching_dims=(0,),
    )
    return lax.gather(
        values,
        index[:, :, None],
        dimension_numbers=numbers,
        slice_sizes=(1, 1),
        mode=lax.GatherScatterMode.PROMISE_IN_BOUNDS,
    )


def groups(count):
    return (count + BLOCKS - 1) // BLOCKS


def taylor_factors(clusters):
    factors = []
    for cluster in range(clusters):
        width = BASE_STEP * 2.0**cluster
        factor = 1.0
        row = []
        for order in range(NDER):
            factor = factor * width / (order + 1)
            row.append(factor)
        factors.append(row)
    return factors


def pairing_blocks(region):
    half = region // 4 % 2
    second = region // 2 % 2
    odd = region % 2
    near, beside = 3 - 3 * second, 2 - odd
    turn = half * (beside - near)
    return [near + turn, 3 * second, 1 + odd, beside - turn]


def predict_kernel(
    state_hbm,
    stiff_hbm,
    star_hbm,
    send_hbm,
    sub_hbm,
    cluster_hbm,
    face_hbm,
    orient_hbm,
    region_index_ref,
    sub_index_ref,
    integral_hbm,
    table_hbm,
    region_hbm0,
    region_hbm1,
    region_hbm2,
    region_hbm3,
    within_hbm0,
    within_hbm1,
    within_hbm2,
    stiff_ref,
    star_ref,
    send_ref,
    sub_ref,
    cluster_ref,
    face_ref,
    orient_ref,
    series_ref,
    product_ref,
    integral_ref,
    table_ref,
    region_ref,
    within_ref,
    arrived,
    sent,
):
    region_hbms = (region_hbm0, region_hbm1, region_hbm2, region_hbm3)
    quants, modes, lanes = state_hbm.shape
    clusters = integral_hbm.shape[0]
    dims = stiff_hbm.shape[0]
    copies = [
        pltpu.make_async_copy(source, target, arrived.at[place])
        for place, (source, target) in enumerate(
            [
                (stiff_hbm, stiff_ref),
                (state_hbm, series_ref.at[0]),
                (star_hbm, star_ref),
                (send_hbm, send_ref),
                (sub_hbm, sub_ref),
                (cluster_hbm, cluster_ref),
                (face_hbm, face_ref),
                (orient_hbm, orient_ref),
            ]
        )
    ]
    for copy in copies:
        copy.start()
    copies[0].wait()
    stacked = jnp.concatenate([stiff_ref[d] for d in range(dims)], axis=0)
    lhs = split_columns(-stacked)
    copies[1].wait()
    block = 5
    blocks = [range(first, min(first + block, quants)) for first in range(0, quants, block)]

    def multiply(slot, rows, values):
        product = jnp.dot(
            lhs, split_rows(jnp.concatenate(values, axis=1)), preferred_element_type=F32
        )
        for place, row in enumerate(rows):
            product_ref[slot, row] = product[:, place * lanes : (place + 1) * lanes]

    for rows in blocks:
        multiply(0, rows, [series_ref[0, row] for row in rows])
    for copy in copies[2:]:
        copy.wait()
    for order in range(1, NDER):
        slot = (order - 1) % 2
        for rows in blocks:
            sums = [None for _ in rows]
            for column in range(quants):
                for d in range(dims):
                    value = product_ref[slot, column, pl.ds(d * modes, modes), :]
                    for place, row in enumerate(rows):
                        term = star_ref[row, column, pl.ds(d, 1), :] * value
                        sums[place] = term if sums[place] is None else sums[place] + term
            for place, row in enumerate(rows):
                series_ref[order, row] = sums[place]
            if order < NDER - 1:
                multiply(1 - slot, rows, sums)

    factors = taylor_factors(clusters)
    per_quant = modes // 8
    count = quants * per_quant
    odd, high = odd_and_high((8, lanes))
    lists = pairing_blocks(region_index_ref[0])
    index = []
    for cluster in range(clusters):
        base = jnp.concatenate(
            [send_ref[0, cluster, pl.ds(lists[s], 1), :] for s in range(BLOCKS)], axis=1
        )
        base = jnp.broadcast_to(base, (8, lanes))
        index.append([base] + [pltpu.roll(base, QUARTER * i, 1) for i in range(1, BLOCKS)])
    sub_slots = sub_ref.shape[2]
    blank = jnp.zeros((1, QUARTER - clusters * sub_slots), jnp.int32)
    row = jnp.concatenate([sub_ref[c] for c in range(clusters)] + [blank], axis=1)
    sub_index = jnp.broadcast_to(jnp.concatenate([row] * BLOCKS, axis=1), (8, lanes))
    owner = lax.broadcasted_iota(jnp.int32, (8, lanes), 1) % QUARTER // sub_slots
    chunk = 4
    leaving = []

    def leave(source, target):
        leaving.append(pltpu.make_async_copy(source, target, sent.at[len(leaving)]))
        leaving[-1].start()

    here = sub_index_ref[0]
    brought = pairing_blocks(region_index_ref[0])
    cluster_row = cluster_ref[...]
    for face in range(face_ref.shape[0]):
        entry = face_ref[pl.ds(face, 1), :]
        place = entry - lanes
        sub_place = place - BLOCKS * QUARTER
        block = place // QUARTER
        slot = sum(jnp.where(block == brought[p], p, 0) for p in range(BLOCKS))
        source = (sub_place // sub_slots) ^ here
        for i in range(BLOCKS):
            region = ((slot + i) & (BLOCKS - 1)) * QUARTER + (place & (QUARTER - 1))
            within = ((source + i) & (BLOCKS - 1)) * QUARTER + cluster_row * sub_slots
            within = within + (sub_place & (sub_slots - 1))
            table_ref[face, pl.ds(i, 1), :] = region & (lanes - 1)
            table_ref[face, pl.ds(BLOCKS + i, 1), :] = within & (lanes - 1)
        table_ref[face, pl.ds(2 * BLOCKS + 2, 1), :] = entry & (lanes - 1)
        table_ref[face, pl.ds(2 * BLOCKS + 3, 1), :] = cluster_row
        kind = jnp.where(place < 0, -1, jnp.where(sub_place < 0, cluster_row, clusters))
        table_ref[face, pl.ds(2 * BLOCKS, 1), :] = kind
        table_ref[face, pl.ds(2 * BLOCKS + 1, 1), :] = orient_ref[pl.ds(face, 1), :]
    leave(table_ref, table_hbm)

    for group in range(groups(count)):
        picked = [[] for _ in range(clusters)]
        shared = []
        for member in range(BLOCKS):
            at = group * BLOCKS + member
            if at >= count:
                for cluster in range(clusters):
                    picked[cluster].append(picked[cluster][-1])
                shared.append(shared[-1])
                continue
            quant, rows = at // per_quant, pl.ds(at % per_quant * 8, 8)
            series = [series_ref[order, quant, rows, :] for order in range(NDER)]
            for cluster in range(clusters):
                total = factors[cluster][0] * series[0]
                for order in range(1, NDER):
                    total = total + factors[cluster][order] * series[order]
                integral_ref[cluster, at] = total
                picked[cluster].append(lane_gather(total, index[cluster][member]))
                other = lane_gather(total, sub_index)
                within = other if cluster == 0 else jnp.where(owner == cluster, other, within)
            shared.append(within)
        for cluster in range(clusters):
            for b, packed in enumerate(turned(odd, high, picked[cluster])):
                region_ref[b, cluster, group] = packed
        for k, packed in enumerate(turned(odd, high, shared)):
            within_ref[(0, 2, 1, 3)[k], group] = packed
        if (group + 1) % chunk == 0:
            part = pl.ds(group + 1 - chunk, chunk)
            for b in range(BLOCKS):
                leave(region_ref.at[b, :, part], region_hbms[b].at[:, part])
            first = (group + 1 - chunk) * BLOCKS
            done = pl.ds(first, min(chunk * BLOCKS, count - first))
            leave(integral_ref.at[:, done], integral_hbm.at[:, done])
    leave(within_ref.at[pl.ds(2, 2)], within_hbm1)
    leave(within_ref.at[0], within_hbm0)
    leave(within_ref.at[pl.ds(1, 1)], within_hbm2)
    for copy in leaving:
        copy.wait()


def near_kernel(table_ref, integral_ref, partner_ref):
    clusters, quants, modes, lanes = integral_ref.shape
    chosen = jnp.broadcast_to(table_ref[0, pl.ds(2 * BLOCKS + 3, 1), :], (8, lanes))
    masks = [chosen == cluster for cluster in range(clusters)]

    def one_face(face, _):
        index = jnp.broadcast_to(table_ref[face, pl.ds(2 * BLOCKS + 2, 1), :], (8, lanes))
        for quant in range(quants):
            for first in range(0, modes, 8):
                rows = pl.ds(first, 8)
                total = lane_gather(integral_ref[0, quant, rows, :], index)
                for cluster in range(1, clusters):
                    other = lane_gather(integral_ref[cluster, quant, rows, :], index)
                    total = jnp.where(masks[cluster], other, total)
                partner_ref[face, quant, rows, :] = total
        return 0

    lax.fori_loop(0, table_ref.shape[0], one_face, 0)


def own_kernel(
    table_ref,
    volume_ref,
    local_ref,
    integral_ref,
    state_ref,
    star_ref,
    plus_ref,
    neighbour_ref,
    result_ref,
    flux_ref,
    lhs_ref,
    product_ref,
):
    quants, modes, lanes = state_ref.shape
    clusters = integral_ref.shape[0]
    dims = volume_ref.shape[0]
    faces, orients = neighbour_ref.shape[:2]
    chosen = jnp.broadcast_to(table_ref[0, pl.ds(2 * BLOCKS + 3, 1), :], (8, lanes))
    masks = [chosen == cluster for cluster in range(clusters)]

    stacked = jnp.concatenate(
        [volume_ref[d] for d in range(dims)] + [-local_ref[f] for f in range(faces)], axis=0
    )
    lhs_ref[...] = split_columns(stacked)
    for quant in range(quants):
        parts = []
        for first in range(0, modes, 8):
            rows = pl.ds(first, 8)
            own = integral_ref[0, quant, rows, :]
            for cluster in range(1, clusters):
                own = jnp.where(masks[cluster], integral_ref[cluster, quant, rows, :], own)
            parts.append(own)
        product_ref[quant] = jnp.dot(
            lhs_ref[...], split_rows(jnp.concatenate(parts, axis=0)), preferred_element_type=F32
        )

    def own_row(row, _):
        total = state_ref[row]
        for column in range(quants):
            for part in range(dims + faces):
                value = product_ref[column, pl.ds(part * modes, modes), :]
                if part < dims:
                    matrix = star_ref[row, column, pl.ds(part, 1), :]
                else:
                    matrix = plus_ref[row, column, pl.ds(part - dims, 1), :]
                total = total + matrix * value
        result_ref[row] = total
        return 0

    lax.fori_loop(0, quants, own_row, 0)

    def one_face(face, _):
        stack = jnp.concatenate([-neighbour_ref[face, o] for o in range(orients)], axis=0)
        flux_ref[face] = split_columns(stack)
        return 0

    lax.fori_loop(0, faces, one_face, 0)


def neighbour_kernel(
    region_refs,
    first_ref,
    beside_ref,
    across_ref,
    table_ref,
    near_ref,
    minus_ref,
    flux_ref,
    own_ref,
    result_ref,
    pool_ref,
    sub_pool_ref,
    partner_ref,
):
    quants, modes, lanes = own_ref.shape
    faces = flux_ref.shape[0]
    clusters = region_refs[0].shape[0]
    orients = flux_ref.shape[1] // modes
    per_quant = modes // 8
    count = quants * per_quant
    odd, high = odd_and_high((8, lanes))

    def spread(face, row):
        return jnp.broadcast_to(table_ref[face, pl.ds(row, 1), :], (8, lanes))

    def unpack(group):
        for cluster in range(clusters):
            pools = turned(odd, high, [region_refs[b][cluster, group] for b in range(BLOCKS)])
            for member, pool in enumerate(pools):
                if group * BLOCKS + member < count:
                    pool_ref[cluster, group * BLOCKS + member] = pool
        within = [first_ref[group], beside_ref[0, group], across_ref[0, group], across_ref[1, group]]
        pools = turned(odd, high, within)
        for member, pool in enumerate(pools):
            if group * BLOCKS + member < count:
                sub_pool_ref[group * BLOCKS + member] = pool

    def gather(face, ats):
        kind = spread(face, 2 * BLOCKS)
        hits = [kind == cluster for cluster in range(clusters + 1)]
        region_index = [spread(face, i) for i in range(BLOCKS)]
        sub_index = [spread(face, BLOCKS + i) for i in range(BLOCKS)]
        for at in ats:
            rows = pl.ds(at % per_quant * 8, 8)
            total = near_ref[face, at // per_quant, rows, :]
            for cluster in range(clusters):
                other = lane_gather(pool_ref[cluster, at], region_index[at % BLOCKS])
                total = jnp.where(hits[cluster], other, total)
            other = lane_gather(sub_pool_ref[at], sub_index[at % BLOCKS])
            partner_ref[face, at // per_quant, rows, :] = jnp.where(hits[clusters], other, total)

    block = 2
    blocks = [range(first, min(first + block, quants)) for first in range(0, quants, block)]

    def flux(face, rows):
        orient = spread(face, 2 * BLOCKS + 1)
        masks = [orient == o for o in range(orients)]
        mixed = [None for _ in rows]
        for column in range(quants):
            value = partner_ref[face, column]
            for place, row in enumerate(rows):
                term = minus_ref[row, column, pl.ds(face, 1), :] * value
                mixed[place] = term if mixed[place] is None else mixed[place] + term
        every = jnp.dot(
            flux_ref[face], split_rows(jnp.concatenate(mixed, axis=1)), preferred_element_type=F32
        )
        for place, row in enumerate(rows):
            for first in range(0, modes, 8):
                columns = slice(place * lanes, (place + 1) * lanes)
                total = every[first : first + 8, columns]
                for o in range(1, orients):
                    at = o * modes + first
                    total = jnp.where(masks[o], every[at : at + 8, columns], total)
                where = pl.ds(first, 8)
                if face == 0:
                    total = total + own_ref[row, where, :]
                else:
                    total = total + result_ref[row, where, :]
                result_ref[row, where, :] = total

    for group in range(groups(count)):
        unpack(group)
    gather(0, range(count))
    for face in range(faces):
        step = (count + len(blocks) - 1) // len(blocks)
        for place, rows in enumerate(blocks):
            flux(face, rows)
            if face + 1 < faces:
                gather(face + 1, range(place * step, min((place + 1) * step, count)))


def whole(count):
    return [pl.BlockSpec(memory_space=pltpu.VMEM) for _ in range(count)]


def far(count):
    return [pl.BlockSpec(memory_space=pltpu.HBM) for _ in range(count)]


def paired(value, axis, pairing):
    count = lax.axis_size(axis)
    pairs = []
    for source in range(count):
        offset = OFFSETS[pairing_blocks(source)[pairing]]
        pairs.append((source, (source + offset) % count))
    return lax.ppermute(value, axis, pairs)


def swapped(value, axis, bit):
    return lax.ppermute(value, axis, [(s, s ^ bit) for s in range(lax.axis_size(axis))])


def local(
    modal_state,
    deriv_stiff,
    volume_stiff,
    local_flux,
    neighbour_flux,
    star_matrices,
    plus_flux,
    minus_flux,
    cluster_ids,
    face_neighbours,
    face_orient,
    send_lists,
    sub_lists,
):
    quants, modes, lanes = modal_state.shape
    clusters = send_lists.shape[2]
    faces, orients = neighbour_flux.shape[:2]
    dims = deriv_stiff.shape[0]
    depth = 3 * modes + 8
    count = quants * modes // 8
    fours = groups(count)
    near_params = pltpu.CompilerParams(vmem_limit_bytes=40 * 1024 * 1024)
    params = pltpu.CompilerParams(vmem_limit_bytes=60 * 1024 * 1024)
    shape = jax.ShapeDtypeStruct
    stars, plus, minus = (
        jnp.transpose(matrix, (1, 2, 0, 3)) for matrix in (star_matrices, plus_flux, minus_flux)
    )
    sends = jnp.transpose(send_lists, (0, 2, 1, 3))
    subs = jnp.transpose(sub_lists, (1, 0, 2))

    here = lax.axis_index("sub").astype(jnp.int32).reshape(1)
    region = lax.axis_index("region").astype(jnp.int32).reshape(1)

    integrals, table, *packed = pl.pallas_call(
        predict_kernel,
        out_shape=(
            shape((clusters, count, 8, lanes), F32),
            shape((faces, 2 * BLOCKS + 8, lanes), jnp.int32),
            *[shape((clusters, fours, 8, lanes), F32)] * BLOCKS,
            shape((fours, 8, lanes), F32),
            shape((2, fours, 8, lanes), F32),
            shape((1, fours, 8, lanes), F32),
        ),
        in_specs=far(8) + [pl.BlockSpec(memory_space=pltpu.SMEM)] * 2,
        out_specs=tuple(far(5 + BLOCKS)),
        scratch_shapes=[
            pltpu.VMEM(deriv_stiff.shape, F32),
            pltpu.VMEM(stars.shape, F32),
            pltpu.VMEM(sends.shape, jnp.int32),
            pltpu.VMEM(subs.shape, jnp.int32),
            pltpu.VMEM((1, lanes), jnp.int32),
            pltpu.VMEM(face_neighbours.shape, jnp.int32),
            pltpu.VMEM(face_orient.shape, jnp.int32),
            pltpu.VMEM((NDER, quants, modes, lanes), F32),
            pltpu.VMEM((2, quants, dims * modes, lanes), F32),
            pltpu.VMEM((clusters, count, 8, lanes), F32),
            pltpu.VMEM((faces, 2 * BLOCKS + 8, lanes), jnp.int32),
            pltpu.VMEM((BLOCKS, clusters, fours, 8, lanes), F32),
            pltpu.VMEM((BLOCKS, fours, 8, lanes), F32),
            pltpu.SemaphoreType.DMA((8,)),
            pltpu.SemaphoreType.DMA((fours + 8,)),
        ],
        compiler_params=params,
        name="predict",
    )(
        modal_state,
        deriv_stiff,
        stars,
        sends,
        subs,
        cluster_ids.reshape(1, lanes),
        face_neighbours,
        face_orient,
        region,
        here,
    )

    arrived = [paired(packed[p], "region", p) for p in range(BLOCKS)]
    first, beside, across = packed[BLOCKS:]
    beside = swapped(beside, "sub", 1)
    across = swapped(jnp.concatenate([across, beside[1:]], axis=0), "sub", 2)
    integrals = integrals.reshape(clusters, quants, modes, lanes)
    near_partner = pl.pallas_call(
        near_kernel,
        out_shape=shape((faces, quants, modes, lanes), F32),
        in_specs=whole(2),
        out_specs=whole(1)[0],
        compiler_params=near_params,
        cost_estimate=pl.CostEstimate(
            flops=4_000_000_000, bytes_accessed=8_000_000, transcendentals=0
        ),
        name="near",
    )(table, integrals)

    own, flux = pl.pallas_call(
        own_kernel,
        out_shape=(
            shape((quants, modes, lanes), F32),
            shape((faces, orients * modes, depth), BF16),
        ),
        in_specs=whole(8),
        out_specs=tuple(whole(2)),
        scratch_shapes=[
            pltpu.VMEM(((dims + faces) * modes, depth), BF16),
            pltpu.VMEM((quants, (dims + faces) * modes, lanes), F32),
        ],
        compiler_params=near_params,
        cost_estimate=pl.CostEstimate(
            flops=4_000_000_000, bytes_accessed=8_000_000, transcendentals=0
        ),
        name="own",
    )(
        table,
        volume_stiff,
        local_flux,
        integrals,
        modal_state,
        stars,
        plus,
        neighbour_flux,
    )

    return pl.pallas_call(
        neighbour_kernel,
        out_shape=shape((quants, modes, lanes), F32),
        in_specs=[whole(BLOCKS), *whole(8)],
        out_specs=whole(1)[0],
        scratch_shapes=[
            pltpu.VMEM((clusters, count, 8, lanes), F32),
            pltpu.VMEM((count, 8, lanes), F32),
            pltpu.VMEM((faces, quants, modes, lanes), F32),
        ],
        compiler_params=near_params,
        name="neighbour",
    )(arrived, first, beside, across, table, near_partner, minus, flux, own)


def solution(mesh):
    return jax.shard_map(
        local,
        mesh=mesh,
        in_specs=(
            P(None, None, ("region", "sub")),
            P(),
            P(),
            P(),
            P(),
            P(None, None, None, ("region", "sub")),
            P(None, None, None, ("region", "sub")),
            P(None, None, None, ("region", "sub")),
            P(("region", "sub")),
            P(None, ("region", "sub")),
            P(None, ("region", "sub")),
            P(("region", "sub"), None, None, None),
            P(("region", "sub"), None, None),
        ),
        out_specs=P(None, None, ("region", "sub")),
        check_vma=False,
    )
```

```python
import jax
import jax.numpy as jnp
from jax import lax
from jax.experimental import pallas as pl
from jax.experimental.pallas import tpu as pltpu
from jax.sharding import PartitionSpec as P

NDER = 6
BASE_STEP = 0.25
OFFSETS = (-2, -1, 1, 2)
BLOCKS = 4
LANES = 128
QUARTER = 32
F32 = jnp.float32
BF16 = jnp.bfloat16


def split_rows(values):
    high = values.astype(BF16).astype(F32)
    low = values - high
    blank = jnp.zeros((8, values.shape[1]), F32)
    return jnp.concatenate([high, high, low, blank], axis=0).astype(BF16)


def split_columns(matrix):
    high = matrix.astype(BF16).astype(F32)
    low = matrix - high
    blank = jnp.zeros((matrix.shape[0], 8), F32)
    return jnp.concatenate([high, low, high, blank], axis=1).astype(BF16)


def odd_and_high(shape):
    quarter = lax.broadcasted_iota(jnp.int32, shape, 1) // QUARTER
    return quarter % 2 == 1, quarter >= 2


def turned(odd, high, rows):
    pairs = [jnp.where(odd, rows[(k + 1) % BLOCKS], rows[k]) for k in range(BLOCKS)]
    return [
        jnp.where(high, pairs[(2 - i) % BLOCKS], pairs[(-i) % BLOCKS]) for i in range(BLOCKS)
    ]


def lane_gather(values, index):
    numbers = lax.GatherDimensionNumbers(
        offset_dims=(),
        collapsed_slice_dims=(1,),
        start_index_map=(1,),
        operand_batching_dims=(0,),
        start_indices_batching_dims=(0,),
    )
    return lax.gather(
        values,
        index[:, :, None],
        dimension_numbers=numbers,
        slice_sizes=(1, 1),
        mode=lax.GatherScatterMode.PROMISE_IN_BOUNDS,
    )


def groups(count):
    return (count + BLOCKS - 1) // BLOCKS


def taylor_factors(clusters):
    factors = []
    for cluster in range(clusters):
        width = BASE_STEP * 2.0**cluster
        factor = 1.0
        row = []
        for order in range(NDER):
            factor = factor * width / (order + 1)
            row.append(factor)
        factors.append(row)
    return factors


def pairing_blocks(region):
    second = region // 2 % 2
    odd = region % 2
    return [3 - 3 * second, 3 * second, 1 + odd, 2 - odd]


def predict_kernel(
    state_hbm,
    stiff_hbm,
    star_hbm,
    send_hbm,
    sub_hbm,
    cluster_hbm,
    face_hbm,
    orient_hbm,
    region_index_ref,
    sub_index_ref,
    integral_hbm,
    table_hbm,
    region_hbm0,
    region_hbm1,
    region_hbm2,
    region_hbm3,
    within_hbm0,
    within_hbm1,
    within_hbm2,
    stiff_ref,
    star_ref,
    send_ref,
    sub_ref,
    cluster_ref,
    face_ref,
    orient_ref,
    series_ref,
    product_ref,
    integral_ref,
    table_ref,
    region_ref,
    within_ref,
    arrived,
    sent,
):
    region_hbms = (region_hbm0, region_hbm1, region_hbm2, region_hbm3)
    quants, modes, lanes = state_hbm.shape
    clusters = integral_hbm.shape[0]
    dims = stiff_hbm.shape[0]
    copies = [
        pltpu.make_async_copy(source, target, arrived.at[place])
        for place, (source, target) in enumerate(
            [
                (stiff_hbm, stiff_ref),
                (state_hbm, series_ref.at[0]),
                (star_hbm, star_ref),
                (send_hbm, send_ref),
                (sub_hbm, sub_ref),
                (cluster_hbm, cluster_ref),
                (face_hbm, face_ref),
                (orient_hbm, orient_ref),
            ]
        )
    ]
    for copy in copies:
        copy.start()
    copies[0].wait()
    stacked = jnp.concatenate([stiff_ref[d] for d in range(dims)], axis=0)
    lhs = split_columns(-stacked)
    copies[1].wait()
    block = 5
    blocks = [range(first, min(first + block, quants)) for first in range(0, quants, block)]

    def multiply(slot, rows, values):
        product = jnp.dot(
            lhs, split_rows(jnp.concatenate(values, axis=1)), preferred_element_type=F32
        )
        for place, row in enumerate(rows):
            product_ref[slot, row] = product[:, place * lanes : (place + 1) * lanes]

    for rows in blocks:
        multiply(0, rows, [series_ref[0, row] for row in rows])
    for copy in copies[2:]:
        copy.wait()
    for order in range(1, NDER):
        slot = (order - 1) % 2
        for rows in blocks:
            sums = [None for _ in rows]
            for column in range(quants):
                for d in range(dims):
                    value = product_ref[slot, column, pl.ds(d * modes, modes), :]
                    for place, row in enumerate(rows):
                        term = star_ref[row, column, pl.ds(d, 1), :] * value
                        sums[place] = term if sums[place] is None else sums[place] + term
            for place, row in enumerate(rows):
                series_ref[order, row] = sums[place]
            if order < NDER - 1:
                multiply(1 - slot, rows, sums)

    factors = taylor_factors(clusters)
    per_quant = modes // 8
    count = quants * per_quant
    odd, high = odd_and_high((8, lanes))
    lists = pairing_blocks(region_index_ref[0])
    index = []
    for cluster in range(clusters):
        base = jnp.concatenate(
            [send_ref[0, cluster, pl.ds(lists[s], 1), :] for s in range(BLOCKS)], axis=1
        )
        base = jnp.broadcast_to(base, (8, lanes))
        index.append([base] + [pltpu.roll(base, QUARTER * i, 1) for i in range(1, BLOCKS)])
    sub_slots = sub_ref.shape[2]
    blank = jnp.zeros((1, QUARTER - clusters * sub_slots), jnp.int32)
    row = jnp.concatenate([sub_ref[c] for c in range(clusters)] + [blank], axis=1)
    sub_index = jnp.broadcast_to(jnp.concatenate([row] * BLOCKS, axis=1), (8, lanes))
    owner = lax.broadcasted_iota(jnp.int32, (8, lanes), 1) % QUARTER // sub_slots
    chunk = 4
    leaving = []

    def leave(source, target):
        leaving.append(pltpu.make_async_copy(source, target, sent.at[len(leaving)]))
        leaving[-1].start()

    here = sub_index_ref[0]
    brought = pairing_blocks(region_index_ref[0])
    cluster_row = cluster_ref[...]
    for face in range(face_ref.shape[0]):
        entry = face_ref[pl.ds(face, 1), :]
        place = entry - lanes
        sub_place = place - BLOCKS * QUARTER
        block = place // QUARTER
        slot = sum(jnp.where(block == brought[p], p, 0) for p in range(BLOCKS))
        source = (sub_place // sub_slots) ^ here
        for i in range(BLOCKS):
            region = ((slot + i) & (BLOCKS - 1)) * QUARTER + (place & (QUARTER - 1))
            within = ((source + i) & (BLOCKS - 1)) * QUARTER + cluster_row * sub_slots
            within = within + (sub_place & (sub_slots - 1))
            table_ref[face, pl.ds(i, 1), :] = region & (lanes - 1)
            table_ref[face, pl.ds(BLOCKS + i, 1), :] = within & (lanes - 1)
        table_ref[face, pl.ds(2 * BLOCKS + 2, 1), :] = entry & (lanes - 1)
        table_ref[face, pl.ds(2 * BLOCKS + 3, 1), :] = cluster_row
        kind = jnp.where(place < 0, -1, jnp.where(sub_place < 0, cluster_row, clusters))
        table_ref[face, pl.ds(2 * BLOCKS, 1), :] = kind
        table_ref[face, pl.ds(2 * BLOCKS + 1, 1), :] = orient_ref[pl.ds(face, 1), :]
    leave(table_ref, table_hbm)

    for group in range(groups(count)):
        picked = [[] for _ in range(clusters)]
        shared = []
        for member in range(BLOCKS):
            at = group * BLOCKS + member
            if at >= count:
                for cluster in range(clusters):
                    picked[cluster].append(picked[cluster][-1])
                shared.append(shared[-1])
                continue
            quant, rows = at // per_quant, pl.ds(at % per_quant * 8, 8)
            series = [series_ref[order, quant, rows, :] for order in range(NDER)]
            for cluster in range(clusters):
                total = factors[cluster][0] * series[0]
                for order in range(1, NDER):
                    total = total + factors[cluster][order] * series[order]
                integral_ref[cluster, at] = total
                picked[cluster].append(lane_gather(total, index[cluster][member]))
                other = lane_gather(total, sub_index)
                within = other if cluster == 0 else jnp.where(owner == cluster, other, within)
            shared.append(within)
        for cluster in range(clusters):
            for b, packed in enumerate(turned(odd, high, picked[cluster])):
                region_ref[b, cluster, group] = packed
        for k, packed in enumerate(turned(odd, high, shared)):
            within_ref[(0, 2, 1, 3)[k], group] = packed
        if (group + 1) % chunk == 0:
            part = pl.ds(group + 1 - chunk, chunk)
            for b in range(BLOCKS):
                leave(region_ref.at[b, :, part], region_hbms[b].at[:, part])
            first = (group + 1 - chunk) * BLOCKS
            done = pl.ds(first, min(chunk * BLOCKS, count - first))
            leave(integral_ref.at[:, done], integral_hbm.at[:, done])
    leave(within_ref.at[pl.ds(2, 2)], within_hbm1)
    leave(within_ref.at[0], within_hbm0)
    leave(within_ref.at[pl.ds(1, 1)], within_hbm2)
    for copy in leaving:
        copy.wait()


def near_kernel(table_ref, integral_ref, partner_ref):
    clusters, quants, modes, lanes = integral_ref.shape
    chosen = jnp.broadcast_to(table_ref[0, pl.ds(2 * BLOCKS + 3, 1), :], (8, lanes))
    masks = [chosen == cluster for cluster in range(clusters)]

    def one_face(face, _):
        index = jnp.broadcast_to(table_ref[face, pl.ds(2 * BLOCKS + 2, 1), :], (8, lanes))
        for quant in range(quants):
            for first in range(0, modes, 8):
                rows = pl.ds(first, 8)
                total = lane_gather(integral_ref[0, quant, rows, :], index)
                for cluster in range(1, clusters):
                    other = lane_gather(integral_ref[cluster, quant, rows, :], index)
                    total = jnp.where(masks[cluster], other, total)
                partner_ref[face, quant, rows, :] = total
        return 0

    lax.fori_loop(0, table_ref.shape[0], one_face, 0)


def own_kernel(
    table_ref,
    volume_ref,
    local_ref,
    integral_ref,
    state_ref,
    star_ref,
    plus_ref,
    neighbour_ref,
    result_ref,
    flux_ref,
    lhs_ref,
    product_ref,
):
    quants, modes, lanes = state_ref.shape
    clusters = integral_ref.shape[0]
    dims = volume_ref.shape[0]
    faces, orients = neighbour_ref.shape[:2]
    chosen = jnp.broadcast_to(table_ref[0, pl.ds(2 * BLOCKS + 3, 1), :], (8, lanes))
    masks = [chosen == cluster for cluster in range(clusters)]

    stacked = jnp.concatenate(
        [volume_ref[d] for d in range(dims)] + [-local_ref[f] for f in range(faces)], axis=0
    )
    lhs_ref[...] = split_columns(stacked)
    for quant in range(quants):
        parts = []
        for first in range(0, modes, 8):
            rows = pl.ds(first, 8)
            own = integral_ref[0, quant, rows, :]
            for cluster in range(1, clusters):
                own = jnp.where(masks[cluster], integral_ref[cluster, quant, rows, :], own)
            parts.append(own)
        product_ref[quant] = jnp.dot(
            lhs_ref[...], split_rows(jnp.concatenate(parts, axis=0)), preferred_element_type=F32
        )

    def own_row(row, _):
        total = state_ref[row]
        for column in range(quants):
            for part in range(dims + faces):
                value = product_ref[column, pl.ds(part * modes, modes), :]
                if part < dims:
                    matrix = star_ref[row, column, pl.ds(part, 1), :]
                else:
                    matrix = plus_ref[row, column, pl.ds(part - dims, 1), :]
                total = total + matrix * value
        result_ref[row] = total
        return 0

    lax.fori_loop(0, quants, own_row, 0)

    def one_face(face, _):
        stack = jnp.concatenate([-neighbour_ref[face, o] for o in range(orients)], axis=0)
        flux_ref[face] = split_columns(stack)
        return 0

    lax.fori_loop(0, faces, one_face, 0)


def neighbour_kernel(
    region_refs,
    first_ref,
    beside_ref,
    across_ref,
    table_ref,
    near_ref,
    minus_ref,
    flux_ref,
    own_ref,
    result_ref,
    pool_ref,
    sub_pool_ref,
    partner_ref,
):
    quants, modes, lanes = own_ref.shape
    faces = flux_ref.shape[0]
    clusters = region_refs[0].shape[0]
    orients = flux_ref.shape[1] // modes
    per_quant = modes // 8
    count = quants * per_quant
    odd, high = odd_and_high((8, lanes))

    def spread(face, row):
        return jnp.broadcast_to(table_ref[face, pl.ds(row, 1), :], (8, lanes))

    def unpack(group):
        for cluster in range(clusters):
            pools = turned(odd, high, [region_refs[b][cluster, group] for b in range(BLOCKS)])
            for member, pool in enumerate(pools):
                if group * BLOCKS + member < count:
                    pool_ref[cluster, group * BLOCKS + member] = pool
        within = [first_ref[group], beside_ref[0, group], across_ref[0, group], across_ref[1, group]]
        pools = turned(odd, high, within)
        for member, pool in enumerate(pools):
            if group * BLOCKS + member < count:
                sub_pool_ref[group * BLOCKS + member] = pool

    def gather(face, ats):
        kind = spread(face, 2 * BLOCKS)
        hits = [kind == cluster for cluster in range(clusters + 1)]
        region_index = [spread(face, i) for i in range(BLOCKS)]
        sub_index = [spread(face, BLOCKS + i) for i in range(BLOCKS)]
        for at in ats:
            rows = pl.ds(at % per_quant * 8, 8)
            total = near_ref[face, at // per_quant, rows, :]
            for cluster in range(clusters):
                other = lane_gather(pool_ref[cluster, at], region_index[at % BLOCKS])
                total = jnp.where(hits[cluster], other, total)
            other = lane_gather(sub_pool_ref[at], sub_index[at % BLOCKS])
            partner_ref[face, at // per_quant, rows, :] = jnp.where(hits[clusters], other, total)

    block = 2
    blocks = [range(first, min(first + block, quants)) for first in range(0, quants, block)]

    def flux(face, rows):
        orient = spread(face, 2 * BLOCKS + 1)
        masks = [orient == o for o in range(orients)]
        mixed = [None for _ in rows]
        for column in range(quants):
            value = partner_ref[face, column]
            for place, row in enumerate(rows):
                term = minus_ref[row, column, pl.ds(face, 1), :] * value
                mixed[place] = term if mixed[place] is None else mixed[place] + term
        every = jnp.dot(
            flux_ref[face], split_rows(jnp.concatenate(mixed, axis=1)), preferred_element_type=F32
        )
        for place, row in enumerate(rows):
            for first in range(0, modes, 8):
                columns = slice(place * lanes, (place + 1) * lanes)
                total = every[first : first + 8, columns]
                for o in range(1, orients):
                    at = o * modes + first
                    total = jnp.where(masks[o], every[at : at + 8, columns], total)
                where = pl.ds(first, 8)
                if face == 0:
                    total = total + own_ref[row, where, :]
                else:
                    total = total + result_ref[row, where, :]
                result_ref[row, where, :] = total

    for group in range(groups(count)):
        unpack(group)
    gather(0, range(count))
    for face in range(faces):
        step = (count + len(blocks) - 1) // len(blocks)
        for place, rows in enumerate(blocks):
            flux(face, rows)
            if face + 1 < faces:
                gather(face + 1, range(place * step, min((place + 1) * step, count)))


def whole(count):
    return [pl.BlockSpec(memory_space=pltpu.VMEM) for _ in range(count)]


def far(count):
    return [pl.BlockSpec(memory_space=pltpu.HBM) for _ in range(count)]


def paired(value, axis, pairing):
    count = lax.axis_size(axis)
    pairs = []
    for source in range(count):
        offset = OFFSETS[pairing_blocks(source)[pairing]]
        pairs.append((source, (source + offset) % count))
    return lax.ppermute(value, axis, pairs)


def swapped(value, axis, bit):
    return lax.ppermute(value, axis, [(s, s ^ bit) for s in range(lax.axis_size(axis))])


def local(
    modal_state,
    deriv_stiff,
    volume_stiff,
    local_flux,
    neighbour_flux,
    star_matrices,
    plus_flux,
    minus_flux,
    cluster_ids,
    face_neighbours,
    face_orient,
    send_lists,
    sub_lists,
):
    quants, modes, lanes = modal_state.shape
    clusters = send_lists.shape[2]
    faces, orients = neighbour_flux.shape[:2]
    dims = deriv_stiff.shape[0]
    depth = 3 * modes + 8
    count = quants * modes // 8
    fours = groups(count)
    near_params = pltpu.CompilerParams(vmem_limit_bytes=40 * 1024 * 1024)
    params = pltpu.CompilerParams(vmem_limit_bytes=60 * 1024 * 1024)
    shape = jax.ShapeDtypeStruct
    stars, plus, minus = (
        jnp.transpose(matrix, (1, 2, 0, 3)) for matrix in (star_matrices, plus_flux, minus_flux)
    )
    sends = jnp.transpose(send_lists, (0, 2, 1, 3))
    subs = jnp.transpose(sub_lists, (1, 0, 2))

    here = lax.axis_index("sub").astype(jnp.int32).reshape(1)
    region = lax.axis_index("region").astype(jnp.int32).reshape(1)

    integrals, table, *packed = pl.pallas_call(
        predict_kernel,
        out_shape=(
            shape((clusters, count, 8, lanes), F32),
            shape((faces, 2 * BLOCKS + 8, lanes), jnp.int32),
            *[shape((clusters, fours, 8, lanes), F32)] * BLOCKS,
            shape((fours, 8, lanes), F32),
            shape((2, fours, 8, lanes), F32),
            shape((1, fours, 8, lanes), F32),
        ),
        in_specs=far(8) + [pl.BlockSpec(memory_space=pltpu.SMEM)] * 2,
        out_specs=tuple(far(5 + BLOCKS)),
        scratch_shapes=[
            pltpu.VMEM(deriv_stiff.shape, F32),
            pltpu.VMEM(stars.shape, F32),
            pltpu.VMEM(sends.shape, jnp.int32),
            pltpu.VMEM(subs.shape, jnp.int32),
            pltpu.VMEM((1, lanes), jnp.int32),
            pltpu.VMEM(face_neighbours.shape, jnp.int32),
            pltpu.VMEM(face_orient.shape, jnp.int32),
            pltpu.VMEM((NDER, quants, modes, lanes), F32),
            pltpu.VMEM((2, quants, dims * modes, lanes), F32),
            pltpu.VMEM((clusters, count, 8, lanes), F32),
            pltpu.VMEM((faces, 2 * BLOCKS + 8, lanes), jnp.int32),
            pltpu.VMEM((BLOCKS, clusters, fours, 8, lanes), F32),
            pltpu.VMEM((BLOCKS, fours, 8, lanes), F32),
            pltpu.SemaphoreType.DMA((8,)),
            pltpu.SemaphoreType.DMA((fours + 8,)),
        ],
        compiler_params=params,
        name="predict",
    )(
        modal_state,
        deriv_stiff,
        stars,
        sends,
        subs,
        cluster_ids.reshape(1, lanes),
        face_neighbours,
        face_orient,
        region,
        here,
    )

    arrived = [paired(packed[p], "region", p) for p in range(BLOCKS)]
    first, beside, across = packed[BLOCKS:]
    beside = swapped(beside, "sub", 1)
    across = swapped(jnp.concatenate([across, beside[1:]], axis=0), "sub", 2)
    integrals = integrals.reshape(clusters, quants, modes, lanes)
    near_partner = pl.pallas_call(
        near_kernel,
        out_shape=shape((faces, quants, modes, lanes), F32),
        in_specs=whole(2),
        out_specs=whole(1)[0],
        compiler_params=near_params,
        cost_estimate=pl.CostEstimate(
            flops=4_000_000_000, bytes_accessed=8_000_000, transcendentals=0
        ),
        name="near",
    )(table, integrals)

    own, flux = pl.pallas_call(
        own_kernel,
        out_shape=(
            shape((quants, modes, lanes), F32),
            shape((faces, orients * modes, depth), BF16),
        ),
        in_specs=whole(8),
        out_specs=tuple(whole(2)),
        scratch_shapes=[
            pltpu.VMEM(((dims + faces) * modes, depth), BF16),
            pltpu.VMEM((quants, (dims + faces) * modes, lanes), F32),
        ],
        compiler_params=near_params,
        cost_estimate=pl.CostEstimate(
            flops=4_000_000_000, bytes_accessed=8_000_000, transcendentals=0
        ),
        name="own",
    )(
        table,
        volume_stiff,
        local_flux,
        integrals,
        modal_state,
        stars,
        plus,
        neighbour_flux,
    )

    return pl.pallas_call(
        neighbour_kernel,
        out_shape=shape((quants, modes, lanes), F32),
        in_specs=[whole(BLOCKS), *whole(8)],
        out_specs=whole(1)[0],
        scratch_shapes=[
            pltpu.VMEM((clusters, count, 8, lanes), F32),
            pltpu.VMEM((count, 8, lanes), F32),
            pltpu.VMEM((faces, quants, modes, lanes), F32),
        ],
        compiler_params=near_params,
        name="neighbour",
    )(arrived, first, beside, across, table, near_partner, minus, flux, own)


def solution(mesh):
    return jax.shard_map(
        local,
        mesh=mesh,
        in_specs=(
            P(None, None, ("region", "sub")),
            P(),
            P(),
            P(),
            P(),
            P(None, None, None, ("region", "sub")),
            P(None, None, None, ("region", "sub")),
            P(None, None, None, ("region", "sub")),
            P(("region", "sub")),
            P(None, ("region", "sub")),
            P(None, ("region", "sub")),
            P(("region", "sub"), None, None, None),
            P(("region", "sub"), None, None),
        ),
        out_specs=P(None, None, ("region", "sub")),
        check_vma=False,
    )
```

```python
import jax
import jax.numpy as jnp
from jax import lax
from jax.experimental import pallas as pl
from jax.experimental.pallas import tpu as pltpu
from jax.sharding import PartitionSpec as P

NDER = 6
BASE_STEP = 0.25
OFFSETS = (-2, -1, 1, 2)
BLOCKS = 4
LANES = 128
QUARTER = 32
F32 = jnp.float32
BF16 = jnp.bfloat16


def split_rows(values):
    high = values.astype(BF16).astype(F32)
    low = values - high
    blank = jnp.zeros((8, values.shape[1]), F32)
    return jnp.concatenate([high, high, low, blank], axis=0).astype(BF16)


def split_columns(matrix):
    high = matrix.astype(BF16).astype(F32)
    low = matrix - high
    blank = jnp.zeros((matrix.shape[0], 8), F32)
    return jnp.concatenate([high, low, high, blank], axis=1).astype(BF16)


def odd_and_high(shape):
    quarter = lax.broadcasted_iota(jnp.int32, shape, 1) // QUARTER
    return quarter % 2 == 1, quarter >= 2


def turned(odd, high, rows):
    pairs = [jnp.where(odd, rows[(k + 1) % BLOCKS], rows[k]) for k in range(BLOCKS)]
    return [
        jnp.where(high, pairs[(2 - i) % BLOCKS], pairs[(-i) % BLOCKS]) for i in range(BLOCKS)
    ]


def lane_gather(values, index):
    numbers = lax.GatherDimensionNumbers(
        offset_dims=(),
        collapsed_slice_dims=(1,),
        start_index_map=(1,),
        operand_batching_dims=(0,),
        start_indices_batching_dims=(0,),
    )
    return lax.gather(
        values,
        index[:, :, None],
        dimension_numbers=numbers,
        slice_sizes=(1, 1),
        mode=lax.GatherScatterMode.PROMISE_IN_BOUNDS,
    )


def groups(count):
    return (count + BLOCKS - 1) // BLOCKS


def taylor_factors(clusters):
    factors = []
    for cluster in range(clusters):
        width = BASE_STEP * 2.0**cluster
        factor = 1.0
        row = []
        for order in range(NDER):
            factor = factor * width / (order + 1)
            row.append(factor)
        factors.append(row)
    return factors


def pairing_blocks(region):
    half = region // 4 % 2
    second = region // 2 % 2
    odd = region % 2
    near, beside = 3 - 3 * second, 2 - odd
    turn = half * (beside - near)
    return [near + turn, 3 * second, 1 + odd, beside - turn]


def predict_kernel(
    state_hbm,
    stiff_hbm,
    star_hbm,
    send_hbm,
    sub_hbm,
    cluster_hbm,
    face_hbm,
    orient_hbm,
    region_index_ref,
    sub_index_ref,
    integral_hbm,
    table_hbm,
    region_hbm0,
    region_hbm1,
    region_hbm2,
    region_hbm3,
    within_hbm0,
    within_hbm1,
    within_hbm2,
    stiff_ref,
    star_ref,
    send_ref,
    sub_ref,
    cluster_ref,
    face_ref,
    orient_ref,
    series_ref,
    product_ref,
    integral_ref,
    table_ref,
    region_ref,
    within_ref,
    arrived,
    sent,
):
    region_hbms = (region_hbm0, region_hbm1, region_hbm2, region_hbm3)
    quants, modes, lanes = state_hbm.shape
    clusters = integral_hbm.shape[0]
    dims = stiff_hbm.shape[0]
    copies = [
        pltpu.make_async_copy(source, target, arrived.at[place])
        for place, (source, target) in enumerate(
            [
                (stiff_hbm, stiff_ref),
                (state_hbm, series_ref.at[0]),
                (star_hbm, star_ref),
                (send_hbm, send_ref),
                (sub_hbm, sub_ref),
                (cluster_hbm, cluster_ref),
                (face_hbm, face_ref),
                (orient_hbm, orient_ref),
            ]
        )
    ]
    for copy in copies:
        copy.start()
    copies[0].wait()
    stacked = jnp.concatenate([stiff_ref[d] for d in range(dims)], axis=0)
    lhs = split_columns(-stacked)
    copies[1].wait()
    block = 5
    blocks = [range(first, min(first + block, quants)) for first in range(0, quants, block)]

    def multiply(slot, rows, values):
        product = jnp.dot(
            lhs, split_rows(jnp.concatenate(values, axis=1)), preferred_element_type=F32
        )
        for place, row in enumerate(rows):
            product_ref[slot, row] = product[:, place * lanes : (place + 1) * lanes]

    for rows in blocks:
        multiply(0, rows, [series_ref[0, row] for row in rows])
    for copy in copies[2:]:
        copy.wait()
    for order in range(1, NDER):
        slot = (order - 1) % 2
        for rows in blocks:
            sums = [None for _ in rows]
            for column in range(quants):
                for d in range(dims):
                    value = product_ref[slot, column, pl.ds(d * modes, modes), :]
                    for place, row in enumerate(rows):
                        term = star_ref[row, column, pl.ds(d, 1), :] * value
                        sums[place] = term if sums[place] is None else sums[place] + term
            for place, row in enumerate(rows):
                series_ref[order, row] = sums[place]
            if order < NDER - 1:
                multiply(1 - slot, rows, sums)

    factors = taylor_factors(clusters)
    per_quant = modes // 8
    count = quants * per_quant
    odd, high = odd_and_high((8, lanes))
    lists = pairing_blocks(region_index_ref[0])
    index = []
    for cluster in range(clusters):
        base = jnp.concatenate(
            [send_ref[0, cluster, pl.ds(lists[s], 1), :] for s in range(BLOCKS)], axis=1
        )
        base = jnp.broadcast_to(base, (8, lanes))
        index.append([base] + [pltpu.roll(base, QUARTER * i, 1) for i in range(1, BLOCKS)])
    sub_slots = sub_ref.shape[2]
    blank = jnp.zeros((1, QUARTER - clusters * sub_slots), jnp.int32)
    row = jnp.concatenate([sub_ref[c] for c in range(clusters)] + [blank], axis=1)
    sub_index = jnp.broadcast_to(jnp.concatenate([row] * BLOCKS, axis=1), (8, lanes))
    owner = lax.broadcasted_iota(jnp.int32, (8, lanes), 1) % QUARTER // sub_slots
    chunk = 4
    leaving = []

    def leave(source, target):
        leaving.append(pltpu.make_async_copy(source, target, sent.at[len(leaving)]))
        leaving[-1].start()

    here = sub_index_ref[0]
    brought = pairing_blocks(region_index_ref[0])
    cluster_row = cluster_ref[...]
    for face in range(face_ref.shape[0]):
        entry = face_ref[pl.ds(face, 1), :]
        place = entry - lanes
        sub_place = place - BLOCKS * QUARTER
        block = place // QUARTER
        slot = sum(jnp.where(block == brought[p], p, 0) for p in range(BLOCKS))
        source = (sub_place // sub_slots) ^ here
        for i in range(BLOCKS):
            region = ((slot + i) & (BLOCKS - 1)) * QUARTER + (place & (QUARTER - 1))
            within = ((source + i) & (BLOCKS - 1)) * QUARTER + cluster_row * sub_slots
            within = within + (sub_place & (sub_slots - 1))
            table_ref[face, pl.ds(i, 1), :] = region & (lanes - 1)
            table_ref[face, pl.ds(BLOCKS + i, 1), :] = within & (lanes - 1)
        table_ref[face, pl.ds(2 * BLOCKS + 2, 1), :] = entry & (lanes - 1)
        table_ref[face, pl.ds(2 * BLOCKS + 3, 1), :] = cluster_row
        kind = jnp.where(place < 0, -1, jnp.where(sub_place < 0, cluster_row, clusters))
        table_ref[face, pl.ds(2 * BLOCKS, 1), :] = kind
        table_ref[face, pl.ds(2 * BLOCKS + 1, 1), :] = orient_ref[pl.ds(face, 1), :]
    leave(table_ref, table_hbm)

    for group in range(groups(count)):
        picked = [[] for _ in range(clusters)]
        shared = []
        for member in range(BLOCKS):
            at = group * BLOCKS + member
            if at >= count:
                for cluster in range(clusters):
                    picked[cluster].append(picked[cluster][-1])
                shared.append(shared[-1])
                continue
            quant, rows = at // per_quant, pl.ds(at % per_quant * 8, 8)
            series = [series_ref[order, quant, rows, :] for order in range(NDER)]
            for cluster in range(clusters):
                total = factors[cluster][0] * series[0]
                for order in range(1, NDER):
                    total = total + factors[cluster][order] * series[order]
                integral_ref[cluster, at] = total
                picked[cluster].append(lane_gather(total, index[cluster][member]))
                other = lane_gather(total, sub_index)
                within = other if cluster == 0 else jnp.where(owner == cluster, other, within)
            shared.append(within)
        for cluster in range(clusters):
            for b, packed in enumerate(turned(odd, high, picked[cluster])):
                region_ref[b, cluster, group] = packed
        for k, packed in enumerate(turned(odd, high, shared)):
            within_ref[(0, 2, 1, 3)[k], group] = packed
        if (group + 1) % chunk == 0:
            part = pl.ds(group + 1 - chunk, chunk)
            for b in range(BLOCKS):
                leave(region_ref.at[b, :, part], region_hbms[b].at[:, part])
            first = (group + 1 - chunk) * BLOCKS
            done = pl.ds(first, min(chunk * BLOCKS, count - first))
            leave(integral_ref.at[:, done], integral_hbm.at[:, done])
    leave(within_ref.at[pl.ds(2, 2)], within_hbm1)
    leave(within_ref.at[0], within_hbm0)
    leave(within_ref.at[pl.ds(1, 1)], within_hbm2)
    for copy in leaving:
        copy.wait()


def near_kernel(table_ref, integral_ref, partner_ref):
    clusters, quants, modes, lanes = integral_ref.shape
    chosen = jnp.broadcast_to(table_ref[0, pl.ds(2 * BLOCKS + 3, 1), :], (8, lanes))
    masks = [chosen == cluster for cluster in range(clusters)]

    def one_face(face, _):
        index = jnp.broadcast_to(table_ref[face, pl.ds(2 * BLOCKS + 2, 1), :], (8, lanes))
        for quant in range(quants):
            for first in range(0, modes, 8):
                rows = pl.ds(first, 8)
                total = lane_gather(integral_ref[0, quant, rows, :], index)
                for cluster in range(1, clusters):
                    other = lane_gather(integral_ref[cluster, quant, rows, :], index)
                    total = jnp.where(masks[cluster], other, total)
                partner_ref[face, quant, rows, :] = total
        return 0

    lax.fori_loop(0, table_ref.shape[0], one_face, 0)


def own_kernel(
    table_ref,
    volume_ref,
    local_ref,
    integral_ref,
    state_ref,
    star_ref,
    plus_ref,
    neighbour_ref,
    result_ref,
    flux_ref,
    lhs_ref,
    product_ref,
):
    quants, modes, lanes = state_ref.shape
    clusters = integral_ref.shape[0]
    dims = volume_ref.shape[0]
    faces, orients = neighbour_ref.shape[:2]
    chosen = jnp.broadcast_to(table_ref[0, pl.ds(2 * BLOCKS + 3, 1), :], (8, lanes))
    masks = [chosen == cluster for cluster in range(clusters)]

    stacked = jnp.concatenate(
        [volume_ref[d] for d in range(dims)] + [-local_ref[f] for f in range(faces)], axis=0
    )
    lhs_ref[...] = split_columns(stacked)
    for quant in range(quants):
        parts = []
        for first in range(0, modes, 8):
            rows = pl.ds(first, 8)
            own = integral_ref[0, quant, rows, :]
            for cluster in range(1, clusters):
                own = jnp.where(masks[cluster], integral_ref[cluster, quant, rows, :], own)
            parts.append(own)
        product_ref[quant] = jnp.dot(
            lhs_ref[...], split_rows(jnp.concatenate(parts, axis=0)), preferred_element_type=F32
        )

    def own_row(row, _):
        total = state_ref[row]
        for column in range(quants):
            for part in range(dims + faces):
                value = product_ref[column, pl.ds(part * modes, modes), :]
                if part < dims:
                    matrix = star_ref[row, column, pl.ds(part, 1), :]
                else:
                    matrix = plus_ref[row, column, pl.ds(part - dims, 1), :]
                total = total + matrix * value
        result_ref[row] = total
        return 0

    lax.fori_loop(0, quants, own_row, 0)

    def one_face(face, _):
        stack = jnp.concatenate([-neighbour_ref[face, o] for o in range(orients)], axis=0)
        flux_ref[face] = split_columns(stack)
        return 0

    lax.fori_loop(0, faces, one_face, 0)


def neighbour_kernel(
    region_refs,
    first_ref,
    beside_ref,
    across_ref,
    table_ref,
    near_ref,
    minus_ref,
    flux_ref,
    own_ref,
    result_ref,
    pool_ref,
    sub_pool_ref,
    partner_ref,
):
    quants, modes, lanes = own_ref.shape
    faces = flux_ref.shape[0]
    clusters = region_refs[0].shape[0]
    orients = flux_ref.shape[1] // modes
    per_quant = modes // 8
    count = quants * per_quant
    odd, high = odd_and_high((8, lanes))

    def spread(face, row):
        return jnp.broadcast_to(table_ref[face, pl.ds(row, 1), :], (8, lanes))

    def unpack(group):
        for cluster in range(clusters):
            brought = [region_refs[b][cluster, group] for b in range(BLOCKS + 1)]
            pools = turned(odd, high, [brought[0] + brought[BLOCKS], *brought[1:BLOCKS]])
            for member, pool in enumerate(pools):
                if group * BLOCKS + member < count:
                    pool_ref[cluster, group * BLOCKS + member] = pool
        within = [first_ref[group], beside_ref[0, group], across_ref[0, group], across_ref[1, group]]
        pools = turned(odd, high, within)
        for member, pool in enumerate(pools):
            if group * BLOCKS + member < count:
                sub_pool_ref[group * BLOCKS + member] = pool

    def gather(face, ats):
        kind = spread(face, 2 * BLOCKS)
        hits = [kind == cluster for cluster in range(clusters + 1)]
        region_index = [spread(face, i) for i in range(BLOCKS)]
        sub_index = [spread(face, BLOCKS + i) for i in range(BLOCKS)]
        for at in ats:
            rows = pl.ds(at % per_quant * 8, 8)
            total = near_ref[face, at // per_quant, rows, :]
            for cluster in range(clusters):
                other = lane_gather(pool_ref[cluster, at], region_index[at % BLOCKS])
                total = jnp.where(hits[cluster], other, total)
            other = lane_gather(sub_pool_ref[at], sub_index[at % BLOCKS])
            partner_ref[face, at // per_quant, rows, :] = jnp.where(hits[clusters], other, total)

    block = 2
    blocks = [range(first, min(first + block, quants)) for first in range(0, quants, block)]

    def flux(face, rows):
        orient = spread(face, 2 * BLOCKS + 1)
        masks = [orient == o for o in range(orients)]
        mixed = [None for _ in rows]
        for column in range(quants):
            value = partner_ref[face, column]
            for place, row in enumerate(rows):
                term = minus_ref[row, column, pl.ds(face, 1), :] * value
                mixed[place] = term if mixed[place] is None else mixed[place] + term
        every = jnp.dot(
            flux_ref[face], split_rows(jnp.concatenate(mixed, axis=1)), preferred_element_type=F32
        )
        for place, row in enumerate(rows):
            for first in range(0, modes, 8):
                columns = slice(place * lanes, (place + 1) * lanes)
                total = every[first : first + 8, columns]
                for o in range(1, orients):
                    at = o * modes + first
                    total = jnp.where(masks[o], every[at : at + 8, columns], total)
                where = pl.ds(first, 8)
                if face == 0:
                    total = total + own_ref[row, where, :]
                else:
                    total = total + result_ref[row, where, :]
                result_ref[row, where, :] = total

    for group in range(groups(count)):
        unpack(group)
    gather(0, range(count))
    for face in range(faces):
        step = (count + len(blocks) - 1) // len(blocks)
        for place, rows in enumerate(blocks):
            flux(face, rows)
            if face + 1 < faces:
                gather(face + 1, range(place * step, min((place + 1) * step, count)))


def whole(count):
    return [pl.BlockSpec(memory_space=pltpu.VMEM) for _ in range(count)]


def far(count):
    return [pl.BlockSpec(memory_space=pltpu.HBM) for _ in range(count)]


def paired(value, axis, pairing, halves=(0, 1)):
    count = lax.axis_size(axis)
    pairs = []
    for source in range(count):
        if source // 4 % 2 in halves:
            offset = OFFSETS[pairing_blocks(source)[pairing]]
            pairs.append((source, (source + offset) % count))
    return lax.ppermute(value, axis, pairs)


def swapped(value, axis, bit):
    return lax.ppermute(value, axis, [(s, s ^ bit) for s in range(lax.axis_size(axis))])


def local(
    modal_state,
    deriv_stiff,
    volume_stiff,
    local_flux,
    neighbour_flux,
    star_matrices,
    plus_flux,
    minus_flux,
    cluster_ids,
    face_neighbours,
    face_orient,
    send_lists,
    sub_lists,
):
    quants, modes, lanes = modal_state.shape
    clusters = send_lists.shape[2]
    faces, orients = neighbour_flux.shape[:2]
    dims = deriv_stiff.shape[0]
    depth = 3 * modes + 8
    count = quants * modes // 8
    fours = groups(count)
    near_params = pltpu.CompilerParams(vmem_limit_bytes=40 * 1024 * 1024)
    params = pltpu.CompilerParams(vmem_limit_bytes=60 * 1024 * 1024)
    shape = jax.ShapeDtypeStruct
    stars, plus, minus = (
        jnp.transpose(matrix, (1, 2, 0, 3)) for matrix in (star_matrices, plus_flux, minus_flux)
    )
    sends = jnp.transpose(send_lists, (0, 2, 1, 3))
    subs = jnp.transpose(sub_lists, (1, 0, 2))

    here = lax.axis_index("sub").astype(jnp.int32).reshape(1)
    region = lax.axis_index("region").astype(jnp.int32).reshape(1)

    integrals, table, *packed = pl.pallas_call(
        predict_kernel,
        out_shape=(
            shape((clusters, count, 8, lanes), F32),
            shape((faces, 2 * BLOCKS + 8, lanes), jnp.int32),
            *[shape((clusters, fours, 8, lanes), F32)] * BLOCKS,
            shape((fours, 8, lanes), F32),
            shape((2, fours, 8, lanes), F32),
            shape((1, fours, 8, lanes), F32),
        ),
        in_specs=far(8) + [pl.BlockSpec(memory_space=pltpu.SMEM)] * 2,
        out_specs=tuple(far(5 + BLOCKS)),
        scratch_shapes=[
            pltpu.VMEM(deriv_stiff.shape, F32),
            pltpu.VMEM(stars.shape, F32),
            pltpu.VMEM(sends.shape, jnp.int32),
            pltpu.VMEM(subs.shape, jnp.int32),
            pltpu.VMEM((1, lanes), jnp.int32),
            pltpu.VMEM(face_neighbours.shape, jnp.int32),
            pltpu.VMEM(face_orient.shape, jnp.int32),
            pltpu.VMEM((NDER, quants, modes, lanes), F32),
            pltpu.VMEM((2, quants, dims * modes, lanes), F32),
            pltpu.VMEM((clusters, count, 8, lanes), F32),
            pltpu.VMEM((faces, 2 * BLOCKS + 8, lanes), jnp.int32),
            pltpu.VMEM((BLOCKS, clusters, fours, 8, lanes), F32),
            pltpu.VMEM((BLOCKS, fours, 8, lanes), F32),
            pltpu.SemaphoreType.DMA((8,)),
            pltpu.SemaphoreType.DMA((fours + 8,)),
        ],
        compiler_params=params,
        name="predict",
    )(
        modal_state,
        deriv_stiff,
        stars,
        sends,
        subs,
        cluster_ids.reshape(1, lanes),
        face_neighbours,
        face_orient,
        region,
        here,
    )

    early = paired(packed[0], "region", 0, (0,))
    arrived = [paired(packed[p], "region", p) for p in range(1, BLOCKS)]
    first, beside, across = packed[BLOCKS:]
    beside = swapped(beside, "sub", 1)
    last, beside = lax.optimization_barrier((packed[0], beside))
    late = paired(last, "region", 0, (1,))
    across = swapped(jnp.concatenate([across, beside[1:]], axis=0), "sub", 2)
    integrals = integrals.reshape(clusters, quants, modes, lanes)
    near_partner = pl.pallas_call(
        near_kernel,
        out_shape=shape((faces, quants, modes, lanes), F32),
        in_specs=whole(2),
        out_specs=whole(1)[0],
        compiler_params=near_params,
        cost_estimate=pl.CostEstimate(
            flops=4_000_000_000, bytes_accessed=8_000_000, transcendentals=0
        ),
        name="near",
    )(table, integrals)

    own, flux = pl.pallas_call(
        own_kernel,
        out_shape=(
            shape((quants, modes, lanes), F32),
            shape((faces, orients * modes, depth), BF16),
        ),
        in_specs=whole(8),
        out_specs=tuple(whole(2)),
        scratch_shapes=[
            pltpu.VMEM(((dims + faces) * modes, depth), BF16),
            pltpu.VMEM((quants, (dims + faces) * modes, lanes), F32),
        ],
        compiler_params=near_params,
        cost_estimate=pl.CostEstimate(
            flops=4_000_000_000, bytes_accessed=8_000_000, transcendentals=0
        ),
        name="own",
    )(
        table,
        volume_stiff,
        local_flux,
        integrals,
        modal_state,
        stars,
        plus,
        neighbour_flux,
    )

    return pl.pallas_call(
        neighbour_kernel,
        out_shape=shape((quants, modes, lanes), F32),
        in_specs=[whole(BLOCKS + 1), *whole(8)],
        out_specs=whole(1)[0],
        scratch_shapes=[
            pltpu.VMEM((clusters, count, 8, lanes), F32),
            pltpu.VMEM((count, 8, lanes), F32),
            pltpu.VMEM((faces, quants, modes, lanes), F32),
        ],
        compiler_params=near_params,
        name="neighbour",
    )([early, *arrived, late], first, beside, across, table, near_partner, minus, flux, own)


def solution(mesh):
    return jax.shard_map(
        local,
        mesh=mesh,
        in_specs=(
            P(None, None, ("region", "sub")),
            P(),
            P(),
            P(),
            P(),
            P(None, None, None, ("region", "sub")),
            P(None, None, None, ("region", "sub")),
            P(None, None, None, ("region", "sub")),
            P(("region", "sub")),
            P(None, ("region", "sub")),
            P(None, ("region", "sub")),
            P(("region", "sub"), None, None, None),
            P(("region", "sub"), None, None),
        ),
        out_specs=P(None, None, ("region", "sub")),
        check_vma=False,
    )
```

```python
import jax
import jax.numpy as jnp
from jax import lax
from jax.experimental import pallas as pl
from jax.experimental.pallas import tpu as pltpu
from jax.sharding import PartitionSpec as P

NDER = 6
BASE_STEP = 0.25
OFFSETS = (-2, -1, 1, 2)
BLOCKS = 4
LANES = 128
QUARTER = 32
F32 = jnp.float32
BF16 = jnp.bfloat16


def split_rows(values):
    high = values.astype(BF16).astype(F32)
    low = values - high
    blank = jnp.zeros((8, values.shape[1]), F32)
    return jnp.concatenate([high, high, low, blank], axis=0).astype(BF16)


def split_columns(matrix):
    high = matrix.astype(BF16).astype(F32)
    low = matrix - high
    blank = jnp.zeros((matrix.shape[0], 8), F32)
    return jnp.concatenate([high, low, high, blank], axis=1).astype(BF16)


def odd_and_high(shape):
    quarter = lax.broadcasted_iota(jnp.int32, shape, 1) // QUARTER
    return quarter % 2 == 1, quarter >= 2


def turned(odd, high, rows):
    pairs = [jnp.where(odd, rows[(k + 1) % BLOCKS], rows[k]) for k in range(BLOCKS)]
    return [
        jnp.where(high, pairs[(2 - i) % BLOCKS], pairs[(-i) % BLOCKS]) for i in range(BLOCKS)
    ]


def lane_gather(values, index):
    numbers = lax.GatherDimensionNumbers(
        offset_dims=(),
        collapsed_slice_dims=(1,),
        start_index_map=(1,),
        operand_batching_dims=(0,),
        start_indices_batching_dims=(0,),
    )
    return lax.gather(
        values,
        index[:, :, None],
        dimension_numbers=numbers,
        slice_sizes=(1, 1),
        mode=lax.GatherScatterMode.PROMISE_IN_BOUNDS,
    )


def groups(count):
    return (count + BLOCKS - 1) // BLOCKS


def taylor_factors(clusters):
    factors = []
    for cluster in range(clusters):
        width = BASE_STEP * 2.0**cluster
        factor = 1.0
        row = []
        for order in range(NDER):
            factor = factor * width / (order + 1)
            row.append(factor)
        factors.append(row)
    return factors


def pairing_blocks(region):
    half = region // 4 % 2
    second = region // 2 % 2
    odd = region % 2
    near, beside = 3 - 3 * second, 2 - odd
    turn = half * (beside - near)
    return [near + turn, 3 * second, 1 + odd, beside - turn]


def predict_kernel(
    state_hbm,
    stiff_hbm,
    star_hbm,
    send_hbm,
    sub_hbm,
    cluster_hbm,
    face_hbm,
    orient_hbm,
    region_index_ref,
    sub_index_ref,
    integral_hbm,
    table_hbm,
    region_hbm0,
    region_hbm1,
    region_hbm2,
    region_hbm3,
    within_hbm0,
    within_hbm1,
    within_hbm2,
    stiff_ref,
    star_ref,
    send_ref,
    sub_ref,
    cluster_ref,
    face_ref,
    orient_ref,
    series_ref,
    product_ref,
    integral_ref,
    table_ref,
    region_ref,
    within_ref,
    arrived,
    sent,
):
    region_hbms = (region_hbm0, region_hbm1, region_hbm2, region_hbm3)
    quants, modes, lanes = state_hbm.shape
    clusters = integral_hbm.shape[0]
    dims = stiff_hbm.shape[0]
    copies = [
        pltpu.make_async_copy(source, target, arrived.at[place])
        for place, (source, target) in enumerate(
            [
                (stiff_hbm, stiff_ref),
                (state_hbm, series_ref.at[0]),
                (star_hbm, star_ref),
                (send_hbm, send_ref),
                (sub_hbm, sub_ref),
                (cluster_hbm, cluster_ref),
                (face_hbm, face_ref),
                (orient_hbm, orient_ref),
            ]
        )
    ]
    for copy in copies:
        copy.start()
    copies[0].wait()
    stacked = jnp.concatenate([stiff_ref[d] for d in range(dims)], axis=0)
    lhs = split_columns(-stacked)
    copies[1].wait()
    block = 5
    blocks = [range(first, min(first + block, quants)) for first in range(0, quants, block)]

    def multiply(slot, rows, values):
        product = jnp.dot(
            lhs, split_rows(jnp.concatenate(values, axis=1)), preferred_element_type=F32
        )
        for place, row in enumerate(rows):
            product_ref[slot, row] = product[:, place * lanes : (place + 1) * lanes]

    for rows in blocks:
        multiply(0, rows, [series_ref[0, row] for row in rows])
    for copy in copies[2:]:
        copy.wait()
    for order in range(1, NDER):
        slot = (order - 1) % 2
        for rows in blocks:
            sums = [None for _ in rows]
            for column in range(quants):
                for d in range(dims):
                    value = product_ref[slot, column, pl.ds(d * modes, modes), :]
                    for place, row in enumerate(rows):
                        term = star_ref[row, column, pl.ds(d, 1), :] * value
                        sums[place] = term if sums[place] is None else sums[place] + term
            for place, row in enumerate(rows):
                series_ref[order, row] = sums[place]
            if order < NDER - 1:
                multiply(1 - slot, rows, sums)

    factors = taylor_factors(clusters)
    per_quant = modes // 8
    count = quants * per_quant
    odd, high = odd_and_high((8, lanes))
    lists = pairing_blocks(region_index_ref[0])
    index = []
    for cluster in range(clusters):
        base = jnp.concatenate(
            [send_ref[0, cluster, pl.ds(lists[s], 1), :] for s in range(BLOCKS)], axis=1
        )
        base = jnp.broadcast_to(base, (8, lanes))
        index.append([base] + [pltpu.roll(base, QUARTER * i, 1) for i in range(1, BLOCKS)])
    sub_slots = sub_ref.shape[2]
    blank = jnp.zeros((1, QUARTER - clusters * sub_slots), jnp.int32)
    row = jnp.concatenate([sub_ref[c] for c in range(clusters)] + [blank], axis=1)
    sub_index = jnp.broadcast_to(jnp.concatenate([row] * BLOCKS, axis=1), (8, lanes))
    owner = lax.broadcasted_iota(jnp.int32, (8, lanes), 1) % QUARTER // sub_slots
    chunk = 4
    leaving = []

    def leave(source, target):
        leaving.append(pltpu.make_async_copy(source, target, sent.at[len(leaving)]))
        leaving[-1].start()

    here = sub_index_ref[0]
    brought = pairing_blocks(region_index_ref[0])
    cluster_row = cluster_ref[...]
    for face in range(face_ref.shape[0]):
        entry = face_ref[pl.ds(face, 1), :]
        place = entry - lanes
        sub_place = place - BLOCKS * QUARTER
        block = place // QUARTER
        slot = sum(jnp.where(block == brought[p], p, 0) for p in range(BLOCKS))
        source = (sub_place // sub_slots) ^ here
        for i in range(BLOCKS):
            region = ((slot + i) & (BLOCKS - 1)) * QUARTER + (place & (QUARTER - 1))
            within = ((source + i) & (BLOCKS - 1)) * QUARTER + cluster_row * sub_slots
            within = within + (sub_place & (sub_slots - 1))
            table_ref[face, pl.ds(i, 1), :] = region & (lanes - 1)
            table_ref[face, pl.ds(BLOCKS + i, 1), :] = within & (lanes - 1)
        table_ref[face, pl.ds(2 * BLOCKS + 2, 1), :] = entry & (lanes - 1)
        table_ref[face, pl.ds(2 * BLOCKS + 3, 1), :] = cluster_row
        kind = jnp.where(place < 0, -1, jnp.where(sub_place < 0, cluster_row, clusters))
        table_ref[face, pl.ds(2 * BLOCKS, 1), :] = kind
        table_ref[face, pl.ds(2 * BLOCKS + 1, 1), :] = orient_ref[pl.ds(face, 1), :]
    leave(table_ref, table_hbm)

    for group in range(groups(count)):
        picked = [[] for _ in range(clusters)]
        shared = []
        for member in range(BLOCKS):
            at = group * BLOCKS + member
            if at >= count:
                for cluster in range(clusters):
                    picked[cluster].append(picked[cluster][-1])
                shared.append(shared[-1])
                continue
            quant, rows = at // per_quant, pl.ds(at % per_quant * 8, 8)
            series = [series_ref[order, quant, rows, :] for order in range(NDER)]
            for cluster in range(clusters):
                total = factors[cluster][0] * series[0]
                for order in range(1, NDER):
                    total = total + factors[cluster][order] * series[order]
                integral_ref[cluster, at] = total
                picked[cluster].append(lane_gather(total, index[cluster][member]))
                other = lane_gather(total, sub_index)
                within = other if cluster == 0 else jnp.where(owner == cluster, other, within)
            shared.append(within)
        for cluster in range(clusters):
            for b, packed in enumerate(turned(odd, high, picked[cluster])):
                region_ref[b, cluster, group] = packed
        for k, packed in enumerate(turned(odd, high, shared)):
            within_ref[(0, 2, 1, 3)[k], group] = packed
        if (group + 1) % chunk == 0:
            part = pl.ds(group + 1 - chunk, chunk)
            for b in range(BLOCKS):
                leave(region_ref.at[b, :, part], region_hbms[b].at[:, part])
            first = (group + 1 - chunk) * BLOCKS
            done = pl.ds(first, min(chunk * BLOCKS, count - first))
            leave(integral_ref.at[:, done], integral_hbm.at[:, done])
    leave(within_ref.at[pl.ds(2, 2)], within_hbm1)
    leave(within_ref.at[0], within_hbm0)
    leave(within_ref.at[pl.ds(1, 1)], within_hbm2)
    for copy in leaving:
        copy.wait()


def near_kernel(table_ref, integral_ref, partner_ref):
    clusters, quants, modes, lanes = integral_ref.shape
    chosen = jnp.broadcast_to(table_ref[0, pl.ds(2 * BLOCKS + 3, 1), :], (8, lanes))
    masks = [chosen == cluster for cluster in range(clusters)]

    def one_face(face, _):
        index = jnp.broadcast_to(table_ref[face, pl.ds(2 * BLOCKS + 2, 1), :], (8, lanes))
        for quant in range(quants):
            for first in range(0, modes, 8):
                rows = pl.ds(first, 8)
                total = lane_gather(integral_ref[0, quant, rows, :], index)
                for cluster in range(1, clusters):
                    other = lane_gather(integral_ref[cluster, quant, rows, :], index)
                    total = jnp.where(masks[cluster], other, total)
                partner_ref[face, quant, rows, :] = total
        return 0

    lax.fori_loop(0, table_ref.shape[0], one_face, 0)


def own_kernel(
    table_ref,
    volume_ref,
    local_ref,
    integral_ref,
    state_ref,
    star_ref,
    plus_ref,
    neighbour_ref,
    result_ref,
    flux_ref,
    lhs_ref,
    product_ref,
):
    quants, modes, lanes = state_ref.shape
    clusters = integral_ref.shape[0]
    dims = volume_ref.shape[0]
    faces, orients = neighbour_ref.shape[:2]
    chosen = jnp.broadcast_to(table_ref[0, pl.ds(2 * BLOCKS + 3, 1), :], (8, lanes))
    masks = [chosen == cluster for cluster in range(clusters)]

    stacked = jnp.concatenate(
        [volume_ref[d] for d in range(dims)] + [-local_ref[f] for f in range(faces)], axis=0
    )
    lhs_ref[...] = split_columns(stacked)
    for quant in range(quants):
        parts = []
        for first in range(0, modes, 8):
            rows = pl.ds(first, 8)
            own = integral_ref[0, quant, rows, :]
            for cluster in range(1, clusters):
                own = jnp.where(masks[cluster], integral_ref[cluster, quant, rows, :], own)
            parts.append(own)
        product_ref[quant] = jnp.dot(
            lhs_ref[...], split_rows(jnp.concatenate(parts, axis=0)), preferred_element_type=F32
        )

    def own_row(row, _):
        total = state_ref[row]
        for column in range(quants):
            for part in range(dims + faces):
                value = product_ref[column, pl.ds(part * modes, modes), :]
                if part < dims:
                    matrix = star_ref[row, column, pl.ds(part, 1), :]
                else:
                    matrix = plus_ref[row, column, pl.ds(part - dims, 1), :]
                total = total + matrix * value
        result_ref[row] = total
        return 0

    lax.fori_loop(0, quants, own_row, 0)

    def one_face(face, _):
        stack = jnp.concatenate([-neighbour_ref[face, o] for o in range(orients)], axis=0)
        flux_ref[face] = split_columns(stack)
        return 0

    lax.fori_loop(0, faces, one_face, 0)


def neighbour_kernel(
    region_refs,
    first_ref,
    beside_ref,
    across_ref,
    table_ref,
    near_ref,
    minus_ref,
    flux_ref,
    own_ref,
    result_ref,
    pool_ref,
    sub_pool_ref,
    partner_ref,
):
    quants, modes, lanes = own_ref.shape
    faces = flux_ref.shape[0]
    clusters = region_refs[0].shape[0]
    orients = flux_ref.shape[1] // modes
    per_quant = modes // 8
    count = quants * per_quant
    odd, high = odd_and_high((8, lanes))

    def spread(face, row):
        return jnp.broadcast_to(table_ref[face, pl.ds(row, 1), :], (8, lanes))

    def unpack(group):
        for cluster in range(clusters):
            pools = turned(odd, high, [region_refs[b][cluster, group] for b in range(BLOCKS)])
            for member, pool in enumerate(pools):
                if group * BLOCKS + member < count:
                    pool_ref[cluster, group * BLOCKS + member] = pool
        within = [first_ref[group], beside_ref[0, group], across_ref[0, group], across_ref[1, group]]
        pools = turned(odd, high, within)
        for member, pool in enumerate(pools):
            if group * BLOCKS + member < count:
                sub_pool_ref[group * BLOCKS + member] = pool

    def gather(face, ats):
        kind = spread(face, 2 * BLOCKS)
        hits = [kind == cluster for cluster in range(clusters + 1)]
        region_index = [spread(face, i) for i in range(BLOCKS)]
        sub_index = [spread(face, BLOCKS + i) for i in range(BLOCKS)]
        for at in ats:
            rows = pl.ds(at % per_quant * 8, 8)
            total = near_ref[face, at // per_quant, rows, :]
            for cluster in range(clusters):
                other = lane_gather(pool_ref[cluster, at], region_index[at % BLOCKS])
                total = jnp.where(hits[cluster], other, total)
            other = lane_gather(sub_pool_ref[at], sub_index[at % BLOCKS])
            partner_ref[face, at // per_quant, rows, :] = jnp.where(hits[clusters], other, total)

    block = 2
    blocks = [range(first, min(first + block, quants)) for first in range(0, quants, block)]

    def mix(face, rows):
        mixed = [None for _ in rows]
        for column in range(quants):
            value = partner_ref[face, column]
            for place, row in enumerate(rows):
                term = minus_ref[row, column, pl.ds(face, 1), :] * value
                mixed[place] = term if mixed[place] is None else mixed[place] + term
        return split_rows(jnp.concatenate(mixed, axis=1))

    def select(face, rows, every):
        orient = spread(face, 2 * BLOCKS + 1)
        masks = [orient == o for o in range(orients)]
        for place, row in enumerate(rows):
            for first in range(0, modes, 8):
                columns = slice(place * lanes, (place + 1) * lanes)
                total = every[first : first + 8, columns]
                for o in range(1, orients):
                    at = o * modes + first
                    total = jnp.where(masks[o], every[at : at + 8, columns], total)
                where = pl.ds(first, 8)
                if face == 0:
                    total = total + own_ref[row, where, :]
                else:
                    total = total + result_ref[row, where, :]
                result_ref[row, where, :] = total

    for group in range(groups(count)):
        unpack(group)
    gather(0, range(count))
    step = (count + len(blocks) - 1) // len(blocks)
    steps = [(face, place) for face in range(faces) for place in range(len(blocks))]
    ready = mix(0, blocks[0])
    for at, (face, place) in enumerate(steps):
        every = jnp.dot(flux_ref[face], ready, preferred_element_type=F32)
        if face + 1 < faces:
            gather(face + 1, range(place * step, min((place + 1) * step, count)))
        if at + 1 < len(steps):
            later, block = steps[at + 1]
            ready = mix(later, blocks[block])
        select(face, blocks[place], every)


def whole(count):
    return [pl.BlockSpec(memory_space=pltpu.VMEM) for _ in range(count)]


def far(count):
    return [pl.BlockSpec(memory_space=pltpu.HBM) for _ in range(count)]


def paired(value, axis, pairing):
    count = lax.axis_size(axis)
    pairs = []
    for source in range(count):
        offset = OFFSETS[pairing_blocks(source)[pairing]]
        pairs.append((source, (source + offset) % count))
    return lax.ppermute(value, axis, pairs)


def swapped(value, axis, bit):
    return lax.ppermute(value, axis, [(s, s ^ bit) for s in range(lax.axis_size(axis))])


def local(
    modal_state,
    deriv_stiff,
    volume_stiff,
    local_flux,
    neighbour_flux,
    star_matrices,
    plus_flux,
    minus_flux,
    cluster_ids,
    face_neighbours,
    face_orient,
    send_lists,
    sub_lists,
):
    quants, modes, lanes = modal_state.shape
    clusters = send_lists.shape[2]
    faces, orients = neighbour_flux.shape[:2]
    dims = deriv_stiff.shape[0]
    depth = 3 * modes + 8
    count = quants * modes // 8
    fours = groups(count)
    near_params = pltpu.CompilerParams(vmem_limit_bytes=40 * 1024 * 1024)
    params = pltpu.CompilerParams(vmem_limit_bytes=60 * 1024 * 1024)
    shape = jax.ShapeDtypeStruct
    stars, plus, minus = (
        jnp.transpose(matrix, (1, 2, 0, 3)) for matrix in (star_matrices, plus_flux, minus_flux)
    )
    sends = jnp.transpose(send_lists, (0, 2, 1, 3))
    subs = jnp.transpose(sub_lists, (1, 0, 2))

    here = lax.axis_index("sub").astype(jnp.int32).reshape(1)
    region = lax.axis_index("region").astype(jnp.int32).reshape(1)

    integrals, table, *packed = pl.pallas_call(
        predict_kernel,
        out_shape=(
            shape((clusters, count, 8, lanes), F32),
            shape((faces, 2 * BLOCKS + 8, lanes), jnp.int32),
            *[shape((clusters, fours, 8, lanes), F32)] * BLOCKS,
            shape((fours, 8, lanes), F32),
            shape((2, fours, 8, lanes), F32),
            shape((1, fours, 8, lanes), F32),
        ),
        in_specs=far(8) + [pl.BlockSpec(memory_space=pltpu.SMEM)] * 2,
        out_specs=tuple(far(5 + BLOCKS)),
        scratch_shapes=[
            pltpu.VMEM(deriv_stiff.shape, F32),
            pltpu.VMEM(stars.shape, F32),
            pltpu.VMEM(sends.shape, jnp.int32),
            pltpu.VMEM(subs.shape, jnp.int32),
            pltpu.VMEM((1, lanes), jnp.int32),
            pltpu.VMEM(face_neighbours.shape, jnp.int32),
            pltpu.VMEM(face_orient.shape, jnp.int32),
            pltpu.VMEM((NDER, quants, modes, lanes), F32),
            pltpu.VMEM((2, quants, dims * modes, lanes), F32),
            pltpu.VMEM((clusters, count, 8, lanes), F32),
            pltpu.VMEM((faces, 2 * BLOCKS + 8, lanes), jnp.int32),
            pltpu.VMEM((BLOCKS, clusters, fours, 8, lanes), F32),
            pltpu.VMEM((BLOCKS, fours, 8, lanes), F32),
            pltpu.SemaphoreType.DMA((8,)),
            pltpu.SemaphoreType.DMA((fours + 8,)),
        ],
        compiler_params=params,
        name="predict",
    )(
        modal_state,
        deriv_stiff,
        stars,
        sends,
        subs,
        cluster_ids.reshape(1, lanes),
        face_neighbours,
        face_orient,
        region,
        here,
    )

    arrived = [paired(packed[p], "region", p) for p in range(BLOCKS)]
    first, beside, across = packed[BLOCKS:]
    beside = swapped(beside, "sub", 1)
    across = swapped(jnp.concatenate([across, beside[1:]], axis=0), "sub", 2)
    integrals = integrals.reshape(clusters, quants, modes, lanes)
    near_partner = pl.pallas_call(
        near_kernel,
        out_shape=shape((faces, quants, modes, lanes), F32),
        in_specs=whole(2),
        out_specs=whole(1)[0],
        compiler_params=near_params,
        cost_estimate=pl.CostEstimate(
            flops=4_000_000_000, bytes_accessed=8_000_000, transcendentals=0
        ),
        name="near",
    )(table, integrals)

    own, flux = pl.pallas_call(
        own_kernel,
        out_shape=(
            shape((quants, modes, lanes), F32),
            shape((faces, orients * modes, depth), BF16),
        ),
        in_specs=whole(8),
        out_specs=tuple(whole(2)),
        scratch_shapes=[
            pltpu.VMEM(((dims + faces) * modes, depth), BF16),
            pltpu.VMEM((quants, (dims + faces) * modes, lanes), F32),
        ],
        compiler_params=near_params,
        cost_estimate=pl.CostEstimate(
            flops=4_000_000_000, bytes_accessed=8_000_000, transcendentals=0
        ),
        name="own",
    )(
        table,
        volume_stiff,
        local_flux,
        integrals,
        modal_state,
        stars,
        plus,
        neighbour_flux,
    )

    return pl.pallas_call(
        neighbour_kernel,
        out_shape=shape((quants, modes, lanes), F32),
        in_specs=[whole(BLOCKS), *whole(8)],
        out_specs=whole(1)[0],
        scratch_shapes=[
            pltpu.VMEM((clusters, count, 8, lanes), F32),
            pltpu.VMEM((count, 8, lanes), F32),
            pltpu.VMEM((faces, quants, modes, lanes), F32),
        ],
        compiler_params=near_params,
        name="neighbour",
    )(arrived, first, beside, across, table, near_partner, minus, flux, own)


def solution(mesh):
    return jax.shard_map(
        local,
        mesh=mesh,
        in_specs=(
            P(None, None, ("region", "sub")),
            P(),
            P(),
            P(),
            P(),
            P(None, None, None, ("region", "sub")),
            P(None, None, None, ("region", "sub")),
            P(None, None, None, ("region", "sub")),
            P(("region", "sub")),
            P(None, ("region", "sub")),
            P(None, ("region", "sub")),
            P(("region", "sub"), None, None, None),
            P(("region", "sub"), None, None),
        ),
        out_specs=P(None, None, ("region", "sub")),
        check_vma=False,
    )
```

```python
import jax
import jax.numpy as jnp
from jax import lax
from jax.experimental import pallas as pl
from jax.experimental.pallas import tpu as pltpu
from jax.sharding import PartitionSpec as P

NDER = 6
BASE_STEP = 0.25
OFFSETS = (-2, -1, 1, 2)
BLOCKS = 4
LANES = 128
QUARTER = 32
F32 = jnp.float32
BF16 = jnp.bfloat16


def split_rows(values):
    high = values.astype(BF16).astype(F32)
    low = values - high
    blank = jnp.zeros((8, values.shape[1]), F32)
    return jnp.concatenate([high, high, low, blank], axis=0).astype(BF16)


def split_columns(matrix):
    high = matrix.astype(BF16).astype(F32)
    low = matrix - high
    blank = jnp.zeros((matrix.shape[0], 8), F32)
    return jnp.concatenate([high, low, high, blank], axis=1).astype(BF16)


def odd_and_high(shape):
    quarter = lax.broadcasted_iota(jnp.int32, shape, 1) // QUARTER
    return quarter % 2 == 1, quarter >= 2


def turned(odd, high, rows):
    pairs = [jnp.where(odd, rows[(k + 1) % BLOCKS], rows[k]) for k in range(BLOCKS)]
    return [
        jnp.where(high, pairs[(2 - i) % BLOCKS], pairs[(-i) % BLOCKS]) for i in range(BLOCKS)
    ]


def lane_gather(values, index):
    numbers = lax.GatherDimensionNumbers(
        offset_dims=(),
        collapsed_slice_dims=(1,),
        start_index_map=(1,),
        operand_batching_dims=(0,),
        start_indices_batching_dims=(0,),
    )
    return lax.gather(
        values,
        index[:, :, None],
        dimension_numbers=numbers,
        slice_sizes=(1, 1),
        mode=lax.GatherScatterMode.PROMISE_IN_BOUNDS,
    )


def groups(count):
    return (count + BLOCKS - 1) // BLOCKS


def taylor_factors(clusters):
    factors = []
    for cluster in range(clusters):
        width = BASE_STEP * 2.0**cluster
        factor = 1.0
        row = []
        for order in range(NDER):
            factor = factor * width / (order + 1)
            row.append(factor)
        factors.append(row)
    return factors


def pairing_blocks(region):
    half = region // 4 % 2
    second = region // 2 % 2
    odd = region % 2
    near, beside = 3 - 3 * second, 2 - odd
    turn = half * (beside - near)
    return [near + turn, 3 * second, 1 + odd, beside - turn]


def predict_kernel(
    state_hbm,
    stiff_hbm,
    star_hbm,
    send_hbm,
    sub_hbm,
    cluster_hbm,
    face_hbm,
    orient_hbm,
    region_index_ref,
    sub_index_ref,
    integral_hbm,
    table_hbm,
    region_hbm0,
    region_hbm1,
    region_hbm2,
    region_hbm3,
    within_hbm0,
    within_hbm1,
    within_hbm2,
    stiff_ref,
    star_ref,
    send_ref,
    sub_ref,
    cluster_ref,
    face_ref,
    orient_ref,
    series_ref,
    product_ref,
    integral_ref,
    table_ref,
    region_ref,
    within_ref,
    arrived,
    sent,
):
    region_hbms = (region_hbm0, region_hbm1, region_hbm2, region_hbm3)
    quants, modes, lanes = state_hbm.shape
    clusters = integral_hbm.shape[0]
    dims = stiff_hbm.shape[0]
    copies = [
        pltpu.make_async_copy(source, target, arrived.at[place])
        for place, (source, target) in enumerate(
            [
                (stiff_hbm, stiff_ref),
                (state_hbm, series_ref.at[0]),
                (star_hbm, star_ref),
                (send_hbm, send_ref),
                (sub_hbm, sub_ref),
                (cluster_hbm, cluster_ref),
                (face_hbm, face_ref),
                (orient_hbm, orient_ref),
            ]
        )
    ]
    for copy in copies:
        copy.start()
    copies[0].wait()
    stacked = jnp.concatenate([stiff_ref[d] for d in range(dims)], axis=0)
    lhs = split_columns(-stacked)
    copies[1].wait()
    block = 5
    blocks = [range(first, min(first + block, quants)) for first in range(0, quants, block)]

    def multiply(slot, rows, values):
        product = jnp.dot(
            lhs, split_rows(jnp.concatenate(values, axis=1)), preferred_element_type=F32
        )
        for place, row in enumerate(rows):
            product_ref[slot, row] = product[:, place * lanes : (place + 1) * lanes]

    for rows in blocks:
        multiply(0, rows, [series_ref[0, row] for row in rows])
    for copy in copies[2:]:
        copy.wait()
    for order in range(1, NDER):
        slot = (order - 1) % 2
        for rows in blocks:
            sums = [None for _ in rows]
            for column in range(quants):
                for d in range(dims):
                    value = product_ref[slot, column, pl.ds(d * modes, modes), :]
                    for place, row in enumerate(rows):
                        term = star_ref[row, column, pl.ds(d, 1), :] * value
                        sums[place] = term if sums[place] is None else sums[place] + term
            for place, row in enumerate(rows):
                series_ref[order, row] = sums[place]
            if order < NDER - 1:
                multiply(1 - slot, rows, sums)

    factors = taylor_factors(clusters)
    per_quant = modes // 8
    count = quants * per_quant
    odd, high = odd_and_high((8, lanes))
    lists = pairing_blocks(region_index_ref[0])
    index = []
    for cluster in range(clusters):
        base = jnp.concatenate(
            [send_ref[0, cluster, pl.ds(lists[s], 1), :] for s in range(BLOCKS)], axis=1
        )
        base = jnp.broadcast_to(base, (8, lanes))
        index.append([base] + [pltpu.roll(base, QUARTER * i, 1) for i in range(1, BLOCKS)])
    sub_slots = sub_ref.shape[2]
    blank = jnp.zeros((1, QUARTER - clusters * sub_slots), jnp.int32)
    row = jnp.concatenate([sub_ref[c] for c in range(clusters)] + [blank], axis=1)
    sub_index = jnp.broadcast_to(jnp.concatenate([row] * BLOCKS, axis=1), (8, lanes))
    owner = lax.broadcasted_iota(jnp.int32, (8, lanes), 1) % QUARTER // sub_slots
    chunk = 4
    leaving = []

    def leave(source, target):
        leaving.append(pltpu.make_async_copy(source, target, sent.at[len(leaving)]))
        leaving[-1].start()

    here = sub_index_ref[0]
    brought = pairing_blocks(region_index_ref[0])
    cluster_row = cluster_ref[...]
    for face in range(face_ref.shape[0]):
        entry = face_ref[pl.ds(face, 1), :]
        place = entry - lanes
        sub_place = place - BLOCKS * QUARTER
        block = place // QUARTER
        slot = sum(jnp.where(block == brought[p], p, 0) for p in range(BLOCKS))
        source = (sub_place // sub_slots) ^ here
        for i in range(BLOCKS):
            region = ((slot + i) & (BLOCKS - 1)) * QUARTER + (place & (QUARTER - 1))
            within = ((source + i) & (BLOCKS - 1)) * QUARTER + cluster_row * sub_slots
            within = within + (sub_place & (sub_slots - 1))
            table_ref[face, pl.ds(i, 1), :] = region & (lanes - 1)
            table_ref[face, pl.ds(BLOCKS + i, 1), :] = within & (lanes - 1)
        table_ref[face, pl.ds(2 * BLOCKS + 2, 1), :] = entry & (lanes - 1)
        table_ref[face, pl.ds(2 * BLOCKS + 3, 1), :] = cluster_row
        kind = jnp.where(place < 0, -1, jnp.where(sub_place < 0, cluster_row, clusters))
        table_ref[face, pl.ds(2 * BLOCKS, 1), :] = kind
        table_ref[face, pl.ds(2 * BLOCKS + 1, 1), :] = orient_ref[pl.ds(face, 1), :]
    leave(table_ref, table_hbm)

    for group in range(groups(count)):
        picked = [[] for _ in range(clusters)]
        shared = []
        for member in range(BLOCKS):
            at = group * BLOCKS + member
            if at >= count:
                for cluster in range(clusters):
                    picked[cluster].append(picked[cluster][-1])
                shared.append(shared[-1])
                continue
            quant, rows = at // per_quant, pl.ds(at % per_quant * 8, 8)
            series = [series_ref[order, quant, rows, :] for order in range(NDER)]
            for cluster in range(clusters):
                total = factors[cluster][0] * series[0]
                for order in range(1, NDER):
                    total = total + factors[cluster][order] * series[order]
                integral_ref[cluster, at] = total
                picked[cluster].append(lane_gather(total, index[cluster][member]))
                other = lane_gather(total, sub_index)
                within = other if cluster == 0 else jnp.where(owner == cluster, other, within)
            shared.append(within)
        for cluster in range(clusters):
            for b, packed in enumerate(turned(odd, high, picked[cluster])):
                region_ref[b, cluster, group] = packed
        for k, packed in enumerate(turned(odd, high, shared)):
            within_ref[(0, 2, 1, 3)[k], group] = packed
        if (group + 1) % chunk == 0:
            part = pl.ds(group + 1 - chunk, chunk)
            for b in range(BLOCKS):
                leave(region_ref.at[b, :, part], region_hbms[b].at[:, part])
            first = (group + 1 - chunk) * BLOCKS
            done = pl.ds(first, min(chunk * BLOCKS, count - first))
            leave(integral_ref.at[:, done], integral_hbm.at[:, done])
    leave(within_ref.at[pl.ds(2, 2)], within_hbm1)
    leave(within_ref.at[0], within_hbm0)
    leave(within_ref.at[pl.ds(1, 1)], within_hbm2)
    for copy in leaving:
        copy.wait()


def near_kernel(table_ref, integral_ref, partner_ref):
    clusters, quants, modes, lanes = integral_ref.shape
    chosen = jnp.broadcast_to(table_ref[0, pl.ds(2 * BLOCKS + 3, 1), :], (8, lanes))
    masks = [chosen == cluster for cluster in range(clusters)]

    def one_face(face, _):
        index = jnp.broadcast_to(table_ref[face, pl.ds(2 * BLOCKS + 2, 1), :], (8, lanes))
        for quant in range(quants):
            for first in range(0, modes, 8):
                rows = pl.ds(first, 8)
                total = lane_gather(integral_ref[0, quant, rows, :], index)
                for cluster in range(1, clusters):
                    other = lane_gather(integral_ref[cluster, quant, rows, :], index)
                    total = jnp.where(masks[cluster], other, total)
                partner_ref[face, quant, rows, :] = total
        return 0

    lax.fori_loop(0, table_ref.shape[0], one_face, 0)


def own_kernel(
    table_ref,
    volume_ref,
    local_ref,
    integral_ref,
    state_ref,
    star_ref,
    plus_ref,
    neighbour_ref,
    result_ref,
    flux_ref,
    lhs_ref,
    product_ref,
):
    quants, modes, lanes = state_ref.shape
    clusters = integral_ref.shape[0]
    dims = volume_ref.shape[0]
    faces, orients = neighbour_ref.shape[:2]
    chosen = jnp.broadcast_to(table_ref[0, pl.ds(2 * BLOCKS + 3, 1), :], (8, lanes))
    masks = [chosen == cluster for cluster in range(clusters)]

    stacked = jnp.concatenate(
        [volume_ref[d] for d in range(dims)] + [-local_ref[f] for f in range(faces)], axis=0
    )
    lhs_ref[...] = split_columns(stacked)
    for quant in range(quants):
        parts = []
        for first in range(0, modes, 8):
            rows = pl.ds(first, 8)
            own = integral_ref[0, quant, rows, :]
            for cluster in range(1, clusters):
                own = jnp.where(masks[cluster], integral_ref[cluster, quant, rows, :], own)
            parts.append(own)
        product_ref[quant] = jnp.dot(
            lhs_ref[...], split_rows(jnp.concatenate(parts, axis=0)), preferred_element_type=F32
        )

    def own_row(row, _):
        total = state_ref[row]
        for column in range(quants):
            for part in range(dims + faces):
                value = product_ref[column, pl.ds(part * modes, modes), :]
                if part < dims:
                    matrix = star_ref[row, column, pl.ds(part, 1), :]
                else:
                    matrix = plus_ref[row, column, pl.ds(part - dims, 1), :]
                total = total + matrix * value
        result_ref[row] = total
        return 0

    lax.fori_loop(0, quants, own_row, 0)

    def one_face(face, _):
        stack = jnp.concatenate([-neighbour_ref[face, o] for o in range(orients)], axis=0)
        flux_ref[face] = split_columns(stack)
        return 0

    lax.fori_loop(0, faces, one_face, 0)


def neighbour_kernel(
    region_refs,
    first_ref,
    beside_ref,
    across_ref,
    table_ref,
    near_ref,
    minus_ref,
    flux_ref,
    own_ref,
    result_ref,
    pool_ref,
    sub_pool_ref,
    partner_ref,
):
    quants, modes, lanes = own_ref.shape
    faces = flux_ref.shape[0]
    clusters = region_refs[0].shape[0]
    orients = flux_ref.shape[1] // modes
    per_quant = modes // 8
    count = quants * per_quant
    odd, high = odd_and_high((8, lanes))

    def spread(face, row):
        return jnp.broadcast_to(table_ref[face, pl.ds(row, 1), :], (8, lanes))

    def unpack(group):
        for cluster in range(clusters):
            pools = turned(odd, high, [region_refs[b][cluster, group] for b in range(BLOCKS)])
            for member, pool in enumerate(pools):
                if group * BLOCKS + member < count:
                    pool_ref[cluster, group * BLOCKS + member] = pool
        within = [first_ref[group], beside_ref[0, group], across_ref[0, group], across_ref[1, group]]
        pools = turned(odd, high, within)
        for member, pool in enumerate(pools):
            if group * BLOCKS + member < count:
                sub_pool_ref[group * BLOCKS + member] = pool

    def gather(face, ats):
        kind = spread(face, 2 * BLOCKS)
        hits = [kind == cluster for cluster in range(clusters + 1)]
        region_index = [spread(face, i) for i in range(BLOCKS)]
        sub_index = [spread(face, BLOCKS + i) for i in range(BLOCKS)]
        for at in ats:
            rows = pl.ds(at % per_quant * 8, 8)
            total = near_ref[face, at // per_quant, rows, :]
            for cluster in range(clusters):
                other = lane_gather(pool_ref[cluster, at], region_index[at % BLOCKS])
                total = jnp.where(hits[cluster], other, total)
            other = lane_gather(sub_pool_ref[at], sub_index[at % BLOCKS])
            partner_ref[face, at // per_quant, rows, :] = jnp.where(hits[clusters], other, total)

    block = 4
    blocks = [range(first, min(first + block, quants)) for first in range(0, quants, block)]

    def flux(face, rows):
        orient = spread(face, 2 * BLOCKS + 1)
        masks = [orient == o for o in range(orients)]
        mixed = [None for _ in rows]
        for column in range(quants):
            value = partner_ref[face, column]
            for place, row in enumerate(rows):
                term = minus_ref[row, column, pl.ds(face, 1), :] * value
                mixed[place] = term if mixed[place] is None else mixed[place] + term
        every = jnp.dot(
            flux_ref[face], split_rows(jnp.concatenate(mixed, axis=1)), preferred_element_type=F32
        )
        for place, row in enumerate(rows):
            for first in range(0, modes, 8):
                columns = slice(place * lanes, (place + 1) * lanes)
                total = every[first : first + 8, columns]
                for o in range(1, orients):
                    at = o * modes + first
                    total = jnp.where(masks[o], every[at : at + 8, columns], total)
                where = pl.ds(first, 8)
                if face == 0:
                    total = total + own_ref[row, where, :]
                else:
                    total = total + result_ref[row, where, :]
                result_ref[row, where, :] = total

    for group in range(groups(count)):
        unpack(group)
    gather(0, range(count))
    for face in range(faces):
        step = (count + len(blocks) - 1) // len(blocks)
        for place, rows in enumerate(blocks):
            flux(face, rows)
            if face + 1 < faces:
                gather(face + 1, range(place * step, min((place + 1) * step, count)))


def whole(count):
    return [pl.BlockSpec(memory_space=pltpu.VMEM) for _ in range(count)]


def far(count):
    return [pl.BlockSpec(memory_space=pltpu.HBM) for _ in range(count)]


def paired(value, axis, pairing):
    count = lax.axis_size(axis)
    pairs = []
    for source in range(count):
        offset = OFFSETS[pairing_blocks(source)[pairing]]
        pairs.append((source, (source + offset) % count))
    return lax.ppermute(value, axis, pairs)


def swapped(value, axis, bit):
    return lax.ppermute(value, axis, [(s, s ^ bit) for s in range(lax.axis_size(axis))])


def local(
    modal_state,
    deriv_stiff,
    volume_stiff,
    local_flux,
    neighbour_flux,
    star_matrices,
    plus_flux,
    minus_flux,
    cluster_ids,
    face_neighbours,
    face_orient,
    send_lists,
    sub_lists,
):
    quants, modes, lanes = modal_state.shape
    clusters = send_lists.shape[2]
    faces, orients = neighbour_flux.shape[:2]
    dims = deriv_stiff.shape[0]
    depth = 3 * modes + 8
    count = quants * modes // 8
    fours = groups(count)
    near_params = pltpu.CompilerParams(vmem_limit_bytes=40 * 1024 * 1024)
    params = pltpu.CompilerParams(vmem_limit_bytes=60 * 1024 * 1024)
    shape = jax.ShapeDtypeStruct
    stars, plus, minus = (
        jnp.transpose(matrix, (1, 2, 0, 3)) for matrix in (star_matrices, plus_flux, minus_flux)
    )
    sends = jnp.transpose(send_lists, (0, 2, 1, 3))
    subs = jnp.transpose(sub_lists, (1, 0, 2))

    here = lax.axis_index("sub").astype(jnp.int32).reshape(1)
    region = lax.axis_index("region").astype(jnp.int32).reshape(1)

    integrals, table, *packed = pl.pallas_call(
        predict_kernel,
        out_shape=(
            shape((clusters, count, 8, lanes), F32),
            shape((faces, 2 * BLOCKS + 8, lanes), jnp.int32),
            *[shape((clusters, fours, 8, lanes), F32)] * BLOCKS,
            shape((fours, 8, lanes), F32),
            shape((2, fours, 8, lanes), F32),
            shape((1, fours, 8, lanes), F32),
        ),
        in_specs=far(8) + [pl.BlockSpec(memory_space=pltpu.SMEM)] * 2,
        out_specs=tuple(far(5 + BLOCKS)),
        scratch_shapes=[
            pltpu.VMEM(deriv_stiff.shape, F32),
            pltpu.VMEM(stars.shape, F32),
            pltpu.VMEM(sends.shape, jnp.int32),
            pltpu.VMEM(subs.shape, jnp.int32),
            pltpu.VMEM((1, lanes), jnp.int32),
            pltpu.VMEM(face_neighbours.shape, jnp.int32),
            pltpu.VMEM(face_orient.shape, jnp.int32),
            pltpu.VMEM((NDER, quants, modes, lanes), F32),
            pltpu.VMEM((2, quants, dims * modes, lanes), F32),
            pltpu.VMEM((clusters, count, 8, lanes), F32),
            pltpu.VMEM((faces, 2 * BLOCKS + 8, lanes), jnp.int32),
            pltpu.VMEM((BLOCKS, clusters, fours, 8, lanes), F32),
            pltpu.VMEM((BLOCKS, fours, 8, lanes), F32),
            pltpu.SemaphoreType.DMA((8,)),
            pltpu.SemaphoreType.DMA((fours + 8,)),
        ],
        compiler_params=params,
        name="predict",
    )(
        modal_state,
        deriv_stiff,
        stars,
        sends,
        subs,
        cluster_ids.reshape(1, lanes),
        face_neighbours,
        face_orient,
        region,
        here,
    )

    arrived = [paired(packed[p], "region", p) for p in range(BLOCKS)]
    first, beside, across = packed[BLOCKS:]
    beside = swapped(beside, "sub", 1)
    across = swapped(jnp.concatenate([across, beside[1:]], axis=0), "sub", 2)
    integrals = integrals.reshape(clusters, quants, modes, lanes)
    near_partner = pl.pallas_call(
        near_kernel,
        out_shape=shape((faces, quants, modes, lanes), F32),
        in_specs=whole(2),
        out_specs=whole(1)[0],
        compiler_params=near_params,
        cost_estimate=pl.CostEstimate(
            flops=4_000_000_000, bytes_accessed=8_000_000, transcendentals=0
        ),
        name="near",
    )(table, integrals)

    own, flux = pl.pallas_call(
        own_kernel,
        out_shape=(
            shape((quants, modes, lanes), F32),
            shape((faces, orients * modes, depth), BF16),
        ),
        in_specs=whole(8),
        out_specs=tuple(whole(2)),
        scratch_shapes=[
            pltpu.VMEM(((dims + faces) * modes, depth), BF16),
            pltpu.VMEM((quants, (dims + faces) * modes, lanes), F32),
        ],
        compiler_params=near_params,
        cost_estimate=pl.CostEstimate(
            flops=4_000_000_000, bytes_accessed=8_000_000, transcendentals=0
        ),
        name="own",
    )(
        table,
        volume_stiff,
        local_flux,
        integrals,
        modal_state,
        stars,
        plus,
        neighbour_flux,
    )

    return pl.pallas_call(
        neighbour_kernel,
        out_shape=shape((quants, modes, lanes), F32),
        in_specs=[whole(BLOCKS), *whole(8)],
        out_specs=whole(1)[0],
        scratch_shapes=[
            pltpu.VMEM((clusters, count, 8, lanes), F32),
            pltpu.VMEM((count, 8, lanes), F32),
            pltpu.VMEM((faces, quants, modes, lanes), F32),
        ],
        compiler_params=near_params,
        name="neighbour",
    )(arrived, first, beside, across, table, near_partner, minus, flux, own)


def solution(mesh):
    return jax.shard_map(
        local,
        mesh=mesh,
        in_specs=(
            P(None, None, ("region", "sub")),
            P(),
            P(),
            P(),
            P(),
            P(None, None, None, ("region", "sub")),
            P(None, None, None, ("region", "sub")),
            P(None, None, None, ("region", "sub")),
            P(("region", "sub")),
            P(None, ("region", "sub")),
            P(None, ("region", "sub")),
            P(("region", "sub"), None, None, None),
            P(("region", "sub"), None, None),
        ),
        out_specs=P(None, None, ("region", "sub")),
        check_vma=False,
    )
```

```python
import jax
import jax.numpy as jnp
from jax import lax
from jax.experimental import pallas as pl
from jax.experimental.pallas import tpu as pltpu
from jax.sharding import PartitionSpec as P

NDER = 6
BASE_STEP = 0.25
OFFSETS = (-2, -1, 1, 2)
BLOCKS = 4
LANES = 128
QUARTER = 32
F32 = jnp.float32
BF16 = jnp.bfloat16


def split_rows(values):
    high = values.astype(BF16).astype(F32)
    low = values - high
    blank = jnp.zeros((8, values.shape[1]), F32)
    return jnp.concatenate([high, high, low, blank], axis=0).astype(BF16)


def split_columns(matrix):
    high = matrix.astype(BF16).astype(F32)
    low = matrix - high
    blank = jnp.zeros((matrix.shape[0], 8), F32)
    return jnp.concatenate([high, low, high, blank], axis=1).astype(BF16)


def odd_and_high(shape):
    quarter = lax.broadcasted_iota(jnp.int32, shape, 1) // QUARTER
    return quarter % 2 == 1, quarter >= 2


def turned(odd, high, rows):
    pairs = [jnp.where(odd, rows[(k + 1) % BLOCKS], rows[k]) for k in range(BLOCKS)]
    return [
        jnp.where(high, pairs[(2 - i) % BLOCKS], pairs[(-i) % BLOCKS]) for i in range(BLOCKS)
    ]


def lane_gather(values, index):
    numbers = lax.GatherDimensionNumbers(
        offset_dims=(),
        collapsed_slice_dims=(1,),
        start_index_map=(1,),
        operand_batching_dims=(0,),
        start_indices_batching_dims=(0,),
    )
    return lax.gather(
        values,
        index[:, :, None],
        dimension_numbers=numbers,
        slice_sizes=(1, 1),
        mode=lax.GatherScatterMode.PROMISE_IN_BOUNDS,
    )


def groups(count):
    return (count + BLOCKS - 1) // BLOCKS


def taylor_factors(clusters):
    factors = []
    for cluster in range(clusters):
        width = BASE_STEP * 2.0**cluster
        factor = 1.0
        row = []
        for order in range(NDER):
            factor = factor * width / (order + 1)
            row.append(factor)
        factors.append(row)
    return factors


def pairing_blocks(region):
    half = region // 4 % 2
    second = region // 2 % 2
    odd = region % 2
    near, beside = 3 - 3 * second, 2 - odd
    turn = half * (beside - near)
    return [near + turn, 1 + odd, 3 * second, beside - turn]


def predict_kernel(
    state_hbm,
    stiff_hbm,
    star_hbm,
    send_hbm,
    sub_hbm,
    cluster_hbm,
    face_hbm,
    orient_hbm,
    region_index_ref,
    sub_index_ref,
    integral_hbm,
    table_hbm,
    region_hbm0,
    region_hbm1,
    region_hbm2,
    region_hbm3,
    within_hbm0,
    within_hbm1,
    within_hbm2,
    stiff_ref,
    star_ref,
    send_ref,
    sub_ref,
    cluster_ref,
    face_ref,
    orient_ref,
    series_ref,
    product_ref,
    integral_ref,
    table_ref,
    region_ref,
    within_ref,
    arrived,
    sent,
):
    region_hbms = (region_hbm0, region_hbm1, region_hbm2, region_hbm3)
    quants, modes, lanes = state_hbm.shape
    clusters = integral_hbm.shape[0]
    dims = stiff_hbm.shape[0]
    copies = [
        pltpu.make_async_copy(source, target, arrived.at[place])
        for place, (source, target) in enumerate(
            [
                (stiff_hbm, stiff_ref),
                (state_hbm, series_ref.at[0]),
                (star_hbm, star_ref),
                (send_hbm, send_ref),
                (sub_hbm, sub_ref),
                (cluster_hbm, cluster_ref),
                (face_hbm, face_ref),
                (orient_hbm, orient_ref),
            ]
        )
    ]
    for copy in copies:
        copy.start()
    copies[0].wait()
    stacked = jnp.concatenate([stiff_ref[d] for d in range(dims)], axis=0)
    lhs = split_columns(-stacked)
    copies[1].wait()
    block = 5
    blocks = [range(first, min(first + block, quants)) for first in range(0, quants, block)]

    def multiply(slot, rows, values):
        product = jnp.dot(
            lhs, split_rows(jnp.concatenate(values, axis=1)), preferred_element_type=F32
        )
        for place, row in enumerate(rows):
            product_ref[slot, row] = product[:, place * lanes : (place + 1) * lanes]

    for rows in blocks:
        multiply(0, rows, [series_ref[0, row] for row in rows])
    for copy in copies[2:]:
        copy.wait()
    for order in range(1, NDER):
        slot = (order - 1) % 2
        for rows in blocks:
            sums = [None for _ in rows]
            for column in range(quants):
                for d in range(dims):
                    value = product_ref[slot, column, pl.ds(d * modes, modes), :]
                    for place, row in enumerate(rows):
                        term = star_ref[row, column, pl.ds(d, 1), :] * value
                        sums[place] = term if sums[place] is None else sums[place] + term
            for place, row in enumerate(rows):
                series_ref[order, row] = sums[place]
            if order < NDER - 1:
                multiply(1 - slot, rows, sums)

    factors = taylor_factors(clusters)
    per_quant = modes // 8
    count = quants * per_quant
    odd, high = odd_and_high((8, lanes))
    lists = pairing_blocks(region_index_ref[0])
    index = []
    for cluster in range(clusters):
        base = jnp.concatenate(
            [send_ref[0, cluster, pl.ds(lists[s], 1), :] for s in range(BLOCKS)], axis=1
        )
        base = jnp.broadcast_to(base, (8, lanes))
        index.append([base] + [pltpu.roll(base, QUARTER * i, 1) for i in range(1, BLOCKS)])
    sub_slots = sub_ref.shape[2]
    blank = jnp.zeros((1, QUARTER - clusters * sub_slots), jnp.int32)
    row = jnp.concatenate([sub_ref[c] for c in range(clusters)] + [blank], axis=1)
    sub_index = jnp.broadcast_to(jnp.concatenate([row] * BLOCKS, axis=1), (8, lanes))
    owner = lax.broadcasted_iota(jnp.int32, (8, lanes), 1) % QUARTER // sub_slots
    chunk = 4
    leaving = []

    def leave(source, target):
        leaving.append(pltpu.make_async_copy(source, target, sent.at[len(leaving)]))
        leaving[-1].start()

    here = sub_index_ref[0]
    brought = pairing_blocks(region_index_ref[0])
    cluster_row = cluster_ref[...]
    for face in range(face_ref.shape[0]):
        entry = face_ref[pl.ds(face, 1), :]
        place = entry - lanes
        sub_place = place - BLOCKS * QUARTER
        block = place // QUARTER
        slot = sum(jnp.where(block == brought[p], p, 0) for p in range(BLOCKS))
        source = (sub_place // sub_slots) ^ here
        for i in range(BLOCKS):
            region = ((slot + i) & (BLOCKS - 1)) * QUARTER + (place & (QUARTER - 1))
            within = ((source + i) & (BLOCKS - 1)) * QUARTER + cluster_row * sub_slots
            within = within + (sub_place & (sub_slots - 1))
            table_ref[face, pl.ds(i, 1), :] = region & (lanes - 1)
            table_ref[face, pl.ds(BLOCKS + i, 1), :] = within & (lanes - 1)
        table_ref[face, pl.ds(2 * BLOCKS + 2, 1), :] = entry & (lanes - 1)
        table_ref[face, pl.ds(2 * BLOCKS + 3, 1), :] = cluster_row
        kind = jnp.where(place < 0, -1, jnp.where(sub_place < 0, cluster_row, clusters))
        table_ref[face, pl.ds(2 * BLOCKS, 1), :] = kind
        table_ref[face, pl.ds(2 * BLOCKS + 1, 1), :] = orient_ref[pl.ds(face, 1), :]
    leave(table_ref, table_hbm)

    for group in range(groups(count)):
        picked = [[] for _ in range(clusters)]
        shared = []
        for member in range(BLOCKS):
            at = group * BLOCKS + member
            if at >= count:
                for cluster in range(clusters):
                    picked[cluster].append(picked[cluster][-1])
                shared.append(shared[-1])
                continue
            quant, rows = at // per_quant, pl.ds(at % per_quant * 8, 8)
            series = [series_ref[order, quant, rows, :] for order in range(NDER)]
            for cluster in range(clusters):
                total = factors[cluster][0] * series[0]
                for order in range(1, NDER):
                    total = total + factors[cluster][order] * series[order]
                integral_ref[cluster, at] = total
                picked[cluster].append(lane_gather(total, index[cluster][member]))
                other = lane_gather(total, sub_index)
                within = other if cluster == 0 else jnp.where(owner == cluster, other, within)
            shared.append(within)
        for cluster in range(clusters):
            for b, packed in enumerate(turned(odd, high, picked[cluster])):
                region_ref[b, cluster, group] = packed
        for k, packed in enumerate(turned(odd, high, shared)):
            within_ref[(0, 2, 1, 3)[k], group] = packed
        if (group + 1) % chunk == 0:
            part = pl.ds(group + 1 - chunk, chunk)
            for b in range(BLOCKS):
                leave(region_ref.at[b, :, part], region_hbms[b].at[:, part])
            first = (group + 1 - chunk) * BLOCKS
            done = pl.ds(first, min(chunk * BLOCKS, count - first))
            leave(integral_ref.at[:, done], integral_hbm.at[:, done])
    leave(within_ref.at[pl.ds(2, 2)], within_hbm1)
    leave(within_ref.at[0], within_hbm0)
    leave(within_ref.at[pl.ds(1, 1)], within_hbm2)
    for copy in leaving:
        copy.wait()


def near_kernel(table_ref, integral_ref, partner_ref):
    clusters, quants, modes, lanes = integral_ref.shape
    chosen = jnp.broadcast_to(table_ref[0, pl.ds(2 * BLOCKS + 3, 1), :], (8, lanes))
    masks = [chosen == cluster for cluster in range(clusters)]

    def one_face(face, _):
        index = jnp.broadcast_to(table_ref[face, pl.ds(2 * BLOCKS + 2, 1), :], (8, lanes))
        for quant in range(quants):
            for first in range(0, modes, 8):
                rows = pl.ds(first, 8)
                total = lane_gather(integral_ref[0, quant, rows, :], index)
                for cluster in range(1, clusters):
                    other = lane_gather(integral_ref[cluster, quant, rows, :], index)
                    total = jnp.where(masks[cluster], other, total)
                partner_ref[face, quant, rows, :] = total
        return 0

    lax.fori_loop(0, table_ref.shape[0], one_face, 0)


def own_kernel(
    table_ref,
    volume_ref,
    local_ref,
    integral_ref,
    state_ref,
    star_ref,
    plus_ref,
    neighbour_ref,
    result_ref,
    flux_ref,
    lhs_ref,
    product_ref,
):
    quants, modes, lanes = state_ref.shape
    clusters = integral_ref.shape[0]
    dims = volume_ref.shape[0]
    faces, orients = neighbour_ref.shape[:2]
    chosen = jnp.broadcast_to(table_ref[0, pl.ds(2 * BLOCKS + 3, 1), :], (8, lanes))
    masks = [chosen == cluster for cluster in range(clusters)]

    stacked = jnp.concatenate(
        [volume_ref[d] for d in range(dims)] + [-local_ref[f] for f in range(faces)], axis=0
    )
    lhs_ref[...] = split_columns(stacked)
    for quant in range(quants):
        parts = []
        for first in range(0, modes, 8):
            rows = pl.ds(first, 8)
            own = integral_ref[0, quant, rows, :]
            for cluster in range(1, clusters):
                own = jnp.where(masks[cluster], integral_ref[cluster, quant, rows, :], own)
            parts.append(own)
        product_ref[quant] = jnp.dot(
            lhs_ref[...], split_rows(jnp.concatenate(parts, axis=0)), preferred_element_type=F32
        )

    def own_row(row, _):
        total = state_ref[row]
        for column in range(quants):
            for part in range(dims + faces):
                value = product_ref[column, pl.ds(part * modes, modes), :]
                if part < dims:
                    matrix = star_ref[row, column, pl.ds(part, 1), :]
                else:
                    matrix = plus_ref[row, column, pl.ds(part - dims, 1), :]
                total = total + matrix * value
        result_ref[row] = total
        return 0

    lax.fori_loop(0, quants, own_row, 0)

    def one_face(face, _):
        stack = jnp.concatenate([-neighbour_ref[face, o] for o in range(orients)], axis=0)
        flux_ref[face] = split_columns(stack)
        return 0

    lax.fori_loop(0, faces, one_face, 0)


def neighbour_kernel(
    region_refs,
    first_ref,
    beside_ref,
    across_ref,
    table_ref,
    near_ref,
    minus_ref,
    flux_ref,
    own_ref,
    result_ref,
    pool_ref,
    sub_pool_ref,
    partner_ref,
):
    quants, modes, lanes = own_ref.shape
    faces = flux_ref.shape[0]
    clusters = region_refs[0].shape[0]
    orients = flux_ref.shape[1] // modes
    per_quant = modes // 8
    count = quants * per_quant
    odd, high = odd_and_high((8, lanes))

    def spread(face, row):
        return jnp.broadcast_to(table_ref[face, pl.ds(row, 1), :], (8, lanes))

    def unpack(group):
        for cluster in range(clusters):
            pools = turned(odd, high, [region_refs[b][cluster, group] for b in range(BLOCKS)])
            for member, pool in enumerate(pools):
                if group * BLOCKS + member < count:
                    pool_ref[cluster, group * BLOCKS + member] = pool
        within = [first_ref[group], beside_ref[0, group], across_ref[0, group], across_ref[1, group]]
        pools = turned(odd, high, within)
        for member, pool in enumerate(pools):
            if group * BLOCKS + member < count:
                sub_pool_ref[group * BLOCKS + member] = pool

    def gather(face, ats):
        kind = spread(face, 2 * BLOCKS)
        hits = [kind == cluster for cluster in range(clusters + 1)]
        region_index = [spread(face, i) for i in range(BLOCKS)]
        sub_index = [spread(face, BLOCKS + i) for i in range(BLOCKS)]
        for at in ats:
            rows = pl.ds(at % per_quant * 8, 8)
            total = near_ref[face, at // per_quant, rows, :]
            for cluster in range(clusters):
                other = lane_gather(pool_ref[cluster, at], region_index[at % BLOCKS])
                total = jnp.where(hits[cluster], other, total)
            other = lane_gather(sub_pool_ref[at], sub_index[at % BLOCKS])
            partner_ref[face, at // per_quant, rows, :] = jnp.where(hits[clusters], other, total)

    block = 4
    blocks = [range(first, min(first + block, quants)) for first in range(0, quants, block)]

    def flux(face, rows):
        orient = spread(face, 2 * BLOCKS + 1)
        masks = [orient == o for o in range(orients)]
        mixed = [None for _ in rows]
        for column in range(quants):
            value = partner_ref[face, column]
            for place, row in enumerate(rows):
                term = minus_ref[row, column, pl.ds(face, 1), :] * value
                mixed[place] = term if mixed[place] is None else mixed[place] + term
        every = jnp.dot(
            flux_ref[face], split_rows(jnp.concatenate(mixed, axis=1)), preferred_element_type=F32
        )
        for place, row in enumerate(rows):
            for first in range(0, modes, 8):
                columns = slice(place * lanes, (place + 1) * lanes)
                total = every[first : first + 8, columns]
                for o in range(1, orients):
                    at = o * modes + first
                    total = jnp.where(masks[o], every[at : at + 8, columns], total)
                where = pl.ds(first, 8)
                if face == 0:
                    total = total + own_ref[row, where, :]
                else:
                    total = total + result_ref[row, where, :]
                result_ref[row, where, :] = total

    for group in range(groups(count)):
        unpack(group)
    gather(0, range(count))
    for face in range(faces):
        step = (count + len(blocks) - 1) // len(blocks)
        for place, rows in enumerate(blocks):
            flux(face, rows)
            if face + 1 < faces:
                gather(face + 1, range(place * step, min((place + 1) * step, count)))


def whole(count):
    return [pl.BlockSpec(memory_space=pltpu.VMEM) for _ in range(count)]


def far(count):
    return [pl.BlockSpec(memory_space=pltpu.HBM) for _ in range(count)]


def paired(value, axis, pairing):
    count = lax.axis_size(axis)
    pairs = []
    for source in range(count):
        offset = OFFSETS[pairing_blocks(source)[pairing]]
        pairs.append((source, (source + offset) % count))
    return lax.ppermute(value, axis, pairs)


def swapped(value, axis, bit):
    return lax.ppermute(value, axis, [(s, s ^ bit) for s in range(lax.axis_size(axis))])


def local(
    modal_state,
    deriv_stiff,
    volume_stiff,
    local_flux,
    neighbour_flux,
    star_matrices,
    plus_flux,
    minus_flux,
    cluster_ids,
    face_neighbours,
    face_orient,
    send_lists,
    sub_lists,
):
    quants, modes, lanes = modal_state.shape
    clusters = send_lists.shape[2]
    faces, orients = neighbour_flux.shape[:2]
    dims = deriv_stiff.shape[0]
    depth = 3 * modes + 8
    count = quants * modes // 8
    fours = groups(count)
    near_params = pltpu.CompilerParams(vmem_limit_bytes=40 * 1024 * 1024)
    params = pltpu.CompilerParams(vmem_limit_bytes=60 * 1024 * 1024)
    shape = jax.ShapeDtypeStruct
    stars, plus, minus = (
        jnp.transpose(matrix, (1, 2, 0, 3)) for matrix in (star_matrices, plus_flux, minus_flux)
    )
    sends = jnp.transpose(send_lists, (0, 2, 1, 3))
    subs = jnp.transpose(sub_lists, (1, 0, 2))

    here = lax.axis_index("sub").astype(jnp.int32).reshape(1)
    region = lax.axis_index("region").astype(jnp.int32).reshape(1)

    integrals, table, *packed = pl.pallas_call(
        predict_kernel,
        out_shape=(
            shape((clusters, count, 8, lanes), F32),
            shape((faces, 2 * BLOCKS + 8, lanes), jnp.int32),
            *[shape((clusters, fours, 8, lanes), F32)] * BLOCKS,
            shape((fours, 8, lanes), F32),
            shape((2, fours, 8, lanes), F32),
            shape((1, fours, 8, lanes), F32),
        ),
        in_specs=far(8) + [pl.BlockSpec(memory_space=pltpu.SMEM)] * 2,
        out_specs=tuple(far(5 + BLOCKS)),
        scratch_shapes=[
            pltpu.VMEM(deriv_stiff.shape, F32),
            pltpu.VMEM(stars.shape, F32),
            pltpu.VMEM(sends.shape, jnp.int32),
            pltpu.VMEM(subs.shape, jnp.int32),
            pltpu.VMEM((1, lanes), jnp.int32),
            pltpu.VMEM(face_neighbours.shape, jnp.int32),
            pltpu.VMEM(face_orient.shape, jnp.int32),
            pltpu.VMEM((NDER, quants, modes, lanes), F32),
            pltpu.VMEM((2, quants, dims * modes, lanes), F32),
            pltpu.VMEM((clusters, count, 8, lanes), F32),
            pltpu.VMEM((faces, 2 * BLOCKS + 8, lanes), jnp.int32),
            pltpu.VMEM((BLOCKS, clusters, fours, 8, lanes), F32),
            pltpu.VMEM((BLOCKS, fours, 8, lanes), F32),
            pltpu.SemaphoreType.DMA((8,)),
            pltpu.SemaphoreType.DMA((fours + 8,)),
        ],
        compiler_params=params,
        name="predict",
    )(
        modal_state,
        deriv_stiff,
        stars,
        sends,
        subs,
        cluster_ids.reshape(1, lanes),
        face_neighbours,
        face_orient,
        region,
        here,
    )

    arrived = [paired(packed[p], "region", p) for p in range(BLOCKS)]
    first, beside, across = packed[BLOCKS:]
    beside = swapped(beside, "sub", 1)
    across = swapped(jnp.concatenate([across, beside[1:]], axis=0), "sub", 2)
    integrals = integrals.reshape(clusters, quants, modes, lanes)
    near_partner = pl.pallas_call(
        near_kernel,
        out_shape=shape((faces, quants, modes, lanes), F32),
        in_specs=whole(2),
        out_specs=whole(1)[0],
        compiler_params=near_params,
        cost_estimate=pl.CostEstimate(
            flops=4_000_000_000, bytes_accessed=8_000_000, transcendentals=0
        ),
        name="near",
    )(table, integrals)

    own, flux = pl.pallas_call(
        own_kernel,
        out_shape=(
            shape((quants, modes, lanes), F32),
            shape((faces, orients * modes, depth), BF16),
        ),
        in_specs=whole(8),
        out_specs=tuple(whole(2)),
        scratch_shapes=[
            pltpu.VMEM(((dims + faces) * modes, depth), BF16),
            pltpu.VMEM((quants, (dims + faces) * modes, lanes), F32),
        ],
        compiler_params=near_params,
        cost_estimate=pl.CostEstimate(
            flops=4_000_000_000, bytes_accessed=8_000_000, transcendentals=0
        ),
        name="own",
    )(
        table,
        volume_stiff,
        local_flux,
        integrals,
        modal_state,
        stars,
        plus,
        neighbour_flux,
    )

    return pl.pallas_call(
        neighbour_kernel,
        out_shape=shape((quants, modes, lanes), F32),
        in_specs=[whole(BLOCKS), *whole(8)],
        out_specs=whole(1)[0],
        scratch_shapes=[
            pltpu.VMEM((clusters, count, 8, lanes), F32),
            pltpu.VMEM((count, 8, lanes), F32),
            pltpu.VMEM((faces, quants, modes, lanes), F32),
        ],
        compiler_params=near_params,
        name="neighbour",
    )(arrived, first, beside, across, table, near_partner, minus, flux, own)


def solution(mesh):
    return jax.shard_map(
        local,
        mesh=mesh,
        in_specs=(
            P(None, None, ("region", "sub")),
            P(),
            P(),
            P(),
            P(),
            P(None, None, None, ("region", "sub")),
            P(None, None, None, ("region", "sub")),
            P(None, None, None, ("region", "sub")),
            P(("region", "sub")),
            P(None, ("region", "sub")),
            P(None, ("region", "sub")),
            P(("region", "sub"), None, None, None),
            P(("region", "sub"), None, None),
        ),
        out_specs=P(None, None, ("region", "sub")),
        check_vma=False,
    )
```

```python
import jax
import jax.numpy as jnp
from jax import lax
from jax.experimental import pallas as pl
from jax.experimental.pallas import tpu as pltpu
from jax.sharding import PartitionSpec as P

NDER = 6
BASE_STEP = 0.25
OFFSETS = (-2, -1, 1, 2)
BLOCKS = 4
LANES = 128
QUARTER = 32
F32 = jnp.float32
BF16 = jnp.bfloat16


def split_rows(values):
    high = values.astype(BF16).astype(F32)
    low = values - high
    blank = jnp.zeros((8, values.shape[1]), F32)
    return jnp.concatenate([high, high, low, blank], axis=0).astype(BF16)


def split_columns(matrix):
    high = matrix.astype(BF16).astype(F32)
    low = matrix - high
    blank = jnp.zeros((matrix.shape[0], 8), F32)
    return jnp.concatenate([high, low, high, blank], axis=1).astype(BF16)


def odd_and_high(shape):
    quarter = lax.broadcasted_iota(jnp.int32, shape, 1) // QUARTER
    return quarter % 2 == 1, quarter >= 2


def turned(odd, high, rows):
    pairs = [jnp.where(odd, rows[(k + 1) % BLOCKS], rows[k]) for k in range(BLOCKS)]
    return [
        jnp.where(high, pairs[(2 - i) % BLOCKS], pairs[(-i) % BLOCKS]) for i in range(BLOCKS)
    ]


def lane_gather(values, index):
    numbers = lax.GatherDimensionNumbers(
        offset_dims=(),
        collapsed_slice_dims=(1,),
        start_index_map=(1,),
        operand_batching_dims=(0,),
        start_indices_batching_dims=(0,),
    )
    return lax.gather(
        values,
        index[:, :, None],
        dimension_numbers=numbers,
        slice_sizes=(1, 1),
        mode=lax.GatherScatterMode.PROMISE_IN_BOUNDS,
    )


def groups(count):
    return (count + BLOCKS - 1) // BLOCKS


def taylor_factors(clusters):
    factors = []
    for cluster in range(clusters):
        width = BASE_STEP * 2.0**cluster
        factor = 1.0
        row = []
        for order in range(NDER):
            factor = factor * width / (order + 1)
            row.append(factor)
        factors.append(row)
    return factors


def pairing_blocks(region, sub):
    half = region // 4 % 2
    second = region // 2 % 2
    odd = region % 2
    near, beside = 3 - 3 * second, 2 - odd
    turn = half * (beside - near)
    far_side, side = 3 * second, 1 + odd
    swap = sub % 2 * (side - far_side)
    return [near + turn, far_side + swap, side - swap, beside - turn]


def predict_kernel(
    state_hbm,
    stiff_hbm,
    star_hbm,
    send_hbm,
    sub_hbm,
    cluster_hbm,
    face_hbm,
    orient_hbm,
    region_index_ref,
    sub_index_ref,
    integral_hbm,
    table_hbm,
    region_hbm0,
    region_hbm1,
    region_hbm2,
    region_hbm3,
    within_hbm0,
    within_hbm1,
    within_hbm2,
    stiff_ref,
    star_ref,
    send_ref,
    sub_ref,
    cluster_ref,
    face_ref,
    orient_ref,
    series_ref,
    product_ref,
    integral_ref,
    table_ref,
    region_ref,
    within_ref,
    arrived,
    sent,
):
    region_hbms = (region_hbm0, region_hbm1, region_hbm2, region_hbm3)
    quants, modes, lanes = state_hbm.shape
    clusters = integral_hbm.shape[0]
    dims = stiff_hbm.shape[0]
    copies = [
        pltpu.make_async_copy(source, target, arrived.at[place])
        for place, (source, target) in enumerate(
            [
                (stiff_hbm, stiff_ref),
                (state_hbm, series_ref.at[0]),
                (star_hbm, star_ref),
                (send_hbm, send_ref),
                (sub_hbm, sub_ref),
                (cluster_hbm, cluster_ref),
                (face_hbm, face_ref),
                (orient_hbm, orient_ref),
            ]
        )
    ]
    for copy in copies:
        copy.start()
    copies[0].wait()
    stacked = jnp.concatenate([stiff_ref[d] for d in range(dims)], axis=0)
    lhs = split_columns(-stacked)
    copies[1].wait()
    block = 5
    blocks = [range(first, min(first + block, quants)) for first in range(0, quants, block)]

    def multiply(slot, rows, values):
        product = jnp.dot(
            lhs, split_rows(jnp.concatenate(values, axis=1)), preferred_element_type=F32
        )
        for place, row in enumerate(rows):
            product_ref[slot, row] = product[:, place * lanes : (place + 1) * lanes]

    for rows in blocks:
        multiply(0, rows, [series_ref[0, row] for row in rows])
    for copy in copies[2:]:
        copy.wait()
    for order in range(1, NDER):
        slot = (order - 1) % 2
        for rows in blocks:
            sums = [None for _ in rows]
            for column in range(quants):
                for d in range(dims):
                    value = product_ref[slot, column, pl.ds(d * modes, modes), :]
                    for place, row in enumerate(rows):
                        term = star_ref[row, column, pl.ds(d, 1), :] * value
                        sums[place] = term if sums[place] is None else sums[place] + term
            for place, row in enumerate(rows):
                series_ref[order, row] = sums[place]
            if order < NDER - 1:
                multiply(1 - slot, rows, sums)

    factors = taylor_factors(clusters)
    per_quant = modes // 8
    count = quants * per_quant
    odd, high = odd_and_high((8, lanes))
    lists = pairing_blocks(region_index_ref[0], sub_index_ref[0])
    index = []
    for cluster in range(clusters):
        base = jnp.concatenate(
            [send_ref[0, cluster, pl.ds(lists[s], 1), :] for s in range(BLOCKS)], axis=1
        )
        base = jnp.broadcast_to(base, (8, lanes))
        index.append([base] + [pltpu.roll(base, QUARTER * i, 1) for i in range(1, BLOCKS)])
    sub_slots = sub_ref.shape[2]
    blank = jnp.zeros((1, QUARTER - clusters * sub_slots), jnp.int32)
    row = jnp.concatenate([sub_ref[c] for c in range(clusters)] + [blank], axis=1)
    sub_index = jnp.broadcast_to(jnp.concatenate([row] * BLOCKS, axis=1), (8, lanes))
    owner = lax.broadcasted_iota(jnp.int32, (8, lanes), 1) % QUARTER // sub_slots
    chunk = 4
    leaving = []

    def leave(source, target):
        leaving.append(pltpu.make_async_copy(source, target, sent.at[len(leaving)]))
        leaving[-1].start()

    here = sub_index_ref[0]
    brought = pairing_blocks(region_index_ref[0], sub_index_ref[0])
    cluster_row = cluster_ref[...]
    for face in range(face_ref.shape[0]):
        entry = face_ref[pl.ds(face, 1), :]
        place = entry - lanes
        sub_place = place - BLOCKS * QUARTER
        block = place // QUARTER
        slot = sum(jnp.where(block == brought[p], p, 0) for p in range(BLOCKS))
        source = (sub_place // sub_slots) ^ here
        for i in range(BLOCKS):
            region = ((slot + i) & (BLOCKS - 1)) * QUARTER + (place & (QUARTER - 1))
            within = ((source + i) & (BLOCKS - 1)) * QUARTER + cluster_row * sub_slots
            within = within + (sub_place & (sub_slots - 1))
            table_ref[face, pl.ds(i, 1), :] = region & (lanes - 1)
            table_ref[face, pl.ds(BLOCKS + i, 1), :] = within & (lanes - 1)
        table_ref[face, pl.ds(2 * BLOCKS + 2, 1), :] = entry & (lanes - 1)
        table_ref[face, pl.ds(2 * BLOCKS + 3, 1), :] = cluster_row
        kind = jnp.where(place < 0, -1, jnp.where(sub_place < 0, cluster_row, clusters))
        table_ref[face, pl.ds(2 * BLOCKS, 1), :] = kind
        table_ref[face, pl.ds(2 * BLOCKS + 1, 1), :] = orient_ref[pl.ds(face, 1), :]
    leave(table_ref, table_hbm)

    for group in range(groups(count)):
        picked = [[] for _ in range(clusters)]
        shared = []
        for member in range(BLOCKS):
            at = group * BLOCKS + member
            if at >= count:
                for cluster in range(clusters):
                    picked[cluster].append(picked[cluster][-1])
                shared.append(shared[-1])
                continue
            quant, rows = at // per_quant, pl.ds(at % per_quant * 8, 8)
            series = [series_ref[order, quant, rows, :] for order in range(NDER)]
            for cluster in range(clusters):
                total = factors[cluster][0] * series[0]
                for order in range(1, NDER):
                    total = total + factors[cluster][order] * series[order]
                integral_ref[cluster, at] = total
                picked[cluster].append(lane_gather(total, index[cluster][member]))
                other = lane_gather(total, sub_index)
                within = other if cluster == 0 else jnp.where(owner == cluster, other, within)
            shared.append(within)
        for cluster in range(clusters):
            for b, packed in enumerate(turned(odd, high, picked[cluster])):
                region_ref[b, cluster, group] = packed
        for k, packed in enumerate(turned(odd, high, shared)):
            within_ref[(0, 2, 1, 3)[k], group] = packed
        if (group + 1) % chunk == 0:
            part = pl.ds(group + 1 - chunk, chunk)
            for b in range(BLOCKS):
                leave(region_ref.at[b, :, part], region_hbms[b].at[:, part])
            first = (group + 1 - chunk) * BLOCKS
            done = pl.ds(first, min(chunk * BLOCKS, count - first))
            leave(integral_ref.at[:, done], integral_hbm.at[:, done])
    leave(within_ref.at[pl.ds(2, 2)], within_hbm1)
    leave(within_ref.at[0], within_hbm0)
    leave(within_ref.at[pl.ds(1, 1)], within_hbm2)
    for copy in leaving:
        copy.wait()


def near_kernel(table_ref, integral_ref, partner_ref):
    clusters, quants, modes, lanes = integral_ref.shape
    chosen = jnp.broadcast_to(table_ref[0, pl.ds(2 * BLOCKS + 3, 1), :], (8, lanes))
    masks = [chosen == cluster for cluster in range(clusters)]

    def one_face(face, _):
        index = jnp.broadcast_to(table_ref[face, pl.ds(2 * BLOCKS + 2, 1), :], (8, lanes))
        for quant in range(quants):
            for first in range(0, modes, 8):
                rows = pl.ds(first, 8)
                total = lane_gather(integral_ref[0, quant, rows, :], index)
                for cluster in range(1, clusters):
                    other = lane_gather(integral_ref[cluster, quant, rows, :], index)
                    total = jnp.where(masks[cluster], other, total)
                partner_ref[face, quant, rows, :] = total
        return 0

    lax.fori_loop(0, table_ref.shape[0], one_face, 0)


def own_kernel(
    table_ref,
    volume_ref,
    local_ref,
    integral_ref,
    state_ref,
    star_ref,
    plus_ref,
    neighbour_ref,
    result_ref,
    flux_ref,
    lhs_ref,
    product_ref,
):
    quants, modes, lanes = state_ref.shape
    clusters = integral_ref.shape[0]
    dims = volume_ref.shape[0]
    faces, orients = neighbour_ref.shape[:2]
    chosen = jnp.broadcast_to(table_ref[0, pl.ds(2 * BLOCKS + 3, 1), :], (8, lanes))
    masks = [chosen == cluster for cluster in range(clusters)]

    stacked = jnp.concatenate(
        [volume_ref[d] for d in range(dims)] + [-local_ref[f] for f in range(faces)], axis=0
    )
    lhs_ref[...] = split_columns(stacked)
    for quant in range(quants):
        parts = []
        for first in range(0, modes, 8):
            rows = pl.ds(first, 8)
            own = integral_ref[0, quant, rows, :]
            for cluster in range(1, clusters):
                own = jnp.where(masks[cluster], integral_ref[cluster, quant, rows, :], own)
            parts.append(own)
        product_ref[quant] = jnp.dot(
            lhs_ref[...], split_rows(jnp.concatenate(parts, axis=0)), preferred_element_type=F32
        )

    def own_row(row, _):
        total = state_ref[row]
        for column in range(quants):
            for part in range(dims + faces):
                value = product_ref[column, pl.ds(part * modes, modes), :]
                if part < dims:
                    matrix = star_ref[row, column, pl.ds(part, 1), :]
                else:
                    matrix = plus_ref[row, column, pl.ds(part - dims, 1), :]
                total = total + matrix * value
        result_ref[row] = total
        return 0

    lax.fori_loop(0, quants, own_row, 0)

    def one_face(face, _):
        stack = jnp.concatenate([-neighbour_ref[face, o] for o in range(orients)], axis=0)
        flux_ref[face] = split_columns(stack)
        return 0

    lax.fori_loop(0, faces, one_face, 0)


def neighbour_kernel(
    region_refs,
    first_ref,
    beside_ref,
    across_ref,
    table_ref,
    near_ref,
    minus_ref,
    flux_ref,
    own_ref,
    result_ref,
    pool_ref,
    sub_pool_ref,
    partner_ref,
):
    quants, modes, lanes = own_ref.shape
    faces = flux_ref.shape[0]
    clusters = region_refs[0].shape[0]
    orients = flux_ref.shape[1] // modes
    per_quant = modes // 8
    count = quants * per_quant
    odd, high = odd_and_high((8, lanes))

    def spread(face, row):
        return jnp.broadcast_to(table_ref[face, pl.ds(row, 1), :], (8, lanes))

    def unpack(group):
        for cluster in range(clusters):
            pools = turned(odd, high, [region_refs[b][cluster, group] for b in range(BLOCKS)])
            for member, pool in enumerate(pools):
                if group * BLOCKS + member < count:
                    pool_ref[cluster, group * BLOCKS + member] = pool
        within = [first_ref[group], beside_ref[0, group], across_ref[0, group], across_ref[1, group]]
        pools = turned(odd, high, within)
        for member, pool in enumerate(pools):
            if group * BLOCKS + member < count:
                sub_pool_ref[group * BLOCKS + member] = pool

    def gather(face, ats):
        kind = spread(face, 2 * BLOCKS)
        hits = [kind == cluster for cluster in range(clusters + 1)]
        region_index = [spread(face, i) for i in range(BLOCKS)]
        sub_index = [spread(face, BLOCKS + i) for i in range(BLOCKS)]
        for at in ats:
            rows = pl.ds(at % per_quant * 8, 8)
            total = near_ref[face, at // per_quant, rows, :]
            for cluster in range(clusters):
                other = lane_gather(pool_ref[cluster, at], region_index[at % BLOCKS])
                total = jnp.where(hits[cluster], other, total)
            other = lane_gather(sub_pool_ref[at], sub_index[at % BLOCKS])
            partner_ref[face, at // per_quant, rows, :] = jnp.where(hits[clusters], other, total)

    block = 4
    blocks = [range(first, min(first + block, quants)) for first in range(0, quants, block)]

    def flux(face, rows):
        orient = spread(face, 2 * BLOCKS + 1)
        masks = [orient == o for o in range(orients)]
        mixed = [None for _ in rows]
        for column in range(quants):
            value = partner_ref[face, column]
            for place, row in enumerate(rows):
                term = minus_ref[row, column, pl.ds(face, 1), :] * value
                mixed[place] = term if mixed[place] is None else mixed[place] + term
        every = jnp.dot(
            flux_ref[face], split_rows(jnp.concatenate(mixed, axis=1)), preferred_element_type=F32
        )
        for place, row in enumerate(rows):
            for first in range(0, modes, 8):
                columns = slice(place * lanes, (place + 1) * lanes)
                total = every[first : first + 8, columns]
                for o in range(1, orients):
                    at = o * modes + first
                    total = jnp.where(masks[o], every[at : at + 8, columns], total)
                where = pl.ds(first, 8)
                if face == 0:
                    total = total + own_ref[row, where, :]
                else:
                    total = total + result_ref[row, where, :]
                result_ref[row, where, :] = total

    for group in range(groups(count)):
        unpack(group)
    gather(0, range(count))
    for face in range(faces):
        step = (count + len(blocks) - 1) // len(blocks)
        for place, rows in enumerate(blocks):
            flux(face, rows)
            if face + 1 < faces:
                gather(face + 1, range(place * step, min((place + 1) * step, count)))


def whole(count):
    return [pl.BlockSpec(memory_space=pltpu.VMEM) for _ in range(count)]


def far(count):
    return [pl.BlockSpec(memory_space=pltpu.HBM) for _ in range(count)]


def paired(value, place):
    regions, subs = lax.axis_size("region"), lax.axis_size("sub")
    pairs = []
    for region in range(regions):
        for sub in range(subs):
            offset = OFFSETS[pairing_blocks(region, sub)[place]]
            pairs.append((region * subs + sub, (region + offset) % regions * subs + sub))
    return lax.ppermute(value, ("region", "sub"), pairs)


def swapped(value, axis, bit):
    return lax.ppermute(value, axis, [(s, s ^ bit) for s in range(lax.axis_size(axis))])


def local(
    modal_state,
    deriv_stiff,
    volume_stiff,
    local_flux,
    neighbour_flux,
    star_matrices,
    plus_flux,
    minus_flux,
    cluster_ids,
    face_neighbours,
    face_orient,
    send_lists,
    sub_lists,
):
    quants, modes, lanes = modal_state.shape
    clusters = send_lists.shape[2]
    faces, orients = neighbour_flux.shape[:2]
    dims = deriv_stiff.shape[0]
    depth = 3 * modes + 8
    count = quants * modes // 8
    fours = groups(count)
    near_params = pltpu.CompilerParams(vmem_limit_bytes=40 * 1024 * 1024)
    params = pltpu.CompilerParams(vmem_limit_bytes=60 * 1024 * 1024)
    shape = jax.ShapeDtypeStruct
    stars, plus, minus = (
        jnp.transpose(matrix, (1, 2, 0, 3)) for matrix in (star_matrices, plus_flux, minus_flux)
    )
    sends = jnp.transpose(send_lists, (0, 2, 1, 3))
    subs = jnp.transpose(sub_lists, (1, 0, 2))

    here = lax.axis_index("sub").astype(jnp.int32).reshape(1)
    region = lax.axis_index("region").astype(jnp.int32).reshape(1)

    integrals, table, *packed = pl.pallas_call(
        predict_kernel,
        out_shape=(
            shape((clusters, count, 8, lanes), F32),
            shape((faces, 2 * BLOCKS + 8, lanes), jnp.int32),
            *[shape((clusters, fours, 8, lanes), F32)] * BLOCKS,
            shape((fours, 8, lanes), F32),
            shape((2, fours, 8, lanes), F32),
            shape((1, fours, 8, lanes), F32),
        ),
        in_specs=far(8) + [pl.BlockSpec(memory_space=pltpu.SMEM)] * 2,
        out_specs=tuple(far(5 + BLOCKS)),
        scratch_shapes=[
            pltpu.VMEM(deriv_stiff.shape, F32),
            pltpu.VMEM(stars.shape, F32),
            pltpu.VMEM(sends.shape, jnp.int32),
            pltpu.VMEM(subs.shape, jnp.int32),
            pltpu.VMEM((1, lanes), jnp.int32),
            pltpu.VMEM(face_neighbours.shape, jnp.int32),
            pltpu.VMEM(face_orient.shape, jnp.int32),
            pltpu.VMEM((NDER, quants, modes, lanes), F32),
            pltpu.VMEM((2, quants, dims * modes, lanes), F32),
            pltpu.VMEM((clusters, count, 8, lanes), F32),
            pltpu.VMEM((faces, 2 * BLOCKS + 8, lanes), jnp.int32),
            pltpu.VMEM((BLOCKS, clusters, fours, 8, lanes), F32),
            pltpu.VMEM((BLOCKS, fours, 8, lanes), F32),
            pltpu.SemaphoreType.DMA((8,)),
            pltpu.SemaphoreType.DMA((fours + 8,)),
        ],
        compiler_params=params,
        name="predict",
    )(
        modal_state,
        deriv_stiff,
        stars,
        sends,
        subs,
        cluster_ids.reshape(1, lanes),
        face_neighbours,
        face_orient,
        region,
        here,
    )

    arrived = [paired(packed[p], p) for p in range(BLOCKS)]
    first, beside, across = packed[BLOCKS:]
    beside = swapped(beside, "sub", 1)
    across = swapped(jnp.concatenate([across, beside[1:]], axis=0), "sub", 2)
    integrals = integrals.reshape(clusters, quants, modes, lanes)
    near_partner = pl.pallas_call(
        near_kernel,
        out_shape=shape((faces, quants, modes, lanes), F32),
        in_specs=whole(2),
        out_specs=whole(1)[0],
        compiler_params=near_params,
        cost_estimate=pl.CostEstimate(
            flops=4_000_000_000, bytes_accessed=8_000_000, transcendentals=0
        ),
        name="near",
    )(table, integrals)

    own, flux = pl.pallas_call(
        own_kernel,
        out_shape=(
            shape((quants, modes, lanes), F32),
            shape((faces, orients * modes, depth), BF16),
        ),
        in_specs=whole(8),
        out_specs=tuple(whole(2)),
        scratch_shapes=[
            pltpu.VMEM(((dims + faces) * modes, depth), BF16),
            pltpu.VMEM((quants, (dims + faces) * modes, lanes), F32),
        ],
        compiler_params=near_params,
        cost_estimate=pl.CostEstimate(
            flops=4_000_000_000, bytes_accessed=8_000_000, transcendentals=0
        ),
        name="own",
    )(
        table,
        volume_stiff,
        local_flux,
        integrals,
        modal_state,
        stars,
        plus,
        neighbour_flux,
    )

    return pl.pallas_call(
        neighbour_kernel,
        out_shape=shape((quants, modes, lanes), F32),
        in_specs=[whole(BLOCKS), *whole(8)],
        out_specs=whole(1)[0],
        scratch_shapes=[
            pltpu.VMEM((clusters, count, 8, lanes), F32),
            pltpu.VMEM((count, 8, lanes), F32),
            pltpu.VMEM((faces, quants, modes, lanes), F32),
        ],
        compiler_params=near_params,
        name="neighbour",
    )(arrived, first, beside, across, table, near_partner, minus, flux, own)


def solution(mesh):
    return jax.shard_map(
        local,
        mesh=mesh,
        in_specs=(
            P(None, None, ("region", "sub")),
            P(),
            P(),
            P(),
            P(),
            P(None, None, None, ("region", "sub")),
            P(None, None, None, ("region", "sub")),
            P(None, None, None, ("region", "sub")),
            P(("region", "sub")),
            P(None, ("region", "sub")),
            P(None, ("region", "sub")),
            P(("region", "sub"), None, None, None),
            P(("region", "sub"), None, None),
        ),
        out_specs=P(None, None, ("region", "sub")),
        check_vma=False,
    )
```
